256 devices in a mesh: dp: 32 (over z, x_hi, core), tensor: 8 (over x_lo, y).
Axes of the slice: x: 4 (x_hi: 2, x_lo: 2; x = x_hi * 2 + x_lo), y: 4, z: 8, core: 2. Of those that a mesh axis runs over, the one named last changes fastest.
Arguments:
- tokens: bfloat16 [16384, 3072], P('dp', 'tensor'), may hold values from -6 to 6
- hidden_cot: bfloat16 [16384, 8192], P('dp', 'tensor'), may hold values from -1.5 to 1.5
- w_gate: bfloat16 [3072, 8192], P(None, 'tensor'), may hold values from -0.109375 to 0.109375
- w_up: bfloat16 [3072, 8192], P(None, 'tensor'), may hold values from -0.109375 to 0.109375
- expert_ids: int32 [16384, 2], P('dp'), may hold values from 0 to 7, as said below
- route_fixed: int32 [16384, 2], P('dp'), may hold values from 4096 to 65535
Outputs:
- token_grad: bfloat16 [16384, 3072], P('dp', 'tensor')
- gate_grad: bfloat16 [3072, 8192], P('dp', 'tensor')
- up_grad: bfloat16 [3072, 8192], P('dp', 'tensor')
- route_grad: float32 [16384], P('dp')
The draws below stay inside these ranges and needn't reach their ends.
Inputs may be any that keep to these rules, and one draw needn't show every extreme that they name: `expert_ids`: each row names 2 different experts; in each aligned block of 512 rows (the rows of one index of dp), between 128 and 256 rows name expert 0, and exactly 256 in some block.
All inputs are finite; a program needn't handle non-finite values.
Results may differ from the reference program's by a relative error of at most 0.0049.
Values may be sent and summed in bfloat16 or wider, within the bound.
No kernel may reach another device: no remote copies, remote signals or barrier semaphores. Data moves between devices by JAX's collectives and lax.ppermute only.
A program may use at most 128 MiB of HBM per device.

```python
import jax
import jax.numpy as jnp
from jax import lax

D = 3072
FF = 8192
EXPERTS = 8
TOP = 2
TOK_DEV = 512
CAP = 256
TOKENS = 16384


def draw_expert_ids(key, part):
    key = jax.random.fold_in(key, 11)
    keys = jax.random.split(key, 6)
    blocks = TOKENS // TOK_DEV
    counts = jax.random.randint(keys[0], (blocks,), CAP // 2, CAP + 1)
    peak = jax.random.randint(keys[1], (), 0, blocks)
    counts = jnp.where(jnp.arange(blocks) == peak, CAP, counts)
    orders = jax.vmap(lambda k: jax.random.permutation(k, TOK_DEV))(jax.random.split(keys[2], blocks))
    ranks = jnp.argsort(orders, axis=1, stable=True).astype(jnp.int32)
    routed = (ranks < counts[:, None]).reshape(TOKENS)
    first = jax.random.randint(keys[3], (TOKENS,), 1, EXPERTS)
    stride = jax.random.randint(keys[4], (TOKENS,), 1, EXPERTS - 1)
    second = 1 + (first - 1 + stride) % (EXPERTS - 1)
    column = jax.random.randint(keys[5], (TOKENS,), 0, 2)
    left = jnp.where(routed, jnp.where(column == 0, 0, first), first)
    right = jnp.where(routed, jnp.where(column == 0, first, 0), second)
    return jnp.stack([left, right], axis=1).astype(jnp.int32)


def with_ends(array, key, least, top_value):
    shape = array.shape
    place = [jax.random.randint(jax.random.fold_in(key, axis), (), 0, shape[axis]) for axis in range(len(shape))]
    array = array.at[tuple(place)].set(least)
    longest = shape.index(max(shape))
    place[longest] = (place[longest] + 1) % shape[longest]
    return array.at[tuple(place)].set(top_value)


def with_spikes(drawn, stream_key, source, target, parts, factor):
    owner, partner = [(jnp.arange(drawn.shape[axis_at]) // (drawn.shape[axis_at] // parts)).reshape([-1 if axis == axis_at else 1 for axis in range(drawn.ndim)]) for axis_at in (source, target)]
    chosen = jax.random.permutation(stream_key, parts)[partner]
    strong = (owner == chosen) | (owner == (partner + parts // 2) % parts)
    return jnp.where(strong, factor * drawn, drawn)


def level_of(rng, shape, shards, least, largest):
    loudness, own = 1.0, jax.random.fold_in(rng, 6)
    for position, shards_of in shards:
        steps = jnp.exp(jax.random.uniform(jax.random.fold_in(own, position), (shards_of,), jnp.float32, least / len(shards), largest / len(shards)))
        loudness = loudness * jnp.repeat(steps, shape[position] // shards_of).reshape([-1 if axis == position else 1 for axis in range(len(shape))])
    return loudness


def centred(key, extent, width, bound, pieces=(), dtype=jnp.bfloat16):
    result = width * jax.random.normal(key, extent, jnp.float32)
    if pieces:
        result = result * level_of(key, extent, pieces, -0.22, 0.18)
    return jnp.clip(result, -bound, bound).astype(dtype)


def heavy_noise(key, extent, scale, limit, shards, heavy, kind=jnp.bfloat16):
    array = scale * jax.random.normal(key, extent, jnp.float32)
    if shards:
        array = array * level_of(key, extent, shards, -0.22, 0.18)
    return jnp.clip(with_spikes(array, jax.random.fold_in(key, 3), *heavy), -limit, limit).astype(kind)


def setup_inputs(seed: int = 0) -> dict:
    arg_keys = jax.random.split(jax.random.key(seed), 7)
    return {
        "tokens": heavy_noise(arg_keys[0], (TOKENS, D), 1.0, 6.0, ((0, 32), (1, 8)), (0, 1, 32, 2.75)),
        "hidden_cot": centred(arg_keys[1], (TOKENS, FF), 0.25, 1.5, ((0, 32), (1, 8))),
        "w_gate": centred(arg_keys[2], (D, FF), D ** -0.5, 0.109375, ((1, 8),)),
        "w_up": centred(arg_keys[3], (D, FF), D ** -0.5, 0.109375, ((1, 8),)),
        "expert_ids": draw_expert_ids(jax.random.fold_in(arg_keys[6], 71), 0),
        "route_fixed": with_ends(jax.random.randint(arg_keys[5], (TOKENS, TOP), 4096, 65536), jax.random.fold_in(arg_keys[5], 1), 4096, 65535).astype(jnp.int32),
    }


def reference(tokens, hidden_cot, w_gate, w_up, expert_ids, route_fixed):
    gate_pre = jnp.dot(tokens, w_gate, preferred_element_type=jnp.float32)
    up_pre = jnp.dot(tokens, w_up, preferred_element_type=jnp.float32)
    selected = expert_ids == 0
    routed = jnp.any(selected, axis=1).astype(jnp.float32)
    share = jnp.sum(jnp.where(selected, route_fixed, 0), axis=1).astype(jnp.float32) / 65536.0
    sigmoid_gate = jax.nn.sigmoid(gate_pre)
    activated = gate_pre * sigmoid_gate
    hidden = (activated * up_pre).astype(jnp.bfloat16)
    hidden = lax.optimization_barrier(hidden)
    hidden_wide = hidden.astype(jnp.float32)
    cot_wide = hidden_cot.astype(jnp.float32)
    route_grad = routed * jnp.sum(hidden_wide * cot_wide, axis=1)
    scaled = share[:, None] * cot_wide
    gate_cot = (scaled * up_pre * sigmoid_gate * (1.0 + gate_pre * (1.0 - sigmoid_gate))).astype(jnp.bfloat16)
    up_cot = (scaled * activated).astype(jnp.bfloat16)
    dims = (((1,), (1,)), ((), ()))
    token_grad = lax.dot_general(gate_cot, w_gate, dims, preferred_element_type=jnp.float32)
    token_grad = token_grad + lax.dot_general(up_cot, w_up, dims, preferred_element_type=jnp.float32)
    rows_dims = (((0,), (0,)), ((), ()))
    gate_grad = lax.dot_general(tokens, gate_cot, rows_dims, preferred_element_type=jnp.float32)
    up_grad = lax.dot_general(tokens, up_cot, rows_dims, preferred_element_type=jnp.float32)
    return (token_grad.astype(jnp.bfloat16), gate_grad.astype(jnp.bfloat16), up_grad.astype(jnp.bfloat16), route_grad)
```

```python
import jax
import jax.numpy as jnp
from jax import lax
from jax.sharding import PartitionSpec as P

CAP = 256
BF = jnp.bfloat16
F32 = jnp.float32


def on_device(tokens, hidden_cot, w_gate, w_up, expert_ids, route_fixed):
    tok_dev, piece = tokens.shape
    width = w_gate.shape[1]
    n_tensor = lax.axis_size("tensor")
    n_dp = lax.axis_size("dp")
    n_z = n_dp // 4
    rows = piece // 4
    t = lax.axis_index("tensor")
    dp = lax.axis_index("dp")
    xh, core = (dp // 2) % 2, dp % 2

    def over_tensor(x, k):
        return lax.ppermute(x, "tensor", [(i, i ^ k) for i in range(n_tensor)])

    def over_dp(x, k):
        return lax.ppermute(x, "dp", [(i, i ^ k) for i in range(n_dp)])

    selected = expert_ids == 0
    flag = jnp.any(selected, axis=1)
    place = jnp.arange(tok_dev, dtype=jnp.int32)
    upto = (place[:, None] <= place[None, :]).astype(BF)
    slot_of = jnp.dot(flag.astype(BF)[None, :], upto, preferred_element_type=F32)[0] - 1.0
    slot_of = jnp.where(flag, slot_of.astype(jnp.int32), -1)
    mask = slot_of[None, :] == jnp.arange(CAP, dtype=jnp.int32)[:, None]
    dispatch = mask.astype(BF)
    share_all = jnp.sum(jnp.where(selected, route_fixed, 0), axis=1).astype(F32) / 65536.0
    share = jnp.sum(jnp.where(mask, share_all[None, :], 0.0), axis=1)

    picked = lax.dot_general(
        tokens, dispatch, (((0,), (1,)), ((), ())), preferred_element_type=F32
    ).astype(BF)
    far_piece = over_dp(
        lax.dynamic_slice_in_dim(picked, (1 - xh) * 2 * rows, 2 * rows, 0), 2
    )
    near = jnp.zeros((n_tensor, piece, CAP), BF)
    for k in range(n_tensor):
        got = over_tensor(picked, k) if k else picked
        near = lax.dynamic_update_index_in_dim(near, got, t ^ k, 0)
    cot_rows = jnp.dot(dispatch, hidden_cot, preferred_element_type=F32).astype(BF)

    gathered = near.reshape(n_tensor * piece, CAP)
    first = (((0,), (0,)), ((), ()))
    gate_pre = lax.dot_general(gathered, w_gate, first, preferred_element_type=F32)
    up_pre = lax.dot_general(gathered, w_up, first, preferred_element_type=F32)
    sig = jax.nn.sigmoid(gate_pre)
    activated = gate_pre * sig
    hidden = lax.optimization_barrier((activated * up_pre).astype(BF))
    cot_wide = cot_rows.astype(F32)
    route_part = jnp.sum(hidden.astype(F32) * cot_wide, axis=1)
    scaled = share[:, None] * cot_wide
    gate_cot = (scaled * up_pre * sig * (1.0 + gate_pre * (1.0 - sig))).astype(BF)
    up_cot = (scaled * activated).astype(BF)

    far = jnp.zeros((n_tensor, 2 * rows, CAP), BF)
    for k in range(n_tensor):
        got = over_tensor(far_piece, k) if k else far_piece
        far = lax.dynamic_update_index_in_dim(far, got, t ^ k, 0)
    near4 = near.reshape(n_tensor, 4, rows, CAP)
    far2 = far.reshape(n_tensor, 2, rows, CAP)
    mine = lambda a, i: lax.dynamic_index_in_dim(a, i, 1, keepdims=False)
    own_rows = mine(near4, xh * 2 + core)
    own_far = mine(far2, core)
    sib_rows = over_dp(mine(near4, xh * 2 + 1 - core), 1)
    sib_far = over_dp(mine(far2, 1 - core), 1)
    left = jnp.concatenate([own_rows, sib_rows, own_far, sib_far], axis=2)
    left = left.reshape(n_tensor * rows, 4 * CAP)

    cots = jnp.concatenate([gate_cot, up_cot], axis=1)
    far_cots = over_dp(cots, 2)
    sib_cots = over_dp(cots, 1)
    sib_far_cots = over_dp(far_cots, 1)
    right = jnp.concatenate([cots, sib_cots, far_cots, sib_far_cots], axis=0)
    part = jnp.dot(left, right, preferred_element_type=F32).astype(BF)
    groups = [[4 * z + q for z in range(n_z)] for q in range(4)]
    summed = lax.psum_scatter(
        part, "dp", scatter_dimension=0, tiled=True, axis_index_groups=groups
    )

    last = (((1,), (1,)), ((), ()))
    total = jnp.zeros((CAP, piece), F32)
    for k in range(n_tensor):
        wg = lax.dynamic_slice_in_dim(w_gate, (t ^ k) * piece, piece, 0)
        wu = lax.dynamic_slice_in_dim(w_up, (t ^ k) * piece, piece, 0)
        out = lax.dot_general(gate_cot, wg, last, preferred_element_type=F32)
        out = out + lax.dot_general(up_cot, wu, last, preferred_element_type=F32)
        total = total + (over_tensor(out.astype(BF), k).astype(F32) if k else out)
    token_grad = lax.dot_general(
        dispatch, total.astype(BF), (((0,), (0,)), ((), ())), preferred_element_type=F32
    ).astype(BF)

    for k in (1, 2, 4):
        route_part = route_part + over_tensor(route_part, k)
    route_grad = jnp.sum(jnp.where(mask, route_part[:, None], 0.0), axis=0)
    return token_grad, summed[:, :width], summed[:, width:], route_grad


def solution(mesh):
    return jax.shard_map(
        on_device,
        mesh=mesh,
        in_specs=(
            P("dp", "tensor"),
            P("dp", "tensor"),
            P(None, "tensor"),
            P(None, "tensor"),
            P("dp", None),
            P("dp", None),
        ),
        out_specs=(P("dp", "tensor"), P("dp", "tensor"), P("dp", "tensor"), P("dp")),
        check_vma=False,
    )
```

```python
import jax
import jax.numpy as jnp
from jax import lax
from jax.experimental import pallas as pl
from jax.experimental.pallas import tpu as pltpu
from jax.sharding import PartitionSpec as P

CAP = 256
CHUNKS = 2
BF = jnp.bfloat16
F32 = jnp.float32
VMEM_BYTES = 48 * 2**20


def whole(shape):
    return pl.BlockSpec(shape, lambda *_: (0,) * len(shape))


def forward_kernel(n, piece, info, *refs):
    pieces = refs[:n]
    wg, wu, cot, share, gate_out, up_out, route_out, left = refs[n:]
    step = pl.program_id(0)

    @pl.when(step == 0)
    def _():
        for k in range(n):
            at = pl.multiple_of((info[0] ^ k) * piece, piece)
            left[:, pl.ds(at, piece)] = pieces[k][...]
        route_out[...] = jnp.zeros_like(route_out)

    gate = jnp.dot(left[...], wg[...], preferred_element_type=F32)
    up = jnp.dot(left[...], wu[...], preferred_element_type=F32)
    sig = jax.nn.sigmoid(gate)
    activated = gate * sig
    hidden = (activated * up).astype(BF).astype(F32)
    cot_wide = cot[...].astype(F32)
    route_out[...] += jnp.sum(hidden * cot_wide, axis=1, keepdims=True)
    scaled = share[...] * cot_wide
    gate_out[...] = (scaled * up * sig * (1.0 + gate * (1.0 - sig))).astype(BF)
    up_out[...] = (scaled * activated).astype(BF)


def forward(info, pieces, w_gate, w_up, cot_rows, share):
    n = len(pieces)
    cap, piece = pieces[0].shape
    d, width = w_gate.shape
    block = width // 4
    cols = lambda rows: pl.BlockSpec((rows, block), lambda j, *_: (0, j))
    return pl.pallas_call(
        lambda *a: forward_kernel(n, piece, *a),
        grid_spec=pltpu.PrefetchScalarGridSpec(
            num_scalar_prefetch=1,
            grid=(4,),
            in_specs=[whole((cap, piece))] * n + [cols(d), cols(d), cols(cap), whole((cap, 1))],
            out_specs=[cols(cap), cols(cap), whole((cap, 1))],
            scratch_shapes=[pltpu.VMEM((cap, d), BF)],
        ),
        out_shape=[
            jax.ShapeDtypeStruct((cap, width), BF),
            jax.ShapeDtypeStruct((cap, width), BF),
            jax.ShapeDtypeStruct((cap, 1), F32),
        ],
        compiler_params=pltpu.CompilerParams(vmem_limit_bytes=VMEM_BYTES),
        cost_estimate=pl.CostEstimate(
            flops=4 * cap * d * width, bytes_accessed=4 * d * width, transcendentals=cap * width
        ),
    )(info, *pieces, w_gate, w_up, cot_rows, share)


def back_kernel(info, gc, uc, wg, wu, own, sent):
    step = pl.program_id(0)
    last = (((1,), (1,)), ((), ()))
    out = lax.dot_general(gc[...], wg[...], last, preferred_element_type=F32)
    out += lax.dot_general(uc[...], wu[...], last, preferred_element_type=F32)

    @pl.when(step == 0)
    def _():
        own[...] = out

    sent[0] = out.astype(BF)


def token_parts(info, gate_cot, up_cot, w_gate, w_up, n):
    cap, width = gate_cot.shape
    d = w_gate.shape[0]
    piece = d // n
    weight = pl.BlockSpec((piece, width), lambda k, s: (s[0] ^ k, 0))
    return pl.pallas_call(
        back_kernel,
        grid_spec=pltpu.PrefetchScalarGridSpec(
            num_scalar_prefetch=1,
            grid=(n,),
            in_specs=[whole((cap, width)), whole((cap, width)), weight, weight],
            out_specs=[
                whole((cap, piece)),
                pl.BlockSpec((1, cap, piece), lambda k, s: (k, 0, 0)),
            ],
        ),
        out_shape=[
            jax.ShapeDtypeStruct((cap, piece), F32),
            jax.ShapeDtypeStruct((n, cap, piece), BF),
        ],
        compiler_params=pltpu.CompilerParams(vmem_limit_bytes=VMEM_BYTES),
        cost_estimate=pl.CostEstimate(
            flops=4 * cap * d * width, bytes_accessed=4 * d * width, transcendentals=0
        ),
    )(info, gate_cot, up_cot, w_gate, w_up)


def assemble_kernel(n, n_z, info, *refs):
    near, far = refs[:n], refs[n : 2 * n]
    out, turned = refs[2 * n :]
    rows, cap = far[0].shape
    for k in range(n):
        at = lax.rem((info[0] ^ k) - info[1] + n_z, n_z)
        turned[...] = near[k][...].T
        start = pl.multiple_of(info[2] * rows, rows)
        out[at, :, :cap] = turned[pl.ds(start, rows), :]
        out[at, :, cap:] = far[k][...]


def assemble(info, near, far, n_z):
    n = len(near)
    cap, piece = near[0].shape
    rows = far[0].shape[0]
    return pl.pallas_call(
        lambda *a: assemble_kernel(n, n_z, *a),
        grid_spec=pltpu.PrefetchScalarGridSpec(
            num_scalar_prefetch=1,
            grid=(1,),
            in_specs=[whole((cap, piece))] * n + [whole((rows, cap))] * n,
            out_specs=whole((n_z, rows, 2 * cap)),
            scratch_shapes=[pltpu.VMEM((piece, cap), BF)],
        ),
        out_shape=jax.ShapeDtypeStruct((n_z, rows, 2 * cap), BF),
        compiler_params=pltpu.CompilerParams(vmem_limit_bytes=VMEM_BYTES),
        cost_estimate=pl.CostEstimate(
            flops=0, bytes_accessed=8 * n * piece * cap, transcendentals=0
        ),
    )(info, *near, *far)


def on_device(tokens, hidden_cot, w_gate, w_up, expert_ids, route_fixed):
    tok_dev, piece = tokens.shape
    width = w_gate.shape[1]
    n_tensor = lax.axis_size("tensor")
    n_dp = lax.axis_size("dp")
    n_z = n_dp // 4
    half = piece // 2
    t = lax.axis_index("tensor")
    dp = lax.axis_index("dp")
    z, xh, core = dp // 4, (dp // 2) % 2, dp % 2
    info = jnp.stack([t, z, xh, core]).astype(jnp.int32)

    def over_tensor(x, k):
        return lax.ppermute(x, "tensor", [(i, i ^ k) for i in range(n_tensor)])

    def over_dp(x, k):
        return lax.ppermute(x, "dp", [(i, i ^ k) for i in range(n_dp)])

    def along_z(x, k):
        return lax.ppermute(x, "dp", [(i, (i + 4 * k) % n_dp) for i in range(n_dp)])

    selected = expert_ids == 0
    flag = jnp.any(selected, axis=1)
    place = jnp.arange(tok_dev, dtype=jnp.int32)
    upto = (place[:, None] <= place[None, :]).astype(BF)
    slot_of = jnp.dot(flag.astype(BF)[None, :], upto, preferred_element_type=F32)[0] - 1.0
    slot_of = jnp.where(flag, slot_of.astype(jnp.int32), -1)
    mask = slot_of[None, :] == jnp.arange(CAP, dtype=jnp.int32)[:, None]
    dispatch = mask.astype(BF)
    share_all = jnp.sum(jnp.where(selected, route_fixed, 0), axis=1).astype(F32) / 65536.0
    share = jnp.sum(jnp.where(mask, share_all[None, :], 0.0), axis=1, keepdims=True)

    picked = jnp.dot(dispatch, tokens, preferred_element_type=F32).astype(BF)
    turned = lax.dot_general(
        tokens, dispatch, (((0,), (1,)), ((), ())), preferred_element_type=F32
    ).astype(BF)
    far_piece = over_dp(lax.dynamic_slice_in_dim(turned, (1 - xh) * half, half, 0), 2)
    near = [over_tensor(picked, k) if k else picked for k in range(n_tensor)]
    cot_rows = jnp.dot(dispatch, hidden_cot, preferred_element_type=F32).astype(BF)

    near, far_piece = lax.optimization_barrier((near, far_piece))
    far = [over_tensor(far_piece, k) if k else far_piece for k in range(n_tensor)]
    gate_cot, up_cot, route_part = forward(info, near, w_gate, w_up, cot_rows, share)
    gate_cot, up_cot, route_part, far = lax.optimization_barrier(
        (gate_cot, up_cot, route_part, far)
    )

    step = width // CHUNKS
    ours = jnp.where(core == 0, gate_cot, up_cot)
    theirs = jnp.where(core == 0, up_cot, gate_cot)
    rights, fars = [], []
    for c in range(CHUNKS):
        cut = lambda a: a[:, c * step : (c + 1) * step]
        right = jnp.concatenate([cut(ours), over_dp(cut(theirs), 1)], axis=0)
        if c:
            right, fars[-1] = lax.optimization_barrier((right, fars[-1]))
        rights.append(right)
        fars.append(over_dp(right, 2))

    left = assemble(info, near, far, n_z)
    left_sib = over_dp(left, 1)
    near_left = jnp.concatenate([left[:, :, :CAP], left_sib[:, :, :CAP]], axis=2)
    far_left = jnp.concatenate([left[:, :, CAP:], left_sib[:, :, CAP:]], axis=2)
    own_part, sent = token_parts(info, gate_cot, up_cot, w_gate, w_up, n_tensor)

    gate_grads, up_grads = [], []
    for c in range(CHUNKS):
        base = jnp.dot(
            near_left.reshape(n_z * half, 2 * CAP), rights[c], preferred_element_type=F32
        ).reshape(n_z, half, step)

        def part(j, c=c, base=base):
            return base[j] + jnp.dot(far_left[j], fars[c], preferred_element_type=F32)

        up_hops = n_z // 2 - c % 2
        down_hops = n_z - 1 - up_hops
        rising = along_z(part(up_hops).astype(BF), 1)
        falling = along_z(part(n_z - down_hops).astype(BF), -1)
        for i in range(1, max(up_hops, down_hops)):
            if i < up_hops:
                rising = along_z((part(up_hops - i) + rising.astype(F32)).astype(BF), 1)
            if i < down_hops:
                falling = along_z((part(n_z - down_hops + i) + falling.astype(F32)).astype(BF), -1)
        total = (part(0) + rising.astype(F32) + falling.astype(F32)).astype(BF)
        total = total.reshape(2, half // 2, step)
        mine = lax.dynamic_index_in_dim(total, core, 0, keepdims=False)
        other = over_dp(lax.dynamic_index_in_dim(total, 1 - core, 0, keepdims=False), 1)
        gate_grads.append(jnp.where(core == 0, mine, other))
        up_grads.append(jnp.where(core == 0, other, mine))
    gate_grad = jnp.concatenate(gate_grads, axis=1)
    up_grad = jnp.concatenate(up_grads, axis=1)

    sent, route_part, _ = lax.optimization_barrier((sent, route_part, fars[-1]))
    total = own_part
    for k in range(1, n_tensor):
        total = total + over_tensor(sent[k], k).astype(F32)
    token_grad = lax.dot_general(
        dispatch, total.astype(BF), (((0,), (0,)), ((), ())), preferred_element_type=F32
    ).astype(BF)
    route_part = route_part[:, 0]
    for k in (1, 2, 4):
        route_part = route_part + over_tensor(route_part, k)
    route_grad = jnp.sum(jnp.where(mask, route_part[:, None], 0.0), axis=0)
    return token_grad, gate_grad, up_grad, route_grad


def solution(mesh):
    return jax.shard_map(
        on_device,
        mesh=mesh,
        in_specs=(
            P("dp", "tensor"),
            P("dp", "tensor"),
            P(None, "tensor"),
            P(None, "tensor"),
            P("dp", None),
            P("dp", None),
        ),
        out_specs=(P("dp", "tensor"), P("dp", "tensor"), P("dp", "tensor"), P("dp")),
        check_vma=False,
    )
```

```python
import jax
import jax.numpy as jnp
from jax import lax
from jax.experimental import pallas as pl
from jax.experimental.pallas import tpu as pltpu
from jax.sharding import PartitionSpec as P

CAP = 256
CHUNKS = 2
BF = jnp.bfloat16
F32 = jnp.float32
MIB = 2**20


def whole(shape):
    return pl.BlockSpec(shape, lambda *_: (0,) * len(shape))


def dispatch_kernel(info, slots, tokens, picked, far, turned):
    cap, rows = picked.shape[0], far.shape[0]
    tok_dev = slots.shape[1]
    ids = lax.broadcasted_iota(jnp.int32, (cap, tok_dev), 0)
    mask = (slots[...] == ids).astype(F32).astype(BF)
    got = jnp.dot(mask, tokens[...], preferred_element_type=F32)
    picked[...] = got.astype(BF)
    turned[...] = got.T.astype(BF)
    start = pl.multiple_of((1 - info[2]) * rows, rows)
    far[...] = turned[pl.ds(start, rows), :]


def dispatch_tokens(info, slots, tokens):
    tok_dev, piece = tokens.shape
    return pl.pallas_call(
        dispatch_kernel,
        grid_spec=pltpu.PrefetchScalarGridSpec(
            num_scalar_prefetch=1,
            grid=(1,),
            in_specs=[whole((1, tok_dev)), whole((tok_dev, piece))],
            out_specs=[whole((CAP, piece)), whole((piece // 2, CAP))],
            scratch_shapes=[pltpu.VMEM((piece, CAP), BF)],
        ),
        out_shape=[
            jax.ShapeDtypeStruct((CAP, piece), BF),
            jax.ShapeDtypeStruct((piece // 2, CAP), BF),
        ],
        compiler_params=pltpu.CompilerParams(vmem_limit_bytes=8 * MIB),
        cost_estimate=pl.CostEstimate(
            flops=2 * CAP * tok_dev * piece, bytes_accessed=4 * tok_dev * piece, transcendentals=0
        ),
    )(info, slots, tokens)


def forward_kernel(n, piece, info, *refs):
    pieces = refs[:n]
    wg, wu, cot, share, mine, other, route_out, left = refs[n:]
    step = pl.program_id(0)

    @pl.when(step == 0)
    def _():
        for k in range(n):
            at = pl.multiple_of((info[0] ^ k) * piece, piece)
            left[:, pl.ds(at, piece)] = pieces[k][...]
        route_out[...] = jnp.zeros_like(route_out)

    gate = jnp.dot(left[...], wg[...], preferred_element_type=F32)
    up = jnp.dot(left[...], wu[...], preferred_element_type=F32)
    sig = jax.nn.sigmoid(gate)
    activated = gate * sig
    hidden = (activated * up).astype(BF).astype(F32)
    cot_wide = cot[...].astype(F32)
    route_out[...] += jnp.sum(hidden * cot_wide, axis=1, keepdims=True)
    scaled = share[...] * cot_wide
    gate_cot = scaled * up * sig * (1.0 + gate * (1.0 - sig))
    up_cot = scaled * activated
    first = info[3] == 0
    mine[0] = jnp.where(first, gate_cot, up_cot).astype(BF)
    other[0] = jnp.where(first, up_cot, gate_cot).astype(BF)


def forward(info, pieces, w_gate, w_up, cot_rows, share):
    n = len(pieces)
    cap, piece = pieces[0].shape
    d, width = w_gate.shape
    steps = 4
    block = width // steps
    per = steps // CHUNKS
    cols = lambda rows: pl.BlockSpec((rows, block), lambda j, *_: (0, j))
    out = pl.BlockSpec((1, cap, block), lambda j, *_: (j // per, 0, j % per))
    cots = jax.ShapeDtypeStruct((CHUNKS, cap, width // CHUNKS), BF)
    return pl.pallas_call(
        lambda *a: forward_kernel(n, piece, *a),
        grid_spec=pltpu.PrefetchScalarGridSpec(
            num_scalar_prefetch=1,
            grid=(steps,),
            in_specs=[whole((cap, piece))] * n + [cols(d), cols(d), cols(cap), whole((cap, 1))],
            out_specs=[out, out, whole((cap, 1))],
            scratch_shapes=[pltpu.VMEM((cap, d), BF)],
        ),
        out_shape=[cots, cots, jax.ShapeDtypeStruct((cap, 1), F32)],
        compiler_params=pltpu.CompilerParams(vmem_limit_bytes=20 * MIB),
        cost_estimate=pl.CostEstimate(
            flops=4 * cap * d * width, bytes_accessed=4 * d * width, transcendentals=cap * width
        ),
    )(info, *pieces, w_gate, w_up, cot_rows, share)


def back_kernel(info, mine, other, wg, wu, own, sent, gt, ut):
    step = pl.program_id(0)
    chunk = mine.shape[2]

    @pl.when(step == 0)
    def _():
        first = info[3] == 0
        for c in range(mine.shape[0]):
            a, b = mine[c], other[c]
            gt[pl.ds(c * chunk, chunk), :] = jnp.where(first, a, b).T
            ut[pl.ds(c * chunk, chunk), :] = jnp.where(first, b, a).T

    out = jnp.dot(wg[...], gt[...], preferred_element_type=F32)
    out += jnp.dot(wu[...], ut[...], preferred_element_type=F32)

    @pl.when(step == 0)
    def _():
        own[0] = out

    @pl.when(step == 1)
    def _():
        own[1] = out

    sent[0] = out.astype(BF)


def token_parts(info, mine, other, w_gate, w_up, n):
    chunks, cap, chunk = mine.shape
    d, width = w_gate.shape
    piece = d // n
    far = n // 2
    place = lambda k: (k % 2) * far + k // 2
    weight = pl.BlockSpec((piece, width), lambda k, s: (s[0] ^ place(k), 0))
    return pl.pallas_call(
        back_kernel,
        grid_spec=pltpu.PrefetchScalarGridSpec(
            num_scalar_prefetch=1,
            grid=(n,),
            in_specs=[whole(mine.shape), whole(other.shape), weight, weight],
            out_specs=[
                whole((2, piece, cap)),
                pl.BlockSpec((1, piece, cap), lambda k, s: (k, 0, 0)),
            ],
            scratch_shapes=[pltpu.VMEM((width, cap), BF), pltpu.VMEM((width, cap), BF)],
        ),
        out_shape=[
            jax.ShapeDtypeStruct((2, piece, cap), F32),
            jax.ShapeDtypeStruct((n, piece, cap), BF),
        ],
        compiler_params=pltpu.CompilerParams(vmem_limit_bytes=16 * MIB),
        cost_estimate=pl.CostEstimate(
            flops=4 * cap * d * width, bytes_accessed=4 * d * width, transcendentals=0
        ),
    )(info, mine, other, w_gate, w_up)


def near_kernel(n, n_z, info, *refs):
    near = refs[:n]
    out, turned = refs[n:]
    rows = out.shape[1]
    for k in range(n):
        at = lax.rem((info[0] ^ k) - info[1] + n_z, n_z)
        turned[...] = near[k][...].T
        start = pl.multiple_of(info[2] * rows, rows)
        out[at] = turned[pl.ds(start, rows), :]


def far_kernel(n, n_z, info, *refs):
    out = refs[-1]
    for y in range(n // 2):
        for x in range(2):
            at = lax.rem((info[0] ^ (y + x * (n // 2))) - info[1] + n_z, n_z)
            out[at] = refs[y][x]


def placed(kernel, info, arrays, rows, cap, n, n_z, scratch):
    return pl.pallas_call(
        lambda *a: kernel(n, n_z, *a),
        grid_spec=pltpu.PrefetchScalarGridSpec(
            num_scalar_prefetch=1,
            grid=(1,),
            in_specs=[whole(a.shape) for a in arrays],
            out_specs=whole((n_z, rows, cap)),
            scratch_shapes=scratch,
        ),
        out_shape=jax.ShapeDtypeStruct((n_z, rows, cap), BF),
        compiler_params=pltpu.CompilerParams(vmem_limit_bytes=12 * MIB),
        cost_estimate=pl.CostEstimate(
            flops=0, bytes_accessed=8 * n * rows * cap, transcendentals=0
        ),
    )(info, *arrays)


def on_device(tokens, hidden_cot, w_gate, w_up, expert_ids, route_fixed):
    tok_dev, piece = tokens.shape
    width = w_gate.shape[1]
    n_tensor = lax.axis_size("tensor")
    n_dp = lax.axis_size("dp")
    n_z = n_dp // 4
    half = piece // 2
    xlo = n_tensor // 2
    t = lax.axis_index("tensor")
    dp = lax.axis_index("dp")
    z, xh, core = dp // 4, (dp // 2) % 2, dp % 2
    info = jnp.stack([t, z, xh, core]).astype(jnp.int32)
    tie = lax.optimization_barrier

    def over_tensor(x, k):
        return lax.ppermute(x, "tensor", [(i, i ^ k) for i in range(n_tensor)])

    def over_dp(x, k):
        return lax.ppermute(x, "dp", [(i, i ^ k) for i in range(n_dp)])

    def along_z(x, k):
        return lax.ppermute(x, "dp", [(i, (i + 4 * k) % n_dp) for i in range(n_dp)])

    selected = expert_ids == 0
    flag = jnp.any(selected, axis=1)
    place = jnp.arange(tok_dev, dtype=jnp.int32)
    upto = (place[:, None] <= place[None, :]).astype(BF)
    slot_of = jnp.dot(flag.astype(BF)[None, :], upto, preferred_element_type=F32)[0] - 1.0
    slot_of = jnp.where(flag, slot_of.astype(jnp.int32), -1)
    mask = slot_of[None, :] == jnp.arange(CAP, dtype=jnp.int32)[:, None]
    dispatch = mask.astype(BF)
    share_all = jnp.sum(jnp.where(selected, route_fixed, 0), axis=1).astype(F32) / 65536.0
    share = jnp.sum(jnp.where(mask, share_all[None, :], 0.0), axis=1, keepdims=True)

    picked, far_piece = dispatch_tokens(info, slot_of[None, :], tokens)
    near = [None] * n_tensor
    near[0] = picked
    near[xlo] = over_tensor(picked, xlo)
    near[1] = over_tensor(picked, 1)
    near[3] = over_tensor(picked, 3)
    near[2] = over_tensor(picked, 2)
    near[xlo + 2] = over_tensor(near[xlo], 2)
    near[xlo + 1] = over_tensor(near[1], xlo)
    near[xlo + 3] = over_tensor(near[3], xlo)
    far_piece = over_dp(far_piece, 2)
    cot_rows = jnp.dot(dispatch, hidden_cot, preferred_element_type=F32).astype(BF)
    near, far_piece = tie((near, far_piece))

    mine, other, route_part = forward(info, near, w_gate, w_up, cot_rows, share)
    far_pair = jnp.stack([far_piece, over_tensor(far_piece, xlo)])
    far = [over_tensor(far_pair, k) if k else far_pair for k in range(xlo)]

    step = width // CHUNKS
    rights, fars = [], []
    for c in range(CHUNKS):
        right = jnp.concatenate([mine[c], over_dp(other[c], 1)], axis=0)
        if c:
            right, fars[-1] = tie((right, fars[-1]))
        rights.append(right)
        fars.append(over_dp(right, 2))

    near_left = placed(
        near_kernel, info, near, half, CAP, n_tensor, n_z, [pltpu.VMEM((piece, CAP), BF)]
    )
    near_sib = over_dp(near_left, 1)
    far_left = placed(far_kernel, info, far, half, CAP, n_tensor, n_z, [])
    far_sib = over_dp(far_left, 1)
    mine_b, other_b, right_b = tie((mine, other, rights[0]))
    own_part, sent = token_parts(info, mine_b, other_b, w_gate, w_up, n_tensor)
    sums = {}
    for k in (1, 3, 2):
        message = sent[2 * k : 2 * k + 2]
        if k == 2:
            message, fars[-1] = tie((message, fars[-1]))
        sums[k] = over_tensor(message, k)

    def product(a, b):
        return jnp.dot(a, b, preferred_element_type=F32)

    gate_grads, up_grads = [], []
    for c in range(CHUNKS):
        flat = lambda a: a.reshape(n_z * half, CAP)
        base = product(flat(near_left), rights[c][:CAP])
        base = (base + product(flat(near_sib), rights[c][CAP:])).reshape(n_z, half, step)

        def part(j, c=c, base=base):
            out = base[j] + product(far_left[j], fars[c][:CAP])
            return out + product(far_sib[j], fars[c][CAP:])

        up_hops = n_z // 2 - c % 2
        down_hops = n_z - 1 - up_hops
        rising = along_z(part(up_hops).astype(BF), 1)
        falling = along_z(part(n_z - down_hops).astype(BF), -1)
        for i in range(1, max(up_hops, down_hops)):
            if i < up_hops:
                rising = along_z((part(up_hops - i) + rising.astype(F32)).astype(BF), 1)
            if i < down_hops:
                falling = along_z((part(n_z - down_hops + i) + falling.astype(F32)).astype(BF), -1)
        total = (part(0) + rising.astype(F32) + falling.astype(F32)).astype(BF)
        total = total.reshape(2, half // 2, step)
        kept = lax.dynamic_index_in_dim(total, core, 0, keepdims=False)
        swapped = over_dp(lax.dynamic_index_in_dim(total, 1 - core, 0, keepdims=False), 1)
        gate_grads.append(jnp.where(core == 0, kept, swapped))
        up_grads.append(jnp.where(core == 0, swapped, kept))
    gate_grad = jnp.concatenate(gate_grads, axis=1)
    up_grad = jnp.concatenate(up_grads, axis=1)

    total = own_part
    for k in (1, 2, 3):
        total = total + sums[k].astype(F32)
    total = total[0] + over_tensor(total[1].astype(BF), xlo).astype(F32)
    token_grad = lax.dot_general(
        dispatch, total.astype(BF), (((0,), (1,)), ((), ())), preferred_element_type=F32
    ).astype(BF)
    route_part, _ = tie((route_part[:, 0], right_b))
    for k in (1, 2, 4):
        route_part = route_part + over_tensor(route_part, k)
    route_grad = jnp.sum(jnp.where(mask, route_part[:, None], 0.0), axis=0)
    return token_grad, gate_grad, up_grad, route_grad


def solution(mesh):
    return jax.shard_map(
        on_device,
        mesh=mesh,
        in_specs=(
            P("dp", "tensor"),
            P("dp", "tensor"),
            P(None, "tensor"),
            P(None, "tensor"),
            P("dp", None),
            P("dp", None),
        ),
        out_specs=(P("dp", "tensor"), P("dp", "tensor"), P("dp", "tensor"), P("dp")),
        check_vma=False,
    )
```

```python
import jax
import jax.numpy as jnp
from jax import lax
from jax.experimental import pallas as pl
from jax.experimental.pallas import tpu as pltpu
from jax.sharding import PartitionSpec as P

CAP = 256
CHUNKS = 2
BF = jnp.bfloat16
F32 = jnp.float32
MIB = 2**20


def whole(shape):
    return pl.BlockSpec(shape, lambda *_: (0,) * len(shape))


def dispatch_kernel(info, slots, tokens, picked, far, turned):
    cap, rows = picked.shape[0], far.shape[0]
    tok_dev = slots.shape[1]
    ids = lax.broadcasted_iota(jnp.int32, (cap, tok_dev), 0)
    mask = (slots[...] == ids).astype(F32).astype(BF)
    got = jnp.dot(mask, tokens[...], preferred_element_type=F32)
    picked[...] = got.astype(BF)
    turned[...] = got.T.astype(BF)
    start = pl.multiple_of((1 - info[2]) * rows, rows)
    far[...] = turned[pl.ds(start, rows), :]


def dispatch_tokens(info, slots, tokens):
    tok_dev, piece = tokens.shape
    return pl.pallas_call(
        dispatch_kernel,
        grid_spec=pltpu.PrefetchScalarGridSpec(
            num_scalar_prefetch=1,
            grid=(1,),
            in_specs=[whole((1, tok_dev)), whole((tok_dev, piece))],
            out_specs=[whole((CAP, piece)), whole((piece // 2, CAP))],
            scratch_shapes=[pltpu.VMEM((piece, CAP), BF)],
        ),
        out_shape=[
            jax.ShapeDtypeStruct((CAP, piece), BF),
            jax.ShapeDtypeStruct((piece // 2, CAP), BF),
        ],
        compiler_params=pltpu.CompilerParams(vmem_limit_bytes=8 * MIB),
        cost_estimate=pl.CostEstimate(
            flops=2 * CAP * tok_dev * piece, bytes_accessed=4 * tok_dev * piece, transcendentals=0
        ),
    )(info, slots, tokens)


def cot_kernel(slots, share_all, cot, rows, share):
    cap, tok_dev = rows.shape[0], slots.shape[1]
    mask = slots[...] == lax.broadcasted_iota(jnp.int32, (cap, tok_dev), 0)
    hot = mask.astype(F32).astype(BF)
    rows[...] = jnp.dot(hot, cot[...], preferred_element_type=F32).astype(BF)
    share[...] = jnp.sum(jnp.where(mask, share_all[...], 0.0), axis=1, keepdims=True)


def dispatch_cots(slots, share_all, hidden_cot):
    tok_dev, width = hidden_cot.shape
    return pl.pallas_call(
        cot_kernel,
        out_shape=[
            jax.ShapeDtypeStruct((CAP, width), BF),
            jax.ShapeDtypeStruct((CAP, 1), F32),
        ],
        compiler_params=pltpu.CompilerParams(vmem_limit_bytes=8 * MIB),
        cost_estimate=pl.CostEstimate(
            flops=2 * CAP * tok_dev * width, bytes_accessed=4 * tok_dev * width, transcendentals=0
        ),
    )(slots, share_all, hidden_cot)


def forward_kernel(n, n_z, piece, info, *refs):
    pieces = refs[:n]
    wg, wu, cot, share = refs[n : n + 4]
    mine, other = refs[n + 4 : n + 4 + CHUNKS], refs[n + 4 + CHUNKS : n + 4 + 2 * CHUNKS]
    near_left, route_out, left, turned = refs[n + 4 + 2 * CHUNKS :]
    step = pl.program_id(0)
    half, block = near_left.shape[1], wg.shape[1]
    per = mine[0].shape[1] // block

    @pl.when(step == 0)
    def _():
        for k in range(n):
            at = pl.multiple_of((info[0] ^ k) * piece, piece)
            left[:, pl.ds(at, piece)] = pieces[k][...]
        route_out[...] = jnp.zeros_like(route_out)

    gate = jnp.dot(left[...], wg[...], preferred_element_type=F32)
    up = jnp.dot(left[...], wu[...], preferred_element_type=F32)
    sig = jax.nn.sigmoid(gate)
    activated = gate * sig
    hidden = (activated * up).astype(BF).astype(F32)
    cot_wide = cot[...].astype(F32)
    route_out[...] += jnp.sum(hidden * cot_wide, axis=1, keepdims=True)
    scaled = share[...] * cot_wide
    gate_cot = scaled * up * sig * (1.0 + gate * (1.0 - sig))
    up_cot = scaled * activated
    first = info[3] == 0
    for j in range(per * CHUNKS):

        @pl.when(step == j)
        def _(j=j):
            cols = slice(j % per * block, (j % per + 1) * block)
            mine[j // per][:, cols] = jnp.where(first, gate_cot, up_cot).astype(BF)
            other[j // per][:, cols] = jnp.where(first, up_cot, gate_cot).astype(BF)
            for k in range(j * n // (per * CHUNKS), (j + 1) * n // (per * CHUNKS)):
                at = lax.rem((info[0] ^ k) - info[1] + n_z, n_z)
                turned[...] = pieces[k][...].T
                start = pl.multiple_of(info[2] * half, half)
                near_left[at] = turned[pl.ds(start, half), :]


def forward(info, pieces, w_gate, w_up, cot_rows, share, n_z):
    n = len(pieces)
    cap, piece = pieces[0].shape
    d, width = w_gate.shape
    steps = 4
    block = width // steps
    cols = lambda rows: pl.BlockSpec((rows, block), lambda j, *_: (0, j))
    chunk = (cap, width // CHUNKS)
    near_left = (n_z, piece // 2, cap)
    outs = [(chunk, BF)] * (2 * CHUNKS) + [(near_left, BF), ((cap, 1), F32)]
    return pl.pallas_call(
        lambda *a: forward_kernel(n, n_z, piece, *a),
        grid_spec=pltpu.PrefetchScalarGridSpec(
            num_scalar_prefetch=1,
            grid=(steps,),
            in_specs=[whole((cap, piece))] * n + [cols(d), cols(d), cols(cap), whole((cap, 1))],
            out_specs=[whole(shape) for shape, _ in outs],
            scratch_shapes=[pltpu.VMEM((cap, d), BF), pltpu.VMEM((piece, cap), BF)],
        ),
        out_shape=[jax.ShapeDtypeStruct(shape, kind) for shape, kind in outs],
        compiler_params=pltpu.CompilerParams(vmem_limit_bytes=24 * MIB),
        cost_estimate=pl.CostEstimate(
            flops=4 * cap * d * width, bytes_accessed=4 * d * width, transcendentals=cap * width
        ),
    )(info, *pieces, w_gate, w_up, cot_rows, share)


def back_kernel(info, *refs):
    mine, other = refs[:CHUNKS], refs[CHUNKS : 2 * CHUNKS]
    wg, wu, own, sent, gt, ut = refs[2 * CHUNKS :]
    step = pl.program_id(0)
    chunk = mine[0].shape[1]

    @pl.when(step == 0)
    def _():
        first = info[3] == 0
        for c in range(CHUNKS):
            a, b = mine[c][...], other[c][...]
            gt[pl.ds(c * chunk, chunk), :] = jnp.where(first, a, b).T
            ut[pl.ds(c * chunk, chunk), :] = jnp.where(first, b, a).T

    out = jnp.dot(wg[...], gt[...], preferred_element_type=F32)
    out += jnp.dot(wu[...], ut[...], preferred_element_type=F32)

    @pl.when(step == 0)
    def _():
        own[0] = out

    @pl.when(step == 1)
    def _():
        own[1] = out

    sent[0] = out.astype(BF)


def token_parts(info, mine, other, w_gate, w_up, n):
    cap, chunk = mine[0].shape
    d, width = w_gate.shape
    piece = d // n
    far = n // 2
    place = lambda k: (k % 2) * far + k // 2
    weight = pl.BlockSpec((piece, width), lambda k, s: (s[0] ^ place(k), 0))
    return pl.pallas_call(
        back_kernel,
        grid_spec=pltpu.PrefetchScalarGridSpec(
            num_scalar_prefetch=1,
            grid=(n,),
            in_specs=[whole((cap, chunk))] * (2 * CHUNKS) + [weight, weight],
            out_specs=[
                whole((2, piece, cap)),
                pl.BlockSpec((1, piece, cap), lambda k, s: (k, 0, 0)),
            ],
            scratch_shapes=[pltpu.VMEM((width, cap), BF), pltpu.VMEM((width, cap), BF)],
        ),
        out_shape=[
            jax.ShapeDtypeStruct((2, piece, cap), F32),
            jax.ShapeDtypeStruct((n, piece, cap), BF),
        ],
        compiler_params=pltpu.CompilerParams(vmem_limit_bytes=16 * MIB),
        cost_estimate=pl.CostEstimate(
            flops=4 * cap * d * width, bytes_accessed=4 * d * width, transcendentals=0
        ),
    )(info, *mine, *other, w_gate, w_up)


def far_kernel(n, n_z, info, *refs):
    out = refs[-1]
    for y in range(n // 2):
        for x in range(2):
            at = lax.rem((info[0] ^ (y + x * (n // 2))) - info[1] + n_z, n_z)
            out[at] = refs[y][x]


def far_operand(info, arrays, n, n_z):
    rows, cap = arrays[0].shape[1:]
    return pl.pallas_call(
        lambda *a: far_kernel(n, n_z, *a),
        grid_spec=pltpu.PrefetchScalarGridSpec(
            num_scalar_prefetch=1,
            grid=(1,),
            in_specs=[whole(a.shape) for a in arrays],
            out_specs=whole((n_z, rows, cap)),
        ),
        out_shape=jax.ShapeDtypeStruct((n_z, rows, cap), BF),
        compiler_params=pltpu.CompilerParams(vmem_limit_bytes=8 * MIB),
        cost_estimate=pl.CostEstimate(
            flops=0, bytes_accessed=4 * n * rows * cap, transcendentals=0
        ),
    )(info, *arrays)


def on_device(tokens, hidden_cot, w_gate, w_up, expert_ids, route_fixed):
    tok_dev, piece = tokens.shape
    width = w_gate.shape[1]
    n_tensor = lax.axis_size("tensor")
    n_dp = lax.axis_size("dp")
    n_z = n_dp // 4
    half = piece // 2
    xlo = n_tensor // 2
    t = lax.axis_index("tensor")
    dp = lax.axis_index("dp")
    z, xh, core = dp // 4, (dp // 2) % 2, dp % 2
    info = jnp.stack([t, z, xh, core]).astype(jnp.int32)
    tie = lax.optimization_barrier

    def over_tensor(x, k):
        return lax.ppermute(x, "tensor", [(i, i ^ k) for i in range(n_tensor)])

    def over_dp(x, k):
        return lax.ppermute(x, "dp", [(i, i ^ k) for i in range(n_dp)])

    def along_z(x, k):
        return lax.ppermute(x, "dp", [(i, (i + 4 * k) % n_dp) for i in range(n_dp)])

    selected = expert_ids == 0
    flag = jnp.any(selected, axis=1)
    place = jnp.arange(tok_dev, dtype=jnp.int32)
    upto = (place[:, None] <= place[None, :]).astype(BF)
    slot_of = jnp.dot(flag.astype(BF)[None, :], upto, preferred_element_type=F32)[0] - 1.0
    slot_of = jnp.where(flag, slot_of.astype(jnp.int32), -1)
    mask = slot_of[None, :] == jnp.arange(CAP, dtype=jnp.int32)[:, None]
    dispatch = mask.astype(BF)
    share_all = jnp.sum(jnp.where(selected, route_fixed, 0), axis=1).astype(F32) / 65536.0

    picked, far_piece = dispatch_tokens(info, slot_of[None, :], tokens)
    near = [None] * n_tensor
    near[xlo] = over_tensor(picked, xlo)
    near[1] = over_tensor(picked, 1)
    near[3] = over_tensor(picked, 3)
    far_piece = over_dp(far_piece, 2)
    picked, near[1], near[3], near[xlo] = tie((picked, near[1], near[3], near[xlo]))
    near[0] = picked
    near[xlo + 1] = over_tensor(near[1], xlo)
    near[xlo + 3] = over_tensor(near[3], xlo)
    near[2] = over_tensor(picked, 2)
    near[xlo + 2] = over_tensor(near[xlo], 2)
    cot_rows, share = dispatch_cots(slot_of[None, :], share_all[None, :], hidden_cot)
    near, far_piece, cot_rows, share = tie((near, far_piece, cot_rows, share))

    w_gate = pltpu.with_memory_space_constraint(w_gate, pltpu.HBM)
    w_up = pltpu.with_memory_space_constraint(w_up, pltpu.HBM)
    outs = forward(info, near, w_gate, w_up, cot_rows, share, n_z)
    mine, other = outs[:CHUNKS], outs[CHUNKS : 2 * CHUNKS]
    near_left, route_part = outs[2 * CHUNKS :]

    def to_partners(c):
        return [mine[c], over_dp(other[c], 1), over_dp(mine[c], 2), over_dp(other[c], 3)]

    cots = [to_partners(0)]
    far_piece, near_left, mine, other, route_part, cots[0][1] = tie(
        (far_piece, near_left, mine, other, route_part, cots[0][1])
    )
    near_sib = over_dp(near_left, 1)
    far_pair = jnp.stack([far_piece, over_tensor(far_piece, xlo)])
    far = [over_tensor(far_pair, k) if k else far_pair for k in range(xlo)]
    far_left = far_operand(info, far, n_tensor, n_z)
    far_sib = over_dp(far_left, 1)
    own_part, sent = token_parts(info, mine, other, w_gate, w_up, n_tensor)
    for c in range(1, CHUNKS):
        mine, other, cots[-1] = tie((mine, other, cots[-1]))
        cots.append(to_partners(c))
    sums = {k: over_tensor(sent[2 * k : 2 * k + 2], k) for k in (1, 3)}

    def product(a, b):
        return jnp.dot(a, b, preferred_element_type=F32)

    class Ring:
        def __init__(self, c):
            flat = lambda a: a.reshape(n_z * half, CAP)
            self.c = c
            base = product(flat(near_left), cots[c][0]) + product(flat(near_sib), cots[c][1])
            self.base = base.reshape(n_z, half, width // CHUNKS)
            self.up_hops = n_z // 2 - c % 2
            self.down_hops = n_z - 1 - self.up_hops
            self.rising = self.falling = None

        def part(self, j):
            c = self.c
            out = self.base[j] + product(far_left[j], cots[c][2])
            return out + product(far_sib[j], cots[c][3])

        def hop(self, i):
            if i < self.up_hops:
                out = self.part(self.up_hops - i)
                out = out if i == 0 else out + self.rising.astype(F32)
                self.rising = along_z(out.astype(BF), 1)
            if i < self.down_hops:
                out = self.part((n_z - self.down_hops + i) % n_z)
                out = out if i == 0 else out + self.falling.astype(F32)
                self.falling = along_z(out.astype(BF), -1)

        def finish(self):
            total = self.part(0) + self.rising.astype(F32) + self.falling.astype(F32)
            total = total.astype(BF).reshape(2, half // 2, width // CHUNKS)
            kept = lax.dynamic_index_in_dim(total, core, 0, keepdims=False)
            swapped = over_dp(lax.dynamic_index_in_dim(total, 1 - core, 0, keepdims=False), 1)
            return jnp.where(core == 0, kept, swapped), jnp.where(core == 0, swapped, kept)

    rings = [Ring(c) for c in range(CHUNKS)]
    for i in range(n_z // 2):
        for ring in rings:
            ring.hop(i)
        if i == 0:
            message, rings[0].rising = tie((sent[4:6], rings[0].rising))
            sums[2] = over_tensor(message, 2)
        else:
            route_part, rings[0].rising = tie((route_part, rings[0].rising))
            if i == 1:
                route_part = route_part[:, 0]
            route_part = route_part + over_tensor(route_part, 1 << (i - 1))
    gate_grads, up_grads = zip(*[ring.finish() for ring in rings])
    gate_grad = jnp.concatenate(gate_grads, axis=1)
    up_grad = jnp.concatenate(up_grads, axis=1)

    total = own_part
    for k in (1, 2, 3):
        total = total + sums[k].astype(F32)
    total = total[0] + over_tensor(total[1].astype(BF), xlo).astype(F32)
    token_grad = lax.dot_general(
        dispatch, total.astype(BF), (((0,), (1,)), ((), ())), preferred_element_type=F32
    ).astype(BF)
    route_grad = jnp.sum(jnp.where(mask, route_part[:, None], 0.0), axis=0)
    return token_grad, gate_grad, up_grad, route_grad


def solution(mesh):
    return jax.shard_map(
        on_device,
        mesh=mesh,
        in_specs=(
            P("dp", "tensor"),
            P("dp", "tensor"),
            P(None, "tensor"),
            P(None, "tensor"),
            P("dp", None),
            P("dp", None),
        ),
        out_specs=(P("dp", "tensor"), P("dp", "tensor"), P("dp", "tensor"), P("dp")),
        check_vma=False,
    )
```

```python
import jax
import jax.numpy as jnp
from jax import lax
from jax.experimental import pallas as pl
from jax.experimental.pallas import tpu as pltpu
from jax.sharding import PartitionSpec as P

CAP = 256
CHUNKS = 2
BF = jnp.bfloat16
F32 = jnp.float32
MIB = 2**20


def whole(shape):
    return pl.BlockSpec(shape, lambda *_: (0,) * len(shape))


def dispatch_kernel(info, slots, tokens, picked, far, turned):
    cap, rows = picked.shape[0], far.shape[0]
    tok_dev = slots.shape[1]
    ids = lax.broadcasted_iota(jnp.int32, (cap, tok_dev), 0)
    mask = (slots[...] == ids).astype(F32).astype(BF)
    got = jnp.dot(mask, tokens[...], preferred_element_type=F32)
    picked[...] = got.astype(BF)
    turned[...] = got.T.astype(BF)
    start = pl.multiple_of((1 - info[2]) * rows, rows)
    far[...] = turned[pl.ds(start, rows), :]


def dispatch_tokens(info, slots, tokens):
    tok_dev, piece = tokens.shape
    return pl.pallas_call(
        dispatch_kernel,
        grid_spec=pltpu.PrefetchScalarGridSpec(
            num_scalar_prefetch=1,
            grid=(1,),
            in_specs=[whole((1, tok_dev)), whole((tok_dev, piece))],
            out_specs=[whole((CAP, piece)), whole((piece // 2, CAP))],
            scratch_shapes=[pltpu.VMEM((piece, CAP), BF)],
        ),
        out_shape=[
            jax.ShapeDtypeStruct((CAP, piece), BF),
            jax.ShapeDtypeStruct((piece // 2, CAP), BF),
        ],
        compiler_params=pltpu.CompilerParams(vmem_limit_bytes=8 * MIB),
        cost_estimate=pl.CostEstimate(
            flops=2 * CAP * tok_dev * piece, bytes_accessed=4 * tok_dev * piece, transcendentals=0
        ),
    )(info, slots, tokens)


def cot_kernel(slots, share_all, cot, rows, share):
    cap, tok_dev = rows.shape[0], slots.shape[1]
    mask = slots[...] == lax.broadcasted_iota(jnp.int32, (cap, tok_dev), 0)
    hot = mask.astype(F32).astype(BF)
    rows[...] = jnp.dot(hot, cot[...], preferred_element_type=F32).astype(BF)
    share[...] = jnp.sum(jnp.where(mask, share_all[...], 0.0), axis=1, keepdims=True)


def dispatch_cots(slots, share_all, hidden_cot):
    tok_dev, width = hidden_cot.shape
    return pl.pallas_call(
        cot_kernel,
        out_shape=[
            jax.ShapeDtypeStruct((CAP, width), BF),
            jax.ShapeDtypeStruct((CAP, 1), F32),
        ],
        compiler_params=pltpu.CompilerParams(vmem_limit_bytes=8 * MIB),
        cost_estimate=pl.CostEstimate(
            flops=2 * CAP * tok_dev * width, bytes_accessed=4 * tok_dev * width, transcendentals=0
        ),
    )(slots, share_all, hidden_cot)


def fetch(rows, wg, wu, held, sems, n, piece):
    for i in range(n):
        at = pl.multiple_of(rows[i] * piece, piece)
        for j, w in enumerate((wg, wu)):
            pltpu.make_async_copy(w.at[pl.ds(at, piece)], held.at[i, j], sems.at[i, j]).start()


def await_block(wg, wu, held, sems, i, piece):
    for j, w in enumerate((wg, wu)):
        pltpu.make_async_copy(w.at[pl.ds(0, piece)], held.at[i, j], sems.at[i, j]).wait()


def early_kernel(n, order, *refs):
    pieces = refs[:n]
    wg, wu, gate, up, later_wg, later_wu, held, sems, late_sems = refs[n:]
    piece = held.shape[2]
    fetch([order[i] for i in range(n)], wg, wu, held, sems, n, piece)
    late = []
    for i in range(n):
        at = pl.multiple_of(order[n + i] * piece, piece)
        for j, (w, to) in enumerate(((wg, later_wg), (wu, later_wu))):
            late.append(
                pltpu.make_async_copy(w.at[pl.ds(at, piece)], to.at[i], late_sems.at[i, j])
            )
            late[-1].start()
    for i in range(n):
        await_block(wg, wu, held, sems, i, piece)
        first = jnp.dot(pieces[i][...], held[i, 0], preferred_element_type=F32)
        second = jnp.dot(pieces[i][...], held[i, 1], preferred_element_type=F32)
        gate[...] = gate[...] + first if i else first
        up[...] = up[...] + second if i else second
    for copy in late:
        copy.wait()


def early(order, pieces, w_gate, w_up):
    n = len(pieces)
    cap, piece = pieces[0].shape
    width = w_gate.shape[1]
    hbm = pl.BlockSpec(memory_space=pl.ANY)
    return pl.pallas_call(
        lambda *a: early_kernel(n, *a),
        grid_spec=pltpu.PrefetchScalarGridSpec(
            num_scalar_prefetch=1,
            grid=(1,),
            in_specs=[whole((cap, piece))] * n + [hbm, hbm],
            out_specs=[whole((cap, width))] * 2
            + [pl.BlockSpec(memory_space=pltpu.VMEM)] * 2,
            scratch_shapes=[
                pltpu.VMEM((n, 2, piece, width), BF),
                pltpu.SemaphoreType.DMA((n, 2)),
                pltpu.SemaphoreType.DMA((n, 2)),
            ],
        ),
        out_shape=[jax.ShapeDtypeStruct((cap, width), F32)] * 2
        + [pltpu.VMEM((n, piece, width), BF)] * 2,
        compiler_params=pltpu.CompilerParams(vmem_limit_bytes=24 * MIB),
        cost_estimate=pl.CostEstimate(
            flops=4 * cap * n * piece * width,
            bytes_accessed=8 * n * piece * width,
            transcendentals=0,
        ),
    )(order, *pieces, w_gate, w_up)


def forward_kernel(n, late, n_z, info, *refs):
    pieces, refs = refs[:n], refs[n:]
    wg, wu, gate_in, up_in, cot, share = refs[:6]
    mine, other = refs[6 : 6 + CHUNKS], refs[6 + CHUNKS : 6 + 2 * CHUNKS]
    near_left, route_out, turned = refs[6 + 2 * CHUNKS :]
    step = pl.program_id(0)
    half, block = near_left.shape[1], cot.shape[1]
    per = mine[0].shape[1] // block

    @pl.when(step == 0)
    def _():
        route_out[...] = jnp.zeros_like(route_out)

    here = pl.ds(pl.multiple_of(step * block, block), block)
    gate, up = gate_in[...], up_in[...]
    for i, k in enumerate(late):
        gate += jnp.dot(pieces[k][...], wg[i, :, here], preferred_element_type=F32)
        up += jnp.dot(pieces[k][...], wu[i, :, here], preferred_element_type=F32)
    sig = jax.nn.sigmoid(gate)
    activated = gate * sig
    hidden = (activated * up).astype(BF).astype(F32)
    cot_wide = cot[...].astype(F32)
    route_out[...] += jnp.sum(hidden * cot_wide, axis=1, keepdims=True)
    scaled = share[...] * cot_wide
    gate_cot = scaled * up * sig * (1.0 + gate * (1.0 - sig))
    up_cot = scaled * activated
    first = info[3] == 0
    for j in range(per * CHUNKS):

        @pl.when(step == j)
        def _(j=j):
            cols = slice(j % per * block, (j % per + 1) * block)
            mine[j // per][:, cols] = jnp.where(first, gate_cot, up_cot).astype(BF)
            other[j // per][:, cols] = jnp.where(first, up_cot, gate_cot).astype(BF)
            for k in range(j * n // (per * CHUNKS), (j + 1) * n // (per * CHUNKS)):
                at = lax.rem((info[0] ^ k) - info[1] + n_z, n_z)
                turned[...] = pieces[k][...].T
                start = pl.multiple_of(info[2] * half, half)
                near_left[at] = turned[pl.ds(start, half), :]


def forward(info, pieces, late, w_gate, w_up, gate, up, cot_rows, share, n_z):
    n = len(pieces)
    cap, piece = pieces[0].shape
    width = w_gate.shape[2]
    steps = 4
    block = width // steps
    cols = pl.BlockSpec((cap, block), lambda j, *_: (0, j))
    chunk = (cap, width // CHUNKS)
    near_left = (n_z, piece // 2, cap)
    outs = [(chunk, BF)] * (2 * CHUNKS) + [(near_left, BF), ((cap, 1), F32)]
    held = pl.BlockSpec(memory_space=pltpu.VMEM)
    return pl.pallas_call(
        lambda *a: forward_kernel(n, late, n_z, *a),
        grid_spec=pltpu.PrefetchScalarGridSpec(
            num_scalar_prefetch=1,
            grid=(steps,),
            in_specs=[whole((cap, piece))] * n + [held, held, cols, cols, cols, whole((cap, 1))],
            out_specs=[whole(shape) for shape, _ in outs],
            scratch_shapes=[pltpu.VMEM((piece, cap), BF)],
        ),
        out_shape=[jax.ShapeDtypeStruct(shape, kind) for shape, kind in outs],
        compiler_params=pltpu.CompilerParams(vmem_limit_bytes=24 * MIB),
        cost_estimate=pl.CostEstimate(
            flops=4 * cap * n * piece * width // 2,
            bytes_accessed=16 * cap * width,
            transcendentals=cap * width,
        ),
    )(info, *pieces, w_gate, w_up, gate, up, cot_rows, share)


def back_kernel(info, *refs):
    mine, other = refs[:CHUNKS], refs[CHUNKS : 2 * CHUNKS]
    wg, wu, own, sent, gt, ut, held, sems = refs[2 * CHUNKS :]
    n, _, piece, _ = held.shape
    chunk = mine[0].shape[1]
    place = [(k % 2) * (n // 2) + k // 2 for k in range(n)]
    fetch([info[0] ^ p for p in place], wg, wu, held, sems, n, piece)
    first = info[3] == 0
    for c in range(CHUNKS):
        a, b = mine[c][...], other[c][...]
        gt[pl.ds(c * chunk, chunk), :] = jnp.where(first, a, b).T
        ut[pl.ds(c * chunk, chunk), :] = jnp.where(first, b, a).T
    for k in range(n):
        await_block(wg, wu, held, sems, k, piece)
        out = jnp.dot(held[k, 0], gt[...], preferred_element_type=F32)
        out += jnp.dot(held[k, 1], ut[...], preferred_element_type=F32)
        if k < 2:
            own[k] = out
        else:
            sent[k - 2] = out.astype(BF)


def token_parts(info, mine, other, w_gate, w_up, n):
    cap, chunk = mine[0].shape
    d, width = w_gate.shape
    piece = d // n
    hbm = pl.BlockSpec(memory_space=pl.ANY)
    return pl.pallas_call(
        back_kernel,
        grid_spec=pltpu.PrefetchScalarGridSpec(
            num_scalar_prefetch=1,
            grid=(1,),
            in_specs=[whole((cap, chunk))] * (2 * CHUNKS) + [hbm, hbm],
            out_specs=[whole((2, piece, cap)), whole((n - 2, piece, cap))],
            scratch_shapes=[
                pltpu.VMEM((width, cap), BF),
                pltpu.VMEM((width, cap), BF),
                pltpu.VMEM((n, 2, piece, width), BF),
                pltpu.SemaphoreType.DMA((n, 2)),
            ],
        ),
        out_shape=[
            jax.ShapeDtypeStruct((2, piece, cap), F32),
            jax.ShapeDtypeStruct((n - 2, piece, cap), BF),
        ],
        compiler_params=pltpu.CompilerParams(vmem_limit_bytes=24 * MIB),
        cost_estimate=pl.CostEstimate(
            flops=4 * cap * d * width, bytes_accessed=4 * d * width, transcendentals=0
        ),
    )(info, *mine, *other, w_gate, w_up)


def far_kernel(n, n_z, info, *refs):
    out = refs[-1]
    for y in range(n // 2):
        for x in range(2):
            at = lax.rem((info[0] ^ (y + x * (n // 2))) - info[1] + n_z, n_z)
            out[at] = refs[y][x]


def far_operand(info, arrays, n, n_z):
    rows, cap = arrays[0].shape[1:]
    return pl.pallas_call(
        lambda *a: far_kernel(n, n_z, *a),
        grid_spec=pltpu.PrefetchScalarGridSpec(
            num_scalar_prefetch=1,
            grid=(1,),
            in_specs=[whole(a.shape) for a in arrays],
            out_specs=whole((n_z, rows, cap)),
        ),
        out_shape=jax.ShapeDtypeStruct((n_z, rows, cap), BF),
        compiler_params=pltpu.CompilerParams(vmem_limit_bytes=8 * MIB),
        cost_estimate=pl.CostEstimate(
            flops=0, bytes_accessed=4 * n * rows * cap, transcendentals=0
        ),
    )(info, *arrays)


def on_device(tokens, hidden_cot, w_gate, w_up, expert_ids, route_fixed):
    tok_dev, piece = tokens.shape
    width = w_gate.shape[1]
    n_tensor = lax.axis_size("tensor")
    n_dp = lax.axis_size("dp")
    n_z = n_dp // 4
    half = piece // 2
    xlo = n_tensor // 2
    t = lax.axis_index("tensor")
    dp = lax.axis_index("dp")
    z, xh, core = dp // 4, (dp // 2) % 2, dp % 2
    info = jnp.stack([t, z, xh, core]).astype(jnp.int32)
    tie = lax.optimization_barrier

    def over_tensor(x, k):
        return lax.ppermute(x, "tensor", [(i, i ^ k) for i in range(n_tensor)])

    def over_dp(x, k):
        return lax.ppermute(x, "dp", [(i, i ^ k) for i in range(n_dp)])

    def along_z(x, k):
        return lax.ppermute(x, "dp", [(i, (i + 4 * k) % n_dp) for i in range(n_dp)])

    selected = expert_ids == 0
    flag = jnp.any(selected, axis=1)
    place = jnp.arange(tok_dev, dtype=jnp.int32)
    upto = (place[:, None] <= place[None, :]).astype(BF)
    slot_of = jnp.dot(flag.astype(BF)[None, :], upto, preferred_element_type=F32)[0] - 1.0
    slot_of = jnp.where(flag, slot_of.astype(jnp.int32), -1)
    mask = slot_of[None, :] == jnp.arange(CAP, dtype=jnp.int32)[:, None]
    dispatch = mask.astype(BF)
    share_all = jnp.sum(jnp.where(selected, route_fixed, 0), axis=1).astype(F32) / 65536.0

    w_gate = pltpu.with_memory_space_constraint(w_gate, pltpu.HBM)
    w_up = pltpu.with_memory_space_constraint(w_up, pltpu.HBM)
    picked, far_piece = dispatch_tokens(info, slot_of[None, :], tokens)
    near = [None] * n_tensor
    near[xlo] = over_tensor(picked, xlo)
    near[1] = over_tensor(picked, 1)
    near[3] = over_tensor(picked, 3)
    far_piece = over_dp(far_piece, 2)
    picked, near[1], near[3], near[xlo] = tie((picked, near[1], near[3], near[xlo]))
    near[0] = picked
    near[xlo + 1] = over_tensor(near[1], xlo)
    near[xlo + 3] = over_tensor(near[3], xlo)
    near[2] = over_tensor(picked, 2)
    near[xlo + 2] = over_tensor(near[xlo], 2)
    far_pair = jnp.stack([far_piece, over_tensor(far_piece, xlo)])
    cot_rows, share = dispatch_cots(slot_of[None, :], share_all[None, :], hidden_cot)
    soon, late = (0, xlo, 1, 3), (xlo + 1, xlo + 3, 2, xlo + 2)
    order = lambda ks: jnp.stack([t ^ k for k in ks]).astype(jnp.int32)
    gate, up, late_gate, late_up = early(
        order(soon + late), [near[k] for k in soon], w_gate, w_up
    )
    near, far_pair, cot_rows, share, gate, up = tie(
        (near, far_pair, cot_rows, share, gate, up)
    )
    outs = forward(info, near, late, late_gate, late_up, gate, up, cot_rows, share, n_z)
    mine, other = outs[:CHUNKS], outs[CHUNKS : 2 * CHUNKS]
    near_left, route_part = outs[2 * CHUNKS :]

    def to_partners(c):
        return [mine[c], over_dp(other[c], 1), over_dp(mine[c], 2), over_dp(other[c], 3)]

    cots = [to_partners(0)]
    far_pair, near_left, mine, other, route_part, cots[0][1] = tie(
        (far_pair, near_left, mine, other, route_part, cots[0][1])
    )
    near_sib = over_dp(near_left, 1)
    far = [far_pair] + [over_tensor(far_pair, k) for k in (1, 2, 3)]
    own_part, sent = token_parts(info, mine, other, w_gate, w_up, n_tensor)
    far, own_part, sent = tie((far, own_part, sent))
    far_left = far_operand(info, far, n_tensor, n_z)
    far_sib = over_dp(far_left, 1)
    for c in range(1, CHUNKS):
        mine, other, cots[-1] = tie((mine, other, cots[-1]))
        cots.append(to_partners(c))
    sums = {k: over_tensor(sent[2 * k - 2 : 2 * k], k) for k in (1, 3)}

    def product(a, b):
        return jnp.dot(a.reshape(n_z * half, CAP), b, preferred_element_type=F32)

    class Ring:
        def __init__(self, c):
            base = product(near_left, cots[c][0]) + product(near_sib, cots[c][1])
            base = tie(base) + product(far_left, cots[c][2])
            base = tie(base + product(far_sib, cots[c][3]))
            self.base = base.reshape(n_z, half, width // CHUNKS)
            self.up_hops = n_z // 2 - c % 2
            self.down_hops = n_z - 1 - self.up_hops
            self.rising = self.falling = None

        def part(self, j):
            return self.base[j]

        def hop(self, i):
            up, down = i < self.up_hops, i < self.down_hops
            if up:
                out = self.part(self.up_hops - i)
                rising = (out if i == 0 else out + self.rising.astype(F32)).astype(BF)
            if down:
                out = self.part((n_z - self.down_hops + i) % n_z)
                falling = (out if i == 0 else out + self.falling.astype(F32)).astype(BF)
            if up and down:
                rising, falling = tie((rising, falling))
            if up:
                self.rising = along_z(rising, 1)
            if down:
                self.falling = along_z(falling, -1)

        def finish(self):
            total = self.part(0) + self.rising.astype(F32) + self.falling.astype(F32)
            total = total.astype(BF).reshape(2, half // 2, width // CHUNKS)
            kept = lax.dynamic_index_in_dim(total, core, 0, keepdims=False)
            swapped = over_dp(lax.dynamic_index_in_dim(total, 1 - core, 0, keepdims=False), 1)
            return jnp.where(core == 0, kept, swapped), jnp.where(core == 0, swapped, kept)

    rings = [Ring(c) for c in range(CHUNKS)]
    for i in range(n_z // 2):
        for ring in rings:
            ring.hop(i)
        if i == 0:
            message, rings[0].rising = tie((sent[2:4], rings[0].rising))
            sums[2] = over_tensor(message, 2)
        else:
            route_part, rings[0].rising = tie((route_part, rings[0].rising))
            if i == 1:
                route_part = route_part[:, 0]
            route_part = route_part + over_tensor(route_part, 1 << (i - 1))
    gate_grads, up_grads = zip(*[ring.finish() for ring in rings])
    gate_grad = jnp.concatenate(gate_grads, axis=1)
    up_grad = jnp.concatenate(up_grads, axis=1)

    total = own_part
    for k in (1, 2, 3):
        total = total + sums[k].astype(F32)
    total = total[0] + over_tensor(total[1].astype(BF), xlo).astype(F32)
    token_grad = lax.dot_general(
        dispatch, total.astype(BF), (((0,), (1,)), ((), ())), preferred_element_type=F32
    ).astype(BF)
    route_grad = jnp.sum(jnp.where(mask, route_part[:, None], 0.0), axis=0)
    return token_grad, gate_grad, up_grad, route_grad


def solution(mesh):
    return jax.shard_map(
        on_device,
        mesh=mesh,
        in_specs=(
            P("dp", "tensor"),
            P("dp", "tensor"),
            P(None, "tensor"),
            P(None, "tensor"),
            P("dp", None),
            P("dp", None),
        ),
        out_specs=(P("dp", "tensor"), P("dp", "tensor"), P("dp", "tensor"), P("dp")),
        check_vma=False,
    )
```

```python
import jax
import jax.numpy as jnp
from jax import lax
from jax.experimental import pallas as pl
from jax.experimental.pallas import tpu as pltpu
from jax.sharding import PartitionSpec as P

CAP = 256
CHUNKS = 2
BF = jnp.bfloat16
F32 = jnp.float32
MIB = 2**20


def whole(shape):
    return pl.BlockSpec(shape, lambda *_: (0,) * len(shape))


def dispatch_kernel(info, slots, tokens, picked, far, turned):
    cap, rows = picked.shape[0], far.shape[0]
    tok_dev = slots.shape[1]
    ids = lax.broadcasted_iota(jnp.int32, (cap, tok_dev), 0)
    mask = (slots[...] == ids).astype(F32).astype(BF)
    got = jnp.dot(mask, tokens[...], preferred_element_type=F32)
    picked[...] = got.astype(BF)
    turned[...] = got.T.astype(BF)
    start = pl.multiple_of((1 - info[2]) * rows, rows)
    far[...] = turned[pl.ds(start, rows), :]


def dispatch_tokens(info, slots, tokens):
    tok_dev, piece = tokens.shape
    return pl.pallas_call(
        dispatch_kernel,
        grid_spec=pltpu.PrefetchScalarGridSpec(
            num_scalar_prefetch=1,
            grid=(1,),
            in_specs=[whole((1, tok_dev)), whole((tok_dev, piece))],
            out_specs=[whole((CAP, piece)), whole((piece // 2, CAP))],
            scratch_shapes=[pltpu.VMEM((piece, CAP), BF)],
        ),
        out_shape=[
            jax.ShapeDtypeStruct((CAP, piece), BF),
            jax.ShapeDtypeStruct((piece // 2, CAP), BF),
        ],
        compiler_params=pltpu.CompilerParams(vmem_limit_bytes=8 * MIB),
        cost_estimate=pl.CostEstimate(
            flops=2 * CAP * tok_dev * piece, bytes_accessed=4 * tok_dev * piece, transcendentals=0
        ),
    )(info, slots, tokens)


def cot_kernel(slots, share_all, cot, rows, share):
    cap, tok_dev = rows.shape[0], slots.shape[1]
    mask = slots[...] == lax.broadcasted_iota(jnp.int32, (cap, tok_dev), 0)
    hot = mask.astype(F32).astype(BF)
    rows[...] = jnp.dot(hot, cot[...], preferred_element_type=F32).astype(BF)
    share[...] = jnp.sum(jnp.where(mask, share_all[...], 0.0), axis=1, keepdims=True)


def dispatch_cots(slots, share_all, hidden_cot):
    tok_dev, width = hidden_cot.shape
    return pl.pallas_call(
        cot_kernel,
        out_shape=[
            jax.ShapeDtypeStruct((CAP, width), BF),
            jax.ShapeDtypeStruct((CAP, 1), F32),
        ],
        compiler_params=pltpu.CompilerParams(vmem_limit_bytes=8 * MIB),
        cost_estimate=pl.CostEstimate(
            flops=2 * CAP * tok_dev * width, bytes_accessed=4 * tok_dev * width, transcendentals=0
        ),
    )(slots, share_all, hidden_cot)


def early_kernel(n, order, *refs):
    pieces = refs[:n]
    wg, wu, gate, up, near, all_g, all_u, held, turned, sems = refs[n:]
    cap, piece = pieces[0].shape
    half = near.shape[1]

    def copies(i):
        start = pl.multiple_of(order[i] * piece, piece)
        return [
            pltpu.make_async_copy(
                w.at[pl.ds(start, piece)], ref.at[pl.ds(i * piece, piece)], sems.at[i, j]
            )
            for j, (w, ref) in enumerate(((wg, all_g), (wu, all_u)))
        ]

    every = [copies(i) for i in range(2 * n)]
    for pair in every:
        for copy in pair:
            copy.start()
    for k in range(n):
        held[:, k * piece : (k + 1) * piece] = pieces[k][...]

    def turn(k, _):
        turned[...] = held[:, pl.ds(pl.multiple_of(k * piece, piece), piece)].T
        start = pl.multiple_of(order[2 * n] * half, half)
        near[k] = turned[pl.ds(start, half), :]
        return 0

    lax.fori_loop(0, n, turn, 0)
    for pair in every[:n]:
        for copy in pair:
            copy.wait()
    block = gate.shape[1] // CHUNKS

    def multiply(c, _):
        here = pl.ds(pl.multiple_of(c * block, block), block)
        gate[:, here] = jnp.dot(held[...], all_g[: n * piece, here], preferred_element_type=F32)
        up[:, here] = jnp.dot(held[...], all_u[: n * piece, here], preferred_element_type=F32)
        return 0

    lax.fori_loop(0, CHUNKS, multiply, 0)
    for pair in every[n:]:
        for copy in pair:
            copy.wait()


def early(order, pieces, w_gate, w_up):
    n = len(pieces)
    cap, piece = pieces[0].shape
    width = w_gate.shape[1]
    hbm = pl.BlockSpec(memory_space=pl.ANY)
    return pl.pallas_call(
        lambda *a: early_kernel(n, *a),
        grid_spec=pltpu.PrefetchScalarGridSpec(
            num_scalar_prefetch=1,
            grid=(1,),
            in_specs=[whole((cap, piece))] * n + [hbm, hbm],
            out_specs=[whole((cap, width))] * 2
            + [whole((n, piece // 2, cap))]
            + [pl.BlockSpec(memory_space=pltpu.VMEM)] * 2,
            scratch_shapes=[
                pltpu.VMEM((cap, n * piece), BF),
                pltpu.VMEM((piece, cap), BF),
                pltpu.SemaphoreType.DMA((2 * n, 2)),
            ],
        ),
        out_shape=[jax.ShapeDtypeStruct((cap, width), F32)] * 2
        + [jax.ShapeDtypeStruct((n, piece // 2, cap), BF)]
        + [pltpu.VMEM((2 * n * piece, width), BF)] * 2,
        compiler_params=pltpu.CompilerParams(vmem_limit_bytes=28 * MIB),
        cost_estimate=pl.CostEstimate(
            flops=4 * cap * n * piece * width,
            bytes_accessed=8 * n * piece * width,
            transcendentals=0,
        ),
    )(order, *pieces, w_gate, w_up)


def forward_kernel(n, soon, late, n_z, info, *refs):
    pieces = refs[:n]
    wg, wu, gate_in, up_in, near_in, cot, share = refs[n : n + 7]
    mine, other = refs[n + 7 : n + 7 + CHUNKS], refs[n + 7 + CHUNKS : n + 7 + 2 * CHUNKS]
    near_left, route_out, held, turned = refs[n + 7 + 2 * CHUNKS :]
    step = pl.program_id(0)
    piece, cap = turned.shape
    half, block = near_left.shape[1], cot.shape[1]
    at = lambda k: lax.rem((info[0] ^ k) - info[1] + n_z, n_z)

    @pl.when(step == 0)
    def _():
        route_out[...] = jnp.zeros_like(route_out)
        for i in range(n):
            held[:, i * piece : (i + 1) * piece] = pieces[i][...]

    here = pl.ds(pl.multiple_of(step * block, block), block)
    gate = gate_in[...] + jnp.dot(held[...], wg[n * piece :, here], preferred_element_type=F32)
    up = up_in[...] + jnp.dot(held[...], wu[n * piece :, here], preferred_element_type=F32)
    sig = jax.nn.sigmoid(gate)
    activated = gate * sig
    hidden = (activated * up).astype(BF).astype(F32)
    cot_wide = cot[...].astype(F32)
    route_out[...] += jnp.sum(hidden * cot_wide, axis=1, keepdims=True)
    scaled = share[...] * cot_wide
    gate_cot = scaled * up * sig * (1.0 + gate * (1.0 - sig))
    up_cot = scaled * activated
    first = info[3] == 0
    own = jnp.where(first, gate_cot, up_cot).astype(BF)
    rest = jnp.where(first, up_cot, gate_cot).astype(BF)
    for c in range(CHUNKS):

        @pl.when(step == c)
        def _(c=c):
            mine[c][...] = own
            other[c][...] = rest

    @pl.when(step == CHUNKS - 1)
    def _():
        for i, k in enumerate(soon):
            near_left[at(k)] = near_in[i]
        for i, k in enumerate(late):
            turned[...] = held[:, i * piece : (i + 1) * piece].T
            start = pl.multiple_of(info[2] * half, half)
            near_left[at(k)] = turned[pl.ds(start, half), :]


def forward(info, pieces, soon, late, w_gate, w_up, gate, up, near, cot_rows, share, n_z):
    n = len(pieces)
    cap, piece = pieces[0].shape
    width = w_gate.shape[1]
    block = width // CHUNKS
    cols = pl.BlockSpec((cap, block), lambda j, *_: (0, j))
    near_left = (n_z, piece // 2, cap)
    outs = [((cap, block), BF)] * (2 * CHUNKS) + [(near_left, BF), ((cap, 1), F32)]
    held = pl.BlockSpec(memory_space=pltpu.VMEM)
    return pl.pallas_call(
        lambda *a: forward_kernel(n, soon, late, n_z, *a),
        grid_spec=pltpu.PrefetchScalarGridSpec(
            num_scalar_prefetch=1,
            grid=(CHUNKS,),
            in_specs=[whole((cap, piece))] * n
            + [held, held, cols, cols, whole(near.shape), cols, whole((cap, 1))],
            out_specs=[whole(shape) for shape, _ in outs],
            scratch_shapes=[pltpu.VMEM((cap, n * piece), BF), pltpu.VMEM((piece, cap), BF)],
        ),
        out_shape=[jax.ShapeDtypeStruct(shape, kind) for shape, kind in outs],
        compiler_params=pltpu.CompilerParams(vmem_limit_bytes=24 * MIB),
        cost_estimate=pl.CostEstimate(
            flops=4 * cap * n * piece * width,
            bytes_accessed=16 * cap * width,
            transcendentals=cap * width,
        ),
    )(info, *pieces, w_gate, w_up, gate, up, near, cot_rows, share)


def back_kernel(info, *refs):
    mine, other = refs[:CHUNKS], refs[CHUNKS : 2 * CHUNKS]
    wg, wu, own, first_out, third_out, second_out, gt, ut = refs[2 * CHUNKS :]
    piece = own.shape[1]
    chunk = mine[0].shape[1]
    first = info[3] == 0
    for c in range(CHUNKS):
        a, b = mine[c][...], other[c][...]
        gt[pl.ds(c * chunk, chunk), :] = jnp.where(first, a, b).T
        ut[pl.ds(c * chunk, chunk), :] = jnp.where(first, b, a).T

    targets = [(own, 0), (own, 1), (first_out, 0), (third_out, 0)]
    targets += [(first_out, 1), (third_out, 1), (second_out, 0), (second_out, 1)]

    def block(i, _):
        rows = pl.ds(pl.multiple_of(i * piece, piece), piece)
        out = jnp.dot(wg[rows, :], gt[...], preferred_element_type=F32)
        out += jnp.dot(wu[rows, :], ut[...], preferred_element_type=F32)
        for j, (ref, at) in enumerate(targets):

            @pl.when(i == j)
            def _(ref=ref, at=at):
                ref[at] = out.astype(ref.dtype)

        return 0

    lax.fori_loop(0, len(targets), block, 0)


def token_parts(info, mine, other, weights, piece):
    cap, chunk = mine[0].shape
    depth, width = weights[0].shape
    pair = (2, piece, cap)
    return pl.pallas_call(
        back_kernel,
        grid_spec=pltpu.PrefetchScalarGridSpec(
            num_scalar_prefetch=1,
            grid=(1,),
            in_specs=[whole((cap, chunk))] * (2 * CHUNKS)
            + [pl.BlockSpec(memory_space=pltpu.VMEM)] * 2,
            out_specs=[whole(pair)] * 4,
            scratch_shapes=[pltpu.VMEM((width, cap), BF), pltpu.VMEM((width, cap), BF)],
        ),
        out_shape=[jax.ShapeDtypeStruct(pair, F32)] + [jax.ShapeDtypeStruct(pair, BF)] * 3,
        compiler_params=pltpu.CompilerParams(vmem_limit_bytes=16 * MIB),
        cost_estimate=pl.CostEstimate(
            flops=4 * cap * depth * width, bytes_accessed=4 * depth * width, transcendentals=0
        ),
    )(info, *mine, *other, *weights)


def after(x, waited):
    def kernel(value, _, out):
        out[...] = value[...]

    return pl.pallas_call(
        kernel,
        grid=(1,),
        in_specs=[whole(x.shape), pl.BlockSpec(memory_space=pl.ANY)],
        out_specs=whole(x.shape),
        out_shape=jax.ShapeDtypeStruct(x.shape, x.dtype),
        compiler_params=pltpu.CompilerParams(vmem_limit_bytes=4 * MIB),
    )(x, waited)


def far_kernel(n, n_z, info, *refs):
    out = refs[-1]
    for y in range(n // 2):
        for x in range(2):
            at = lax.rem((info[0] ^ (y + x * (n // 2))) - info[1] + n_z, n_z)
            out[at] = refs[y][x]


def far_operand(info, arrays, n, n_z):
    rows, cap = arrays[0].shape[1:]
    return pl.pallas_call(
        lambda *a: far_kernel(n, n_z, *a),
        grid_spec=pltpu.PrefetchScalarGridSpec(
            num_scalar_prefetch=1,
            grid=(1,),
            in_specs=[whole(a.shape) for a in arrays],
            out_specs=whole((n_z, rows, cap)),
        ),
        out_shape=jax.ShapeDtypeStruct((n_z, rows, cap), BF),
        compiler_params=pltpu.CompilerParams(vmem_limit_bytes=8 * MIB),
        cost_estimate=pl.CostEstimate(
            flops=0, bytes_accessed=4 * n * rows * cap, transcendentals=0
        ),
    )(info, *arrays)


def on_device(tokens, hidden_cot, w_gate, w_up, expert_ids, route_fixed):
    tok_dev, piece = tokens.shape
    width = w_gate.shape[1]
    n_tensor = lax.axis_size("tensor")
    n_dp = lax.axis_size("dp")
    n_z = n_dp // 4
    half = piece // 2
    xlo = n_tensor // 2
    t = lax.axis_index("tensor")
    dp = lax.axis_index("dp")
    z, xh, core = dp // 4, (dp // 2) % 2, dp % 2
    info = jnp.stack([t, z, xh, core]).astype(jnp.int32)
    tie = lax.optimization_barrier

    def over_tensor(x, k):
        return lax.ppermute(x, "tensor", [(i, i ^ k) for i in range(n_tensor)])

    def over_dp(x, k):
        return lax.ppermute(x, "dp", [(i, i ^ k) for i in range(n_dp)])

    def along_z(x, k):
        return lax.ppermute(x, "dp", [(i, (i + 4 * k) % n_dp) for i in range(n_dp)])

    selected = expert_ids == 0
    flag = jnp.any(selected, axis=1)
    place = jnp.arange(tok_dev, dtype=jnp.int32)
    upto = (place[:, None] <= place[None, :]).astype(BF)
    slot_of = jnp.dot(flag.astype(BF)[None, :], upto, preferred_element_type=F32)[0] - 1.0
    slot_of = jnp.where(flag, slot_of.astype(jnp.int32), -1)
    mask = slot_of[None, :] == jnp.arange(CAP, dtype=jnp.int32)[:, None]
    dispatch = mask.astype(BF)
    share_all = jnp.sum(jnp.where(selected, route_fixed, 0), axis=1).astype(F32) / 65536.0

    hidden_cot = pltpu.with_memory_space_constraint(hidden_cot, pltpu.HBM)
    tokens = pltpu.with_memory_space_constraint(tokens, pltpu.HBM)
    w_gate = pltpu.with_memory_space_constraint(w_gate, pltpu.HBM)
    w_up = pltpu.with_memory_space_constraint(w_up, pltpu.HBM)
    picked, far_piece = dispatch_tokens(info, slot_of[None, :], tokens)
    cot_rows, share = dispatch_cots(slot_of[None, :], share_all[None, :], hidden_cot)
    near = [None] * n_tensor
    near[xlo] = over_tensor(picked, xlo)
    near[1] = over_tensor(picked, 1)
    near[3] = over_tensor(picked, 3)
    far_piece = over_dp(far_piece, 2)
    picked, near[1], near[3], near[xlo], cot_rows, share = tie(
        (picked, near[1], near[3], near[xlo], cot_rows, share)
    )
    near[0] = picked
    near[xlo + 1] = over_tensor(near[1], xlo)
    near[xlo + 3] = over_tensor(near[3], xlo)
    near[2] = over_tensor(picked, 2)
    near[xlo + 2] = over_tensor(near[xlo], 2)
    soon, late = (0, xlo, 1, 3), (xlo + 1, xlo + 3, 2, xlo + 2)
    order = jnp.stack([t ^ k for k in soon + late] + [xh]).astype(jnp.int32)
    gate, up, near_soon, *weights = early(order, [near[k] for k in soon], w_gate, w_up)
    far_piece, near[late[0]] = tie((far_piece, near[late[0]]))
    far_pair = jnp.stack([far_piece, over_tensor(far_piece, xlo)])
    late_near, far_pair, gate, up = tie(([near[k] for k in late], far_pair, gate, up))
    outs = forward(
        info, late_near, soon, late, *weights, gate, up, near_soon, cot_rows, share, n_z
    )
    mine, other = outs[:CHUNKS], outs[CHUNKS : 2 * CHUNKS]
    near_left, route_part = outs[2 * CHUNKS :]

    def to_partners(c):
        return [mine[c], over_dp(other[c], 1), over_dp(mine[c], 2), over_dp(other[c], 3)]

    cots = [to_partners(0)]
    far_pair, near_left, mine, other, route_part, cots[0][1] = tie(
        (far_pair, near_left, mine, other, route_part, cots[0][1])
    )
    near_sib = over_dp(near_left, 1)
    far = [far_pair] + [over_tensor(far_pair, k) for k in (1, 3)]
    far_pair, near_sib = tie((far_pair, near_sib))
    far.insert(2, over_tensor(far_pair, 2))
    own_part, *sent = token_parts(info, mine, other, weights, piece)
    far, own_part, sent, mine, other = tie((far, own_part, sent, mine, other))
    far_left = far_operand(info, far, n_tensor, n_z)
    far_sib = over_dp(far_left, 1)
    for c in range(1, CHUNKS):
        mine, other, cots[-1] = tie((mine, other, cots[-1]))
        cots.append(to_partners(c))
    sums = {1: over_tensor(sent[0], 1)}

    def product(a, b):
        return jnp.dot(a.reshape(n_z * half, CAP), b, preferred_element_type=F32)

    class Ring:
        def __init__(self, c):
            base = product(lefts[0], cots[c][0]) + product(lefts[1], cots[c][1])
            base = tie(base) + product(far_left, cots[c][2])
            base = tie(base + product(far_sib, cots[c][3]))
            self.base = base.reshape(n_z, half, width // CHUNKS)
            self.up_hops = n_z // 2 - c % 2
            self.down_hops = n_z - 1 - self.up_hops
            self.rising = self.falling = None

        def part(self, j):
            return self.base[j]

        def hop(self, i):
            up, down = i < self.up_hops, i < self.down_hops
            if up:
                out = self.part(self.up_hops - i)
                rising = (out if i == 0 else out + self.rising.astype(F32)).astype(BF)
            if down:
                out = self.part((n_z - self.down_hops + i) % n_z)
                falling = (out if i == 0 else out + self.falling.astype(F32)).astype(BF)
            if up and down:
                rising, falling = tie((rising, falling))
            if up:
                self.rising = along_z(rising, 1)
            if down:
                self.falling = along_z(falling, -1)

        def finish(self):
            total = self.part(0) + self.rising.astype(F32) + self.falling.astype(F32)
            total = total.astype(BF).reshape(2, half // 2, width // CHUNKS)
            return total

    lefts = [near_left, near_sib]
    rings = []
    for c in range(CHUNKS):
        rings.append(Ring(c))
        lefts, rings[c].base = tie((lefts, rings[c].base))
    route_part = route_part.reshape(1, CAP)
    for i in range(n_z // 2):
        for ring in rings:
            ring.hop(i)
        waited = rings[0].rising
        if i < 2:
            sums[3 - i] = over_tensor(after(sent[1 + i], waited), 3 - i)
        if i < 3:
            route_part = after(route_part, waited)
            route_part = route_part + over_tensor(route_part, 1 << i)
    whole_rows = jnp.concatenate([ring.finish() for ring in rings], axis=2)
    kept = lax.dynamic_index_in_dim(whole_rows, core, 0, keepdims=False)
    swapped = over_dp(lax.dynamic_index_in_dim(whole_rows, 1 - core, 0, keepdims=False), 1)
    gate_grad = jnp.where(core == 0, kept, swapped)
    up_grad = jnp.where(core == 0, swapped, kept)

    total = own_part
    for k in (1, 2, 3):
        total = total + sums[k].astype(F32)
    total = total[0] + over_tensor(total[1].astype(BF), xlo).astype(F32)
    token_grad = lax.dot_general(
        dispatch, total.astype(BF), (((0,), (1,)), ((), ())), preferred_element_type=F32
    ).astype(BF)
    route_grad = jnp.sum(jnp.where(mask, route_part[0][:, None], 0.0), axis=0)
    return token_grad, gate_grad, up_grad, route_grad


def solution(mesh):
    return jax.shard_map(
        on_device,
        mesh=mesh,
        in_specs=(
            P("dp", "tensor"),
            P("dp", "tensor"),
            P(None, "tensor"),
            P(None, "tensor"),
            P("dp", None),
            P("dp", None),
        ),
        out_specs=(P("dp", "tensor"), P("dp", "tensor"), P("dp", "tensor"), P("dp")),
        check_vma=False,
    )
```

```python
import jax
import jax.numpy as jnp
from jax import lax
from jax.experimental import pallas as pl
from jax.experimental.pallas import tpu as pltpu
from jax.sharding import PartitionSpec as P

CAP = 256
CHUNKS = 2
EXTRA = 16
BF = jnp.bfloat16
F32 = jnp.float32
MIB = 2**20


def whole(shape):
    return pl.BlockSpec(shape, lambda *_: (0,) * len(shape))


def dispatch_kernel(info, slots, tokens, picked, far, turned):
    cap, rows = picked.shape[0], far.shape[0]
    tok_dev = slots.shape[1]
    ids = lax.broadcasted_iota(jnp.int32, (cap, tok_dev), 0)
    mask = (slots[...] == ids).astype(F32).astype(BF)
    got = jnp.dot(mask, tokens[...], preferred_element_type=F32)
    picked[...] = got.astype(BF)
    turned[...] = got.T.astype(BF)
    start = pl.multiple_of((1 - info[2]) * rows, rows)
    far[...] = turned[pl.ds(start, rows), :]


def dispatch_tokens(info, slots, tokens):
    tok_dev, piece = tokens.shape
    return pl.pallas_call(
        dispatch_kernel,
        grid_spec=pltpu.PrefetchScalarGridSpec(
            num_scalar_prefetch=1,
            grid=(1,),
            in_specs=[whole((1, tok_dev)), whole((tok_dev, piece))],
            out_specs=[whole((CAP, piece)), whole((piece // 2, CAP))],
            scratch_shapes=[pltpu.VMEM((piece, CAP), BF)],
        ),
        out_shape=[
            jax.ShapeDtypeStruct((CAP, piece), BF),
            jax.ShapeDtypeStruct((piece // 2, CAP), BF),
        ],
        compiler_params=pltpu.CompilerParams(vmem_limit_bytes=8 * MIB),
        cost_estimate=pl.CostEstimate(
            flops=2 * CAP * tok_dev * piece, bytes_accessed=4 * tok_dev * piece, transcendentals=0
        ),
    )(info, slots, tokens)


def cot_kernel(slots, share_all, cot, rows, share):
    cap, tok_dev = rows.shape[0], slots.shape[1]
    mask = slots[...] == lax.broadcasted_iota(jnp.int32, (cap, tok_dev), 0)
    hot = mask.astype(F32).astype(BF)
    rows[...] = jnp.dot(hot, cot[...], preferred_element_type=F32).astype(BF)
    share[...] = jnp.sum(jnp.where(mask, share_all[...], 0.0), axis=1, keepdims=True)


def dispatch_cots(slots, share_all, hidden_cot):
    tok_dev, width = hidden_cot.shape
    return pl.pallas_call(
        cot_kernel,
        out_shape=[
            jax.ShapeDtypeStruct((CAP, width), BF),
            jax.ShapeDtypeStruct((CAP, 1), F32),
        ],
        compiler_params=pltpu.CompilerParams(vmem_limit_bytes=8 * MIB),
        cost_estimate=pl.CostEstimate(
            flops=2 * CAP * tok_dev * width, bytes_accessed=4 * tok_dev * width, transcendentals=0
        ),
    )(slots, share_all, hidden_cot)


def early_kernel(n, order, *refs):
    pieces = refs[:n]
    wg, wu, gate, up, near, all_g, all_u, held, turned, sems = refs[n:]
    cap, piece = pieces[0].shape
    half = near.shape[1]

    def copies(i):
        start = pl.multiple_of(order[i] * piece, piece)
        return [
            pltpu.make_async_copy(
                w.at[pl.ds(start, piece)], ref.at[pl.ds(i * piece, piece)], sems.at[i, j]
            )
            for j, (w, ref) in enumerate(((wg, all_g), (wu, all_u)))
        ]

    every = [copies(i) for i in range(2 * n)]
    for pair in every:
        for copy in pair:
            copy.start()
    for k in range(n):
        held[:, k * piece : (k + 1) * piece] = pieces[k][...]

    def turn(k, _):
        turned[...] = held[:, pl.ds(pl.multiple_of(k * piece, piece), piece)].T
        start = pl.multiple_of(order[2 * n] * half, half)
        near[k] = turned[pl.ds(start, half), :]
        return 0

    lax.fori_loop(0, n, turn, 0)
    for pair in every[:n]:
        for copy in pair:
            copy.wait()
    block = gate.shape[1] // CHUNKS

    def multiply(c, _):
        here = pl.ds(pl.multiple_of(c * block, block), block)
        gate[:, here] = jnp.dot(held[...], all_g[: n * piece, here], preferred_element_type=F32)
        up[:, here] = jnp.dot(held[...], all_u[: n * piece, here], preferred_element_type=F32)
        return 0

    lax.fori_loop(0, CHUNKS, multiply, 0)
    for pair in every[n:]:
        for copy in pair:
            copy.wait()


def early(order, pieces, w_gate, w_up):
    n = len(pieces)
    cap, piece = pieces[0].shape
    width = w_gate.shape[1]
    hbm = pl.BlockSpec(memory_space=pl.ANY)
    return pl.pallas_call(
        lambda *a: early_kernel(n, *a),
        grid_spec=pltpu.PrefetchScalarGridSpec(
            num_scalar_prefetch=1,
            grid=(1,),
            in_specs=[whole((cap, piece))] * n + [hbm, hbm],
            out_specs=[whole((cap, width))] * 2
            + [whole((n, piece // 2, cap))]
            + [pl.BlockSpec(memory_space=pltpu.VMEM)] * 2,
            scratch_shapes=[
                pltpu.VMEM((cap, n * piece), BF),
                pltpu.VMEM((piece, cap), BF),
                pltpu.SemaphoreType.DMA((2 * n, 2)),
            ],
        ),
        out_shape=[jax.ShapeDtypeStruct((cap, width), F32)] * 2
        + [jax.ShapeDtypeStruct((n, piece // 2, cap), BF)]
        + [pltpu.VMEM((2 * n * piece, width), BF)] * 2,
        compiler_params=pltpu.CompilerParams(vmem_limit_bytes=14 * MIB),
        cost_estimate=pl.CostEstimate(
            flops=4 * cap * n * piece * width,
            bytes_accessed=8 * n * piece * width,
            transcendentals=0,
        ),
    )(order, *pieces, w_gate, w_up)


def forward_kernel(n, soon, late, n_z, info, *refs):
    pieces = refs[:n]
    wg, wu, gate_in, up_in, near_in, cot, share = refs[n : n + 7]
    mine, other = refs[n + 7 : n + 7 + CHUNKS], refs[n + 7 + CHUNKS : n + 7 + 2 * CHUNKS]
    near_left, route_out, held, turned, route = refs[n + 7 + 2 * CHUNKS :]
    step = pl.program_id(0)
    piece, cap = turned.shape
    half, block = near_left.shape[1], cot.shape[1]
    at = lambda k: lax.rem((info[0] ^ k) - info[1] + n_z, n_z)

    @pl.when(step == 0)
    def _():
        route[...] = jnp.zeros_like(route)
        for i in range(n):
            held[:, i * piece : (i + 1) * piece] = pieces[i][...]

    here = pl.ds(pl.multiple_of(step * block, block), block)
    gate = gate_in[...] + jnp.dot(held[...], wg[n * piece :, here], preferred_element_type=F32)
    up = up_in[...] + jnp.dot(held[...], wu[n * piece :, here], preferred_element_type=F32)
    sig = jax.nn.sigmoid(gate)
    activated = gate * sig
    hidden = (activated * up).astype(BF).astype(F32)
    cot_wide = cot[...].astype(F32)
    route[...] += jnp.sum(hidden * cot_wide, axis=1, keepdims=True)
    scaled = share[...] * cot_wide
    gate_cot = scaled * up * sig * (1.0 + gate * (1.0 - sig))
    up_cot = scaled * activated
    first = info[3] == 0
    own = jnp.where(first, gate_cot, up_cot).astype(BF)
    rest = jnp.where(first, up_cot, gate_cot).astype(BF)
    for c in range(CHUNKS):

        @pl.when(step == c)
        def _(c=c):
            mine[c][...] = own
            other[c][...] = rest

    @pl.when(step == CHUNKS - 1)
    def _():
        route_out[...] = jnp.broadcast_to(route[...], (cap, 128)).T[:1, :]
        for i, k in enumerate(soon):
            near_left[at(k)] = near_in[i]
        for i, k in enumerate(late):
            turned[...] = held[:, i * piece : (i + 1) * piece].T
            start = pl.multiple_of(info[2] * half, half)
            near_left[at(k)] = turned[pl.ds(start, half), :]


def forward(info, pieces, soon, late, w_gate, w_up, gate, up, near, cot_rows, share, n_z):
    n = len(pieces)
    cap, piece = pieces[0].shape
    width = w_gate.shape[1]
    block = width // CHUNKS
    cols = pl.BlockSpec((cap, block), lambda j, *_: (0, j))
    near_left = (n_z, piece // 2, cap)
    outs = [((cap, block), BF)] * (2 * CHUNKS) + [(near_left, BF), ((1, cap), F32)]
    held = pl.BlockSpec(memory_space=pltpu.VMEM)
    return pl.pallas_call(
        lambda *a: forward_kernel(n, soon, late, n_z, *a),
        grid_spec=pltpu.PrefetchScalarGridSpec(
            num_scalar_prefetch=1,
            grid=(CHUNKS,),
            in_specs=[whole((cap, piece))] * n
            + [held, held, cols, cols, whole(near.shape), cols, whole((cap, 1))],
            out_specs=[whole(shape) for shape, _ in outs],
            scratch_shapes=[
                pltpu.VMEM((cap, n * piece), BF),
                pltpu.VMEM((piece, cap), BF),
                pltpu.VMEM((cap, 1), F32),
            ],
        ),
        out_shape=[jax.ShapeDtypeStruct(shape, kind) for shape, kind in outs],
        compiler_params=pltpu.CompilerParams(vmem_limit_bytes=20 * MIB),
        cost_estimate=pl.CostEstimate(
            flops=4 * cap * n * piece * width,
            bytes_accessed=16 * cap * width,
            transcendentals=cap * width,
        ),
    )(info, *pieces, w_gate, w_up, gate, up, near, cot_rows, share)


def in_terms(row):
    high = row.astype(BF).astype(F32)
    middle = (row - high).astype(BF).astype(F32)
    low = row - high - middle
    at = lax.broadcasted_iota(jnp.int32, (EXTRA, row.shape[1]), 0)
    terms = jnp.where(at == 0, high, jnp.where(at == 1, middle, jnp.where(at == 2, low, 0.0)))
    return terms.astype(BF)


def row_of(terms):
    return jnp.sum(terms.astype(F32), axis=0, keepdims=True)


def back_kernel(info, *refs):
    mine, other = refs[:CHUNKS], refs[CHUNKS : 2 * CHUNKS]
    route, _, wg, wu, own, first_out, third_out, second_out, gt, ut = refs[2 * CHUNKS :]
    piece = own.shape[1]
    chunk = mine[0].shape[1]
    first = info[3] == 0
    for c in range(CHUNKS):
        a, b = mine[c][...], other[c][...]
        gt[pl.ds(c * chunk, chunk), :] = jnp.where(first, a, b).T
        ut[pl.ds(c * chunk, chunk), :] = jnp.where(first, b, a).T

    targets = [(own, 0), (own, 1), (first_out, 0), (third_out, 0)]
    targets += [(first_out, 1), (third_out, 1), (second_out, 0), (second_out, 1)]

    def block(i, _):
        rows = pl.ds(pl.multiple_of(i * piece, piece), piece)
        out = jnp.dot(wg[rows, :], gt[...], preferred_element_type=F32)
        out += jnp.dot(wu[rows, :], ut[...], preferred_element_type=F32)
        for j, (ref, at) in enumerate(targets):

            @pl.when(i == j)
            def _(ref=ref, at=at):
                ref[at, :piece, :] = out.astype(ref.dtype)

        return 0

    lax.fori_loop(0, len(targets), block, 0)
    terms = in_terms(route[...])
    for ref in (first_out, third_out, second_out):
        for at in range(2):
            ref[at, piece:, :] = terms


def token_parts(info, mine, other, route, waited, weights, piece):
    cap, chunk = mine[0].shape
    depth, width = weights[0].shape
    pair, message = (2, piece, cap), (2, piece + EXTRA, cap)
    return pl.pallas_call(
        back_kernel,
        grid_spec=pltpu.PrefetchScalarGridSpec(
            num_scalar_prefetch=1,
            grid=(1,),
            in_specs=[whole((cap, chunk))] * (2 * CHUNKS)
            + [whole((1, cap)), pl.BlockSpec(memory_space=pl.ANY)]
            + [pl.BlockSpec(memory_space=pltpu.VMEM)] * 2,
            out_specs=[whole(pair)] + [whole(message)] * 3,
            scratch_shapes=[pltpu.VMEM((width, cap), BF), pltpu.VMEM((width, cap), BF)],
        ),
        out_shape=[jax.ShapeDtypeStruct(pair, F32)] + [jax.ShapeDtypeStruct(message, BF)] * 3,
        compiler_params=pltpu.CompilerParams(vmem_limit_bytes=14 * MIB),
        cost_estimate=pl.CostEstimate(
            flops=4 * cap * depth * width, bytes_accessed=4 * depth * width, transcendentals=0
        ),
    )(info, *mine, *other, route, waited, *weights)


def after(x, waited):
    def kernel(value, _, out):
        out[...] = value[...]

    return pl.pallas_call(
        kernel,
        grid=(1,),
        in_specs=[whole(x.shape), pl.BlockSpec(memory_space=pl.ANY)],
        out_specs=whole(x.shape),
        out_shape=jax.ShapeDtypeStruct(x.shape, x.dtype),
        compiler_params=pltpu.CompilerParams(vmem_limit_bytes=4 * MIB),
    )(x, waited)


def combine_kernel(own, route, first, third, second, kept, kept_route, sent):
    piece = own.shape[1]
    rows = [row_of(ref[0, piece:, :]) for ref in (first, third, second)]
    kept_route[...] = (route[...] + rows[0]) + (rows[1] + rows[2])
    for at in range(2):
        total = own[at]
        for ref in (first, third, second):
            total += ref[at, :piece, :].astype(F32)
        if at == 0:
            kept[...] = total
        else:
            sent[:piece, :] = total.astype(BF)
    sent[piece:, :] = in_terms(kept_route[...])


def combine(own, route, parts):
    _, piece, cap = own.shape
    shapes = [((piece, cap), F32), ((1, cap), F32), ((piece + EXTRA, cap), BF)]
    return pl.pallas_call(
        combine_kernel,
        out_shape=[jax.ShapeDtypeStruct(shape, kind) for shape, kind in shapes],
        compiler_params=pltpu.CompilerParams(vmem_limit_bytes=6 * MIB),
        cost_estimate=pl.CostEstimate(
            flops=8 * piece * cap, bytes_accessed=30 * piece * cap, transcendentals=0
        ),
    )(own, route, *parts)


def hop_kernel(has, n_waits, *refs):
    n = len(has)
    parts, refs = refs[:n], refs[n:]
    got, outs = refs[: sum(has)], refs[sum(has) + n_waits :]
    taken = 0
    for i in range(n):
        total = parts[i][0]
        if has[i]:
            total += got[taken][...].astype(F32)
            taken += 1
        outs[i][...] = total.astype(BF)


def hop_sums(base, places, arrived, waited):
    _, rows, cols = base.shape
    got = [a for a in arrived if a is not None]
    n = len(places)
    block = lambda j: pl.BlockSpec((1, rows, cols), lambda i: (j, 0, 0))
    return pl.pallas_call(
        lambda *a: hop_kernel([x is not None for x in arrived], len(waited), *a),
        grid=(1,),
        in_specs=[block(j) for j in places]
        + [whole((rows, cols))] * len(got)
        + [pl.BlockSpec(memory_space=pl.ANY)] * len(waited),
        out_specs=[whole((rows, cols))] * n,
        out_shape=[jax.ShapeDtypeStruct((rows, cols), BF)] * n,
        compiler_params=pltpu.CompilerParams(vmem_limit_bytes=6 * MIB),
        cost_estimate=pl.CostEstimate(
            flops=2 * n * rows * cols, bytes_accessed=8 * n * rows * cols, transcendentals=0
        ),
    )(*[base] * n, *got, *waited)


def far_kernel(n, n_z, info, *refs):
    out = refs[-1]
    for y in range(n // 2):
        for x in range(2):
            at = lax.rem((info[0] ^ (y + x * (n // 2))) - info[1] + n_z, n_z)
            out[at] = refs[y][x]


def far_operand(info, arrays, n, n_z):
    rows, cap = arrays[0].shape[1:]
    return pl.pallas_call(
        lambda *a: far_kernel(n, n_z, *a),
        grid_spec=pltpu.PrefetchScalarGridSpec(
            num_scalar_prefetch=1,
            grid=(1,),
            in_specs=[whole(a.shape) for a in arrays],
            out_specs=whole((n_z, rows, cap)),
        ),
        out_shape=jax.ShapeDtypeStruct((n_z, rows, cap), BF),
        compiler_params=pltpu.CompilerParams(vmem_limit_bytes=8 * MIB),
        cost_estimate=pl.CostEstimate(
            flops=0, bytes_accessed=4 * n * rows * cap, transcendentals=0
        ),
    )(info, *arrays)


def on_device(tokens, hidden_cot, w_gate, w_up, expert_ids, route_fixed):
    tok_dev, piece = tokens.shape
    width = w_gate.shape[1]
    n_tensor = lax.axis_size("tensor")
    n_dp = lax.axis_size("dp")
    n_z = n_dp // 4
    half = piece // 2
    xlo = n_tensor // 2
    t = lax.axis_index("tensor")
    dp = lax.axis_index("dp")
    z, xh, core = dp // 4, (dp // 2) % 2, dp % 2
    info = jnp.stack([t, z, xh, core]).astype(jnp.int32)
    tie = lax.optimization_barrier

    def over_tensor(x, k):
        return lax.ppermute(x, "tensor", [(i, i ^ k) for i in range(n_tensor)])

    def over_dp(x, k):
        return lax.ppermute(x, "dp", [(i, i ^ k) for i in range(n_dp)])

    def along_z(x, k):
        return lax.ppermute(x, "dp", [(i, (i + 4 * k) % n_dp) for i in range(n_dp)])

    selected = expert_ids == 0
    flag = jnp.any(selected, axis=1)
    place = jnp.arange(tok_dev, dtype=jnp.int32)
    upto = (place[:, None] <= place[None, :]).astype(BF)
    slot_of = jnp.dot(flag.astype(BF)[None, :], upto, preferred_element_type=F32)[0] - 1.0
    slot_of = jnp.where(flag, slot_of.astype(jnp.int32), -1)
    mask = slot_of[None, :] == jnp.arange(CAP, dtype=jnp.int32)[:, None]
    dispatch = mask.astype(BF)
    share_all = jnp.sum(jnp.where(selected, route_fixed, 0), axis=1).astype(F32) / 65536.0

    hidden_cot = pltpu.with_memory_space_constraint(hidden_cot, pltpu.HBM)
    tokens = pltpu.with_memory_space_constraint(tokens, pltpu.HBM)
    w_gate = pltpu.with_memory_space_constraint(w_gate, pltpu.HBM)
    w_up = pltpu.with_memory_space_constraint(w_up, pltpu.HBM)
    picked, far_piece = dispatch_tokens(info, slot_of[None, :], tokens)
    cot_rows, share = dispatch_cots(slot_of[None, :], share_all[None, :], hidden_cot)
    near = [None] * n_tensor
    near[xlo] = over_tensor(picked, xlo)
    near[1] = over_tensor(picked, 1)
    near[3] = over_tensor(picked, 3)
    far_piece = over_dp(far_piece, 2)
    picked, near[1], near[3], near[xlo], cot_rows, share = tie(
        (picked, near[1], near[3], near[xlo], cot_rows, share)
    )
    near[0] = picked
    near[xlo + 1] = over_tensor(near[1], xlo)
    near[xlo + 3] = over_tensor(near[3], xlo)
    near[2] = over_tensor(picked, 2)
    near[xlo + 2] = over_tensor(near[xlo], 2)
    soon, late = (0, xlo, 1, 3), (xlo + 1, xlo + 3, 2, xlo + 2)
    order = jnp.stack([t ^ k for k in soon + late] + [xh]).astype(jnp.int32)
    gate, up, near_soon, *weights = early(order, [near[k] for k in soon], w_gate, w_up)
    far_piece, near[late[3]] = tie((far_piece, near[late[3]]))
    far_pair = jnp.stack([far_piece, over_tensor(far_piece, xlo)])
    late_near, gate, up = tie(([near[k] for k in late], gate, up))
    outs = forward(
        info, late_near, soon, late, *weights, gate, up, near_soon, cot_rows, share, n_z
    )
    mine, other = outs[:CHUNKS], outs[CHUNKS : 2 * CHUNKS]
    near_left, route_part = outs[2 * CHUNKS :]

    def to_partners(c):
        return [mine[c], over_dp(other[c], 1), over_dp(mine[c], 2), over_dp(other[c], 3)]

    cots = [to_partners(0)]
    near_sib = over_dp(near_left, 1)
    far = [far_pair] + [over_tensor(far_pair, k) for k in (1, 3)]
    far_pair, near_sib = tie((far_pair, near_sib))
    far.insert(2, over_tensor(far_pair, 2))
    own_part, *sent = token_parts(info, mine, other, route_part, far_pair, weights, piece)

    def product(a, b):
        return jnp.dot(a.reshape(n_z * half, CAP), b, preferred_element_type=F32)

    close = product(near_left, cots[0][0]) + product(near_sib, cots[0][1])
    far, own_part, sent, mine, other, close = tie((far, own_part, sent, mine, other, close))
    far_left = far_operand(info, far, n_tensor, n_z)
    far_sib = over_dp(far_left, 1)
    for c in range(1, CHUNKS):
        mine, other, cots[-1] = tie((mine, other, cots[-1]))
        cots.append(to_partners(c))
    step = width // CHUNKS

    def sums_of(c, close):
        base = tie(close) + product(far_left, cots[c][2])
        base = tie(base + product(far_sib, cots[c][3]))
        return base.reshape(n_z, half, step)

    class Ring:
        def __init__(self, c, base):
            self.base = base
            self.up_hops = n_z // 2 - c % 2
            self.down_hops = n_z - 1 - self.up_hops
            self.rising = self.falling = None

        def hop(self, i, waited):
            places, arrived = [], []
            if i < self.up_hops:
                places.append(self.up_hops - i)
                arrived.append(self.rising)
            if i < self.down_hops:
                places.append((n_z - self.down_hops + i) % n_z)
                arrived.append(self.falling)
            out = hop_sums(self.base, places, arrived, waited)
            if i < self.up_hops:
                self.rising = along_z(out[0], 1)
            if i < self.down_hops:
                self.falling = along_z(out[-1], -1)
            return out[0]

        def finish(self):
            total = self.base[0] + self.rising.astype(F32) + self.falling.astype(F32)
            return total.astype(BF).reshape(2, half // 2, step)

    rings = [Ring(0, sums_of(0, close))]
    waited = rings[0].hop(0, [])
    sums = {1: over_tensor(after(sent[0], waited), 1)}
    for c in range(1, CHUNKS):
        lefts = [after(near_left, waited), near_sib]
        close = product(lefts[0], cots[c][0]) + product(lefts[1], cots[c][1])
        rings.append(Ring(c, sums_of(c, close)))
        waited = rings[c].hop(0, [waited])
    for i in range(1, n_z // 2):
        waited = rings[0].hop(i, [waited])
        if i < 3:
            sums[4 - i] = over_tensor(after(sent[i], waited), 4 - i)
        for ring in rings[1:]:
            waited = ring.hop(i, [waited, sums[(1, 3, 2)[i - 1]]])
    whole_rows = jnp.concatenate([ring.finish() for ring in rings], axis=2)
    kept = lax.dynamic_index_in_dim(whole_rows, core, 0, keepdims=False)
    swapped = over_dp(lax.dynamic_index_in_dim(whole_rows, 1 - core, 0, keepdims=False), 1)
    gate_grad = jnp.where(core == 0, kept, swapped)
    up_grad = jnp.where(core == 0, swapped, kept)

    total, route_total, message = combine(own_part, route_part, [sums[1], sums[3], sums[2]])
    message = over_tensor(message, xlo)
    total = total + message[:piece].astype(F32)
    route_total = route_total + row_of(message[piece:])
    token_grad = lax.dot_general(
        dispatch, total.astype(BF), (((0,), (1,)), ((), ())), preferred_element_type=F32
    ).astype(BF)
    route_grad = jnp.sum(jnp.where(mask, route_total[0][:, None], 0.0), axis=0)
    return token_grad, gate_grad, up_grad, route_grad


def solution(mesh):
    return jax.shard_map(
        on_device,
        mesh=mesh,
        in_specs=(
            P("dp", "tensor"),
            P("dp", "tensor"),
            P(None, "tensor"),
            P(None, "tensor"),
            P("dp", None),
            P("dp", None),
        ),
        out_specs=(P("dp", "tensor"), P("dp", "tensor"), P("dp", "tensor"), P("dp")),
        check_vma=False,
    )
```

```python
import jax
import jax.numpy as jnp
from jax import lax
from jax.experimental import pallas as pl
from jax.experimental.pallas import tpu as pltpu
from jax.sharding import PartitionSpec as P

CAP = 256
CHUNKS = 2
EXTRA = 16
BF = jnp.bfloat16
F32 = jnp.float32
MIB = 2**20


def whole(shape):
    return pl.BlockSpec(shape, lambda *_: (0,) * len(shape))


def placed(info, k, n_z):
    ahead = lax.rem((info[0] ^ k) - info[1] + n_z, n_z)
    behind = lax.rem(n_z - ahead, n_z)
    first = info[3] == 0
    return jnp.where(first, ahead, behind), jnp.where(first, behind, ahead)


def dispatch_kernel(info, slots, tokens, picked, far, turned):
    cap, rows = picked.shape[0], far.shape[0]
    tok_dev = slots.shape[1]
    ids = lax.broadcasted_iota(jnp.int32, (cap, tok_dev), 0)
    mask = (slots[...] == ids).astype(F32).astype(BF)
    got = jnp.dot(mask, tokens[...], preferred_element_type=F32)
    picked[...] = got.astype(BF)
    turned[...] = got.T.astype(BF)
    start = pl.multiple_of((1 - info[2]) * rows, rows)
    far[...] = turned[pl.ds(start, rows), :]


def dispatch_tokens(info, slots, tokens):
    tok_dev, piece = tokens.shape
    return pl.pallas_call(
        dispatch_kernel,
        grid_spec=pltpu.PrefetchScalarGridSpec(
            num_scalar_prefetch=1,
            grid=(1,),
            in_specs=[whole((1, tok_dev)), whole((tok_dev, piece))],
            out_specs=[whole((CAP, piece)), whole((piece // 2, CAP))],
            scratch_shapes=[pltpu.VMEM((piece, CAP), BF)],
        ),
        out_shape=[
            jax.ShapeDtypeStruct((CAP, piece), BF),
            jax.ShapeDtypeStruct((piece // 2, CAP), BF),
        ],
        compiler_params=pltpu.CompilerParams(vmem_limit_bytes=8 * MIB),
        cost_estimate=pl.CostEstimate(
            flops=2 * CAP * tok_dev * piece, bytes_accessed=4 * tok_dev * piece, transcendentals=0
        ),
    )(info, slots, tokens)


def cot_kernel(slots, share_all, cot, rows, share):
    cap, tok_dev = rows.shape[0], slots.shape[1]
    mask = slots[...] == lax.broadcasted_iota(jnp.int32, (cap, tok_dev), 0)
    hot = mask.astype(F32).astype(BF)
    rows[...] = jnp.dot(hot, cot[...], preferred_element_type=F32).astype(BF)
    share[...] = jnp.sum(jnp.where(mask, share_all[...], 0.0), axis=1, keepdims=True)


def dispatch_cots(slots, share_all, hidden_cot):
    tok_dev, width = hidden_cot.shape
    return pl.pallas_call(
        cot_kernel,
        out_shape=[
            jax.ShapeDtypeStruct((CAP, width), BF),
            jax.ShapeDtypeStruct((CAP, 1), F32),
        ],
        compiler_params=pltpu.CompilerParams(vmem_limit_bytes=8 * MIB),
        cost_estimate=pl.CostEstimate(
            flops=2 * CAP * tok_dev * width, bytes_accessed=4 * tok_dev * width, transcendentals=0
        ),
    )(slots, share_all, hidden_cot)


def early_kernel(n, order, *refs):
    pieces = refs[:n]
    wg, wu, gate, up, near, all_g, all_u, held, turned, sems = refs[n:]
    cap, piece = pieces[0].shape
    half = near.shape[1]

    def copies(i):
        start = pl.multiple_of(order[i] * piece, piece)
        return [
            pltpu.make_async_copy(
                w.at[pl.ds(start, piece)], ref.at[pl.ds(i * piece, piece)], sems.at[i, j]
            )
            for j, (w, ref) in enumerate(((wg, all_g), (wu, all_u)))
        ]

    every = [copies(i) for i in range(2 * n)]
    for pair in every:
        for copy in pair:
            copy.start()
    for k in range(n):
        held[:, k * piece : (k + 1) * piece] = pieces[k][...]

    def turn(k, _):
        turned[...] = held[:, pl.ds(pl.multiple_of(k * piece, piece), piece)].T
        start = pl.multiple_of(order[2 * n] * half, half)
        near[k] = turned[pl.ds(start, half), :]
        return 0

    lax.fori_loop(0, n, turn, 0)
    for pair in every[:n]:
        for copy in pair:
            copy.wait()
    block = gate.shape[1] // CHUNKS

    def multiply(c, _):
        here = pl.ds(pl.multiple_of(c * block, block), block)
        gate[:, here] = jnp.dot(held[...], all_g[: n * piece, here], preferred_element_type=F32)
        up[:, here] = jnp.dot(held[...], all_u[: n * piece, here], preferred_element_type=F32)
        return 0

    lax.fori_loop(0, CHUNKS, multiply, 0)
    for pair in every[n:]:
        for copy in pair:
            copy.wait()


def early(order, pieces, w_gate, w_up):
    n = len(pieces)
    cap, piece = pieces[0].shape
    width = w_gate.shape[1]
    hbm = pl.BlockSpec(memory_space=pl.ANY)
    return pl.pallas_call(
        lambda *a: early_kernel(n, *a),
        grid_spec=pltpu.PrefetchScalarGridSpec(
            num_scalar_prefetch=1,
            grid=(1,),
            in_specs=[whole((cap, piece))] * n + [hbm, hbm],
            out_specs=[whole((cap, width))] * 2
            + [whole((n, piece // 2, cap))]
            + [pl.BlockSpec(memory_space=pltpu.VMEM)] * 2,
            scratch_shapes=[
                pltpu.VMEM((cap, n * piece), BF),
                pltpu.VMEM((piece, cap), BF),
                pltpu.SemaphoreType.DMA((2 * n, 2)),
            ],
        ),
        out_shape=[jax.ShapeDtypeStruct((cap, width), F32)] * 2
        + [jax.ShapeDtypeStruct((n, piece // 2, cap), BF)]
        + [pltpu.VMEM((2 * n * piece, width), BF)] * 2,
        compiler_params=pltpu.CompilerParams(vmem_limit_bytes=14 * MIB),
        cost_estimate=pl.CostEstimate(
            flops=4 * cap * n * piece * width,
            bytes_accessed=8 * n * piece * width,
            transcendentals=0,
        ),
    )(order, *pieces, w_gate, w_up)


def forward_kernel(n, soon, late, n_z, info, *refs):
    pieces = refs[:n]
    wg, wu, gate_in, up_in, near_in, cot, share = refs[n : n + 7]
    mine, other = refs[n + 7 : n + 7 + CHUNKS], refs[n + 7 + CHUNKS : n + 7 + 2 * CHUNKS]
    near_left, near_send, route_out, held, turned, route = refs[n + 7 + 2 * CHUNKS :]
    step = pl.program_id(0)
    piece, cap = turned.shape
    half, block = near_left.shape[1], cot.shape[1]

    @pl.when(step == 0)
    def _():
        route[...] = jnp.zeros_like(route)
        for i in range(n):
            held[:, i * piece : (i + 1) * piece] = pieces[i][...]

    here = pl.ds(pl.multiple_of(step * block, block), block)
    gate = gate_in[...] + jnp.dot(held[...], wg[n * piece :, here], preferred_element_type=F32)
    up = up_in[...] + jnp.dot(held[...], wu[n * piece :, here], preferred_element_type=F32)
    sig = jax.nn.sigmoid(gate)
    activated = gate * sig
    hidden = (activated * up).astype(BF).astype(F32)
    cot_wide = cot[...].astype(F32)
    route[...] += jnp.sum(hidden * cot_wide, axis=1, keepdims=True)
    scaled = share[...] * cot_wide
    gate_cot = scaled * up * sig * (1.0 + gate * (1.0 - sig))
    up_cot = scaled * activated
    first = info[3] == 0
    own = jnp.where(first, gate_cot, up_cot).astype(BF)
    rest = jnp.where(first, up_cot, gate_cot).astype(BF)
    for c in range(CHUNKS):

        @pl.when(step == c)
        def _(c=c):
            mine[c][...] = own
            other[c][...] = rest

    @pl.when(step == CHUNKS - 1)
    def _():
        route_out[...] = jnp.broadcast_to(route[...], (cap, 128)).T[:1, :]
        for i, k in enumerate(soon):
            at, there = placed(info, k, n_z)
            near_left[at] = near_in[i]
            near_send[there] = near_in[i]
        for i, k in enumerate(late):
            turned[...] = held[:, i * piece : (i + 1) * piece].T
            start = pl.multiple_of(info[2] * half, half)
            at, there = placed(info, k, n_z)
            near_left[at] = turned[pl.ds(start, half), :]
            near_send[there] = turned[pl.ds(start, half), :]


def forward(info, pieces, soon, late, w_gate, w_up, gate, up, near, cot_rows, share, n_z):
    n = len(pieces)
    cap, piece = pieces[0].shape
    width = w_gate.shape[1]
    block = width // CHUNKS
    cols = pl.BlockSpec((cap, block), lambda j, *_: (0, j))
    near_left = (n_z, piece // 2, cap)
    outs = [((cap, block), BF)] * (2 * CHUNKS) + [(near_left, BF)] * 2 + [((1, cap), F32)]
    held = pl.BlockSpec(memory_space=pltpu.VMEM)
    return pl.pallas_call(
        lambda *a: forward_kernel(n, soon, late, n_z, *a),
        grid_spec=pltpu.PrefetchScalarGridSpec(
            num_scalar_prefetch=1,
            grid=(CHUNKS,),
            in_specs=[whole((cap, piece))] * n
            + [held, held, cols, cols, whole(near.shape), cols, whole((cap, 1))],
            out_specs=[whole(shape) for shape, _ in outs],
            scratch_shapes=[
                pltpu.VMEM((cap, n * piece), BF),
                pltpu.VMEM((piece, cap), BF),
                pltpu.VMEM((cap, 1), F32),
            ],
        ),
        out_shape=[jax.ShapeDtypeStruct(shape, kind) for shape, kind in outs],
        compiler_params=pltpu.CompilerParams(vmem_limit_bytes=20 * MIB),
        cost_estimate=pl.CostEstimate(
            flops=4 * cap * n * piece * width,
            bytes_accessed=16 * cap * width,
            transcendentals=cap * width,
        ),
    )(info, *pieces, w_gate, w_up, gate, up, near, cot_rows, share)


def in_terms(row):
    high = row.astype(BF).astype(F32)
    middle = (row - high).astype(BF).astype(F32)
    low = row - high - middle
    at = lax.broadcasted_iota(jnp.int32, (EXTRA, row.shape[1]), 0)
    terms = jnp.where(at == 0, high, jnp.where(at == 1, middle, jnp.where(at == 2, low, 0.0)))
    return terms.astype(BF)


def row_of(terms):
    return jnp.sum(terms.astype(F32), axis=0, keepdims=True)


def back_kernel(info, *refs):
    mine, other = refs[:CHUNKS], refs[CHUNKS : 2 * CHUNKS]
    route, _, wg, wu, own, first_out, third_out, second_out, gt, ut = refs[2 * CHUNKS :]
    piece = own.shape[1]
    chunk = mine[0].shape[1]
    first = info[3] == 0
    for c in range(CHUNKS):
        a, b = mine[c][...], other[c][...]
        gt[pl.ds(c * chunk, chunk), :] = jnp.where(first, a, b).T
        ut[pl.ds(c * chunk, chunk), :] = jnp.where(first, b, a).T

    targets = [(own, 0), (own, 1), (first_out, 0), (third_out, 0)]
    targets += [(first_out, 1), (third_out, 1), (second_out, 0), (second_out, 1)]

    def block(i, _):
        rows = pl.ds(pl.multiple_of(i * piece, piece), piece)
        out = jnp.dot(wg[rows, :], gt[...], preferred_element_type=F32)
        out += jnp.dot(wu[rows, :], ut[...], preferred_element_type=F32)
        for j, (ref, at) in enumerate(targets):

            @pl.when(i == j)
            def _(ref=ref, at=at):
                ref[at, :piece, :] = out.astype(ref.dtype)

        return 0

    lax.fori_loop(0, len(targets), block, 0)
    terms = in_terms(route[...])
    for ref in (first_out, third_out, second_out):
        for at in range(2):
            ref[at, piece:, :] = terms


def token_parts(info, mine, other, route, waited, weights, piece):
    cap, chunk = mine[0].shape
    depth, width = weights[0].shape
    pair, message = (2, piece, cap), (2, piece + EXTRA, cap)
    return pl.pallas_call(
        back_kernel,
        grid_spec=pltpu.PrefetchScalarGridSpec(
            num_scalar_prefetch=1,
            grid=(1,),
            in_specs=[whole((cap, chunk))] * (2 * CHUNKS)
            + [whole((1, cap)), pl.BlockSpec(memory_space=pl.ANY)]
            + [pl.BlockSpec(memory_space=pltpu.VMEM)] * 2,
            out_specs=[whole(pair)] + [whole(message)] * 3,
            scratch_shapes=[pltpu.VMEM((width, cap), BF), pltpu.VMEM((width, cap), BF)],
        ),
        out_shape=[jax.ShapeDtypeStruct(pair, F32)] + [jax.ShapeDtypeStruct(message, BF)] * 3,
        compiler_params=pltpu.CompilerParams(vmem_limit_bytes=14 * MIB),
        cost_estimate=pl.CostEstimate(
            flops=4 * cap * depth * width, bytes_accessed=4 * depth * width, transcendentals=0
        ),
    )(info, *mine, *other, route, waited, *weights)


def after(x, waited):
    def kernel(value, _, out):
        out[...] = value[...]

    return pl.pallas_call(
        kernel,
        grid=(1,),
        in_specs=[whole(x.shape), pl.BlockSpec(memory_space=pl.ANY)],
        out_specs=whole(x.shape),
        out_shape=jax.ShapeDtypeStruct(x.shape, x.dtype),
        compiler_params=pltpu.CompilerParams(vmem_limit_bytes=4 * MIB),
    )(x, waited)


def combine_kernel(own, route, first, third, second, kept, kept_route, sent):
    piece = own.shape[1]
    rows = [row_of(ref[0, piece:, :]) for ref in (first, third, second)]
    kept_route[...] = (route[...] + rows[0]) + (rows[1] + rows[2])
    for at in range(2):
        total = own[at]
        for ref in (first, third, second):
            total += ref[at, :piece, :].astype(F32)
        if at == 0:
            kept[...] = total
        else:
            sent[:piece, :] = total.astype(BF)
    sent[piece:, :] = in_terms(kept_route[...])


def combine(own, route, parts):
    _, piece, cap = own.shape
    shapes = [((piece, cap), F32), ((1, cap), F32), ((piece + EXTRA, cap), BF)]
    return pl.pallas_call(
        combine_kernel,
        out_shape=[jax.ShapeDtypeStruct(shape, kind) for shape, kind in shapes],
        compiler_params=pltpu.CompilerParams(vmem_limit_bytes=6 * MIB),
        cost_estimate=pl.CostEstimate(
            flops=8 * piece * cap, bytes_accessed=30 * piece * cap, transcendentals=0
        ),
    )(own, route, *parts)


def hop_kernel(has, n_waits, *refs):
    n = len(has)
    parts, refs = refs[:n], refs[n:]
    got, outs = refs[: sum(has)], refs[sum(has) + n_waits :]
    taken = 0
    for i in range(n):
        total = parts[i][0]
        if has[i]:
            total += got[taken][...].astype(F32)
            taken += 1
        outs[i][...] = total.astype(BF)


def hop_sums(base, places, arrived, waited):
    _, rows, cols = base.shape
    got = [a for a in arrived if a is not None]
    n = len(places)
    block = lambda j: pl.BlockSpec((1, rows, cols), lambda i: (j, 0, 0))
    return pl.pallas_call(
        lambda *a: hop_kernel([x is not None for x in arrived], len(waited), *a),
        grid=(1,),
        in_specs=[block(j) for j in places]
        + [whole((rows, cols))] * len(got)
        + [pl.BlockSpec(memory_space=pl.ANY)] * len(waited),
        out_specs=[whole((rows, cols))] * n,
        out_shape=[jax.ShapeDtypeStruct((rows, cols), BF)] * n,
        compiler_params=pltpu.CompilerParams(vmem_limit_bytes=6 * MIB),
        cost_estimate=pl.CostEstimate(
            flops=2 * n * rows * cols, bytes_accessed=8 * n * rows * cols, transcendentals=0
        ),
    )(*[base] * n, *got, *waited)


def far_kernel(n, n_z, info, *refs):
    out, send = refs[-2:]
    for y in range(n // 2):
        for x in range(2):
            at, there = placed(info, y + x * (n // 2), n_z)
            out[at] = refs[y][x]
            send[there] = refs[y][x]


def far_operand(info, arrays, n, n_z):
    rows, cap = arrays[0].shape[1:]
    return pl.pallas_call(
        lambda *a: far_kernel(n, n_z, *a),
        grid_spec=pltpu.PrefetchScalarGridSpec(
            num_scalar_prefetch=1,
            grid=(1,),
            in_specs=[whole(a.shape) for a in arrays],
            out_specs=[whole((n_z, rows, cap))] * 2,
        ),
        out_shape=[jax.ShapeDtypeStruct((n_z, rows, cap), BF)] * 2,
        compiler_params=pltpu.CompilerParams(vmem_limit_bytes=8 * MIB),
        cost_estimate=pl.CostEstimate(
            flops=0, bytes_accessed=4 * n * rows * cap, transcendentals=0
        ),
    )(info, *arrays)


def on_device(tokens, hidden_cot, w_gate, w_up, expert_ids, route_fixed):
    tok_dev, piece = tokens.shape
    width = w_gate.shape[1]
    n_tensor = lax.axis_size("tensor")
    n_dp = lax.axis_size("dp")
    n_z = n_dp // 4
    half = piece // 2
    xlo = n_tensor // 2
    t = lax.axis_index("tensor")
    dp = lax.axis_index("dp")
    z, xh, core = dp // 4, (dp // 2) % 2, dp % 2
    info = jnp.stack([t, z, xh, core]).astype(jnp.int32)
    tie = lax.optimization_barrier

    def over_tensor(x, k):
        return lax.ppermute(x, "tensor", [(i, i ^ k) for i in range(n_tensor)])

    def over_dp(x, k):
        return lax.ppermute(x, "dp", [(i, i ^ k) for i in range(n_dp)])

    def along_z(x, k):
        pairs = [(i, (i + 4 * (k if i % 2 == 0 else -k)) % n_dp) for i in range(n_dp)]
        return lax.ppermute(x, "dp", pairs)

    def over_both(x, k, m):
        n_all = n_dp * n_tensor
        pairs = [(i, i ^ (k * n_tensor + m)) for i in range(n_all)]
        return lax.ppermute(x, ("dp", "tensor"), pairs)

    selected = expert_ids == 0
    flag = jnp.any(selected, axis=1)
    place = jnp.arange(tok_dev, dtype=jnp.int32)
    upto = (place[:, None] <= place[None, :]).astype(BF)
    slot_of = jnp.dot(flag.astype(BF)[None, :], upto, preferred_element_type=F32)[0] - 1.0
    slot_of = jnp.where(flag, slot_of.astype(jnp.int32), -1)
    mask = slot_of[None, :] == jnp.arange(CAP, dtype=jnp.int32)[:, None]
    dispatch = mask.astype(BF)
    share_all = jnp.sum(jnp.where(selected, route_fixed, 0), axis=1).astype(F32) / 65536.0

    hidden_cot = pltpu.with_memory_space_constraint(hidden_cot, pltpu.HBM)
    tokens = pltpu.with_memory_space_constraint(tokens, pltpu.HBM)
    w_gate = pltpu.with_memory_space_constraint(w_gate, pltpu.HBM)
    w_up = pltpu.with_memory_space_constraint(w_up, pltpu.HBM)
    picked, far_piece = dispatch_tokens(info, slot_of[None, :], tokens)
    cot_rows, share = dispatch_cots(slot_of[None, :], share_all[None, :], hidden_cot)
    near = [None] * n_tensor
    near[xlo] = over_tensor(picked, xlo)
    near[1] = over_tensor(picked, 1)
    near[3] = over_tensor(picked, 3)
    far_other = over_both(far_piece, 2, xlo)
    picked, near[1], near[3], near[xlo], cot_rows, share, far_other, far_piece = tie(
        (picked, near[1], near[3], near[xlo], cot_rows, share, far_other, far_piece)
    )
    far_piece = over_dp(far_piece, 2)
    near[0] = picked
    near[xlo + 1] = over_tensor(near[1], xlo)
    near[xlo + 3] = over_tensor(near[3], xlo)
    near[2] = over_tensor(picked, 2)
    near[xlo + 2] = over_tensor(near[xlo], 2)
    soon, late = (0, xlo, 1, 3), (xlo + 1, xlo + 3, 2, xlo + 2)
    order = jnp.stack([t ^ k for k in soon + late] + [xh]).astype(jnp.int32)
    gate, up, near_soon, *weights = early(order, [near[k] for k in soon], w_gate, w_up)
    far_pair = jnp.stack([far_piece, far_other])
    late_near, gate, up, far_pair = tie(([near[k] for k in late], gate, up, far_pair))
    outs = forward(
        info, late_near, soon, late, *weights, gate, up, near_soon, cot_rows, share, n_z
    )
    mine, other = outs[:CHUNKS], outs[CHUNKS : 2 * CHUNKS]
    near_left, near_send, route_part = outs[2 * CHUNKS :]

    def to_partners(c):
        return [mine[c], over_dp(other[c], 1), over_dp(mine[c], 2), over_dp(other[c], 3)]

    cots = [to_partners(0)]
    near_sib = over_dp(near_send, 1)
    far_pair, near_sib = tie((far_pair, near_sib))
    far = [far_pair] + [over_tensor(far_pair, k) for k in (1, 2, 3)]
    own_part, *sent = token_parts(info, mine, other, route_part, far_pair, weights, piece)

    def product(a, b):
        return jnp.dot(a.reshape(n_z * half, CAP), b, preferred_element_type=F32)

    close = product(near_left, cots[0][0]) + product(near_sib, cots[0][1])
    far, own_part, sent, mine, other, close = tie((far, own_part, sent, mine, other, close))
    far_left, far_send = far_operand(info, far, n_tensor, n_z)
    far_sib = over_dp(far_send, 1)
    for c in range(1, CHUNKS):
        mine, other, cots[-1] = tie((mine, other, cots[-1]))
        cots.append(to_partners(c))
    step = width // CHUNKS

    def sums_of(c, close):
        base = tie(close) + product(far_left, cots[c][2])
        base = tie(base + product(far_sib, cots[c][3]))
        return base.reshape(n_z, half, step)

    class Ring:
        def __init__(self, c, base):
            self.base = base
            self.up_hops = n_z // 2 - c % 2
            self.down_hops = n_z - 1 - self.up_hops
            self.rising = self.falling = None

        def hop(self, i, waited):
            places, arrived = [], []
            if i < self.up_hops:
                places.append(self.up_hops - i)
                arrived.append(self.rising)
            if i < self.down_hops:
                places.append((n_z - self.down_hops + i) % n_z)
                arrived.append(self.falling)
            out = hop_sums(self.base, places, arrived, waited)
            if i < self.up_hops:
                self.rising = along_z(out[0], 1)
            if i < self.down_hops:
                self.falling = along_z(out[-1], -1)
            return out[0]

        def finish(self):
            total = self.base[0] + self.rising.astype(F32) + self.falling.astype(F32)
            return total.astype(BF).reshape(2, half // 2, step)

    rings = [Ring(0, sums_of(0, close))]
    waited = rings[0].hop(0, [])
    sums = {1: over_tensor(after(sent[0], waited), 1)}
    for c in range(1, CHUNKS):
        lefts = [after(near_left, waited), near_sib]
        close = product(lefts[0], cots[c][0]) + product(lefts[1], cots[c][1])
        rings.append(Ring(c, sums_of(c, close)))
        waited = rings[c].hop(0, [waited])
    for i in range(1, n_z // 2):
        waited = rings[0].hop(i, [waited])
        if i < 3:
            sums[4 - i] = over_tensor(after(sent[i], waited), 4 - i)
        else:
            parts = [sums[1], sums[3], sums[2]]
            total, route_total, message = combine(own_part, route_part, parts)
        for ring in rings[1:]:
            waited = ring.hop(i, [waited, message if i == 3 else sums[(1, 3)[i - 1]]])
    whole_rows = jnp.concatenate([ring.finish() for ring in rings], axis=2)
    kept = lax.dynamic_index_in_dim(whole_rows, core, 0, keepdims=False)
    swapped = over_dp(lax.dynamic_index_in_dim(whole_rows, 1 - core, 0, keepdims=False), 1)
    gate_grad = jnp.where(core == 0, kept, swapped)
    up_grad = jnp.where(core == 0, swapped, kept)

    message = over_tensor(message, xlo)
    total = total + message[:piece].astype(F32)
    route_total = route_total + row_of(message[piece:])
    token_grad = lax.dot_general(
        dispatch, total.astype(BF), (((0,), (1,)), ((), ())), preferred_element_type=F32
    ).astype(BF)
    route_grad = jnp.sum(jnp.where(mask, route_total[0][:, None], 0.0), axis=0)
    return token_grad, gate_grad, up_grad, route_grad


def solution(mesh):
    return jax.shard_map(
        on_device,
        mesh=mesh,
        in_specs=(
            P("dp", "tensor"),
            P("dp", "tensor"),
            P(None, "tensor"),
            P(None, "tensor"),
            P("dp", None),
            P("dp", None),
        ),
        out_specs=(P("dp", "tensor"), P("dp", "tensor"), P("dp", "tensor"), P("dp")),
        check_vma=False,
    )
```

```python
import jax
import jax.numpy as jnp
from jax import lax
from jax.experimental import pallas as pl
from jax.experimental.pallas import tpu as pltpu
from jax.sharding import PartitionSpec as P

CAP = 256
CHUNKS = 2
EXTRA = 16
BF = jnp.bfloat16
F32 = jnp.float32
MIB = 2**20


def whole(shape):
    return pl.BlockSpec(shape, lambda *_: (0,) * len(shape))


def placed(info, k, n_z):
    ahead = lax.rem((info[0] ^ k) - info[1] + n_z, n_z)
    behind = lax.rem(n_z - ahead, n_z)
    first = info[3] == 0
    return jnp.where(first, ahead, behind), jnp.where(first, behind, ahead)


def dispatch_kernel(info, slots, tokens, picked, far, turned):
    cap, rows = picked.shape[0], far.shape[0]
    tok_dev = slots.shape[1]
    ids = lax.broadcasted_iota(jnp.int32, (cap, tok_dev), 0)
    mask = (slots[...] == ids).astype(F32).astype(BF)
    got = jnp.dot(mask, tokens[...], preferred_element_type=F32)
    picked[...] = got.astype(BF)
    turned[...] = got.T.astype(BF)
    start = pl.multiple_of((1 - info[2]) * rows, rows)
    far[...] = turned[pl.ds(start, rows), :]


def dispatch_tokens(info, slots, tokens):
    tok_dev, piece = tokens.shape
    return pl.pallas_call(
        dispatch_kernel,
        grid_spec=pltpu.PrefetchScalarGridSpec(
            num_scalar_prefetch=1,
            grid=(1,),
            in_specs=[whole((1, tok_dev)), whole((tok_dev, piece))],
            out_specs=[whole((CAP, piece)), whole((piece // 2, CAP))],
            scratch_shapes=[pltpu.VMEM((piece, CAP), BF)],
        ),
        out_shape=[
            jax.ShapeDtypeStruct((CAP, piece), BF),
            jax.ShapeDtypeStruct((piece // 2, CAP), BF),
        ],
        compiler_params=pltpu.CompilerParams(vmem_limit_bytes=8 * MIB),
        cost_estimate=pl.CostEstimate(
            flops=2 * CAP * tok_dev * piece, bytes_accessed=4 * tok_dev * piece, transcendentals=0
        ),
    )(info, slots, tokens)


def cot_kernel(slots, share_all, cot, rows, share):
    cap, tok_dev = rows.shape[0], slots.shape[1]
    mask = slots[...] == lax.broadcasted_iota(jnp.int32, (cap, tok_dev), 0)
    hot = mask.astype(F32).astype(BF)
    rows[...] = jnp.dot(hot, cot[...], preferred_element_type=F32).astype(BF)
    share[...] = jnp.sum(jnp.where(mask, share_all[...], 0.0), axis=1, keepdims=True)


def dispatch_cots(slots, share_all, hidden_cot):
    tok_dev, width = hidden_cot.shape
    return pl.pallas_call(
        cot_kernel,
        out_shape=[
            jax.ShapeDtypeStruct((CAP, width), BF),
            jax.ShapeDtypeStruct((CAP, 1), F32),
        ],
        compiler_params=pltpu.CompilerParams(vmem_limit_bytes=8 * MIB),
        cost_estimate=pl.CostEstimate(
            flops=2 * CAP * tok_dev * width, bytes_accessed=4 * tok_dev * width, transcendentals=0
        ),
    )(slots, share_all, hidden_cot)


def early_kernel(n, order, *refs):
    pieces = refs[:n]
    wg, wu, gate, up, near, all_g, all_u, held, turned, sems = refs[n:]
    cap, piece = pieces[0].shape
    half = near.shape[1]

    def copies(i):
        start = pl.multiple_of(order[i] * piece, piece)
        return [
            pltpu.make_async_copy(
                w.at[pl.ds(start, piece)], ref.at[pl.ds(i * piece, piece)], sems.at[i, j]
            )
            for j, (w, ref) in enumerate(((wg, all_g), (wu, all_u)))
        ]

    every = [copies(i) for i in range(2 * n)]
    for pair in every:
        for copy in pair:
            copy.start()
    for k in range(n):
        held[:, k * piece : (k + 1) * piece] = pieces[k][...]

    def turn(k, _):
        turned[...] = held[:, pl.ds(pl.multiple_of(k * piece, piece), piece)].T
        start = pl.multiple_of(order[2 * n] * half, half)
        near[k] = turned[pl.ds(start, half), :]
        return 0

    lax.fori_loop(0, n, turn, 0)
    for pair in every[:n]:
        for copy in pair:
            copy.wait()
    block = gate.shape[1] // CHUNKS

    def multiply(c, _):
        here = pl.ds(pl.multiple_of(c * block, block), block)
        gate[:, here] = jnp.dot(held[...], all_g[: n * piece, here], preferred_element_type=F32)
        up[:, here] = jnp.dot(held[...], all_u[: n * piece, here], preferred_element_type=F32)
        return 0

    lax.fori_loop(0, CHUNKS, multiply, 0)
    for pair in every[n:]:
        for copy in pair:
            copy.wait()


def early(order, pieces, w_gate, w_up):
    n = len(pieces)
    cap, piece = pieces[0].shape
    width = w_gate.shape[1]
    hbm = pl.BlockSpec(memory_space=pl.ANY)
    return pl.pallas_call(
        lambda *a: early_kernel(n, *a),
        grid_spec=pltpu.PrefetchScalarGridSpec(
            num_scalar_prefetch=1,
            grid=(1,),
            in_specs=[whole((cap, piece))] * n + [hbm, hbm],
            out_specs=[whole((cap, width))] * 2
            + [whole((n, piece // 2, cap))]
            + [pl.BlockSpec(memory_space=pltpu.VMEM)] * 2,
            scratch_shapes=[
                pltpu.VMEM((cap, n * piece), BF),
                pltpu.VMEM((piece, cap), BF),
                pltpu.SemaphoreType.DMA((2 * n, 2)),
            ],
        ),
        out_shape=[jax.ShapeDtypeStruct((cap, width), F32)] * 2
        + [jax.ShapeDtypeStruct((n, piece // 2, cap), BF)]
        + [pltpu.VMEM((2 * n * piece, width), BF)] * 2,
        compiler_params=pltpu.CompilerParams(vmem_limit_bytes=14 * MIB),
        cost_estimate=pl.CostEstimate(
            flops=4 * cap * n * piece * width,
            bytes_accessed=8 * n * piece * width,
            transcendentals=0,
        ),
    )(order, *pieces, w_gate, w_up)


def forward_kernel(n, soon, late, n_z, info, *refs):
    pieces = refs[:n]
    wg, wu, gate_in, up_in, near_in, cot, share = refs[n : n + 7]
    mine, other = refs[n + 7 : n + 7 + CHUNKS], refs[n + 7 + CHUNKS : n + 7 + 2 * CHUNKS]
    near_left, near_send, route_out, held, turned, route = refs[n + 7 + 2 * CHUNKS :]
    step = pl.program_id(0)
    piece, cap = turned.shape
    half, block = near_left.shape[1], cot.shape[1]

    @pl.when(step == 0)
    def _():
        route[...] = jnp.zeros_like(route)
        for i in range(n):
            held[:, i * piece : (i + 1) * piece] = pieces[i][...]

    here = pl.ds(pl.multiple_of(step * block, block), block)
    gate = gate_in[...] + jnp.dot(held[...], wg[n * piece :, here], preferred_element_type=F32)
    up = up_in[...] + jnp.dot(held[...], wu[n * piece :, here], preferred_element_type=F32)
    sig = jax.nn.sigmoid(gate)
    activated = gate * sig
    hidden = (activated * up).astype(BF).astype(F32)
    cot_wide = cot[...].astype(F32)
    route[...] += jnp.sum(hidden * cot_wide, axis=1, keepdims=True)
    scaled = share[...] * cot_wide
    gate_cot = scaled * up * sig * (1.0 + gate * (1.0 - sig))
    up_cot = scaled * activated
    first = info[3] == 0
    own = jnp.where(first, gate_cot, up_cot).astype(BF)
    rest = jnp.where(first, up_cot, gate_cot).astype(BF)
    for c in range(CHUNKS):

        @pl.when(step == c)
        def _(c=c):
            mine[c][...] = own
            other[c][...] = rest

    @pl.when(step == CHUNKS - 1)
    def _():
        route_out[...] = jnp.broadcast_to(route[...], (cap, 128)).T[:1, :]
        for i, k in enumerate(soon):
            at, there = placed(info, k, n_z)
            near_left[at] = near_in[i]
            near_send[there] = near_in[i]
        for i, k in enumerate(late):
            turned[...] = held[:, i * piece : (i + 1) * piece].T
            start = pl.multiple_of(info[2] * half, half)
            at, there = placed(info, k, n_z)
            near_left[at] = turned[pl.ds(start, half), :]
            near_send[there] = turned[pl.ds(start, half), :]


def forward(info, pieces, soon, late, w_gate, w_up, gate, up, near, cot_rows, share, n_z):
    n = len(pieces)
    cap, piece = pieces[0].shape
    width = w_gate.shape[1]
    block = width // CHUNKS
    cols = pl.BlockSpec((cap, block), lambda j, *_: (0, j))
    near_left = (n_z, piece // 2, cap)
    outs = [((cap, block), BF)] * (2 * CHUNKS) + [(near_left, BF)] * 2 + [((1, cap), F32)]
    held = pl.BlockSpec(memory_space=pltpu.VMEM)
    return pl.pallas_call(
        lambda *a: forward_kernel(n, soon, late, n_z, *a),
        grid_spec=pltpu.PrefetchScalarGridSpec(
            num_scalar_prefetch=1,
            grid=(CHUNKS,),
            in_specs=[whole((cap, piece))] * n
            + [held, held, cols, cols, whole(near.shape), cols, whole((cap, 1))],
            out_specs=[whole(shape) for shape, _ in outs],
            scratch_shapes=[
                pltpu.VMEM((cap, n * piece), BF),
                pltpu.VMEM((piece, cap), BF),
                pltpu.VMEM((cap, 1), F32),
            ],
        ),
        out_shape=[jax.ShapeDtypeStruct(shape, kind) for shape, kind in outs],
        compiler_params=pltpu.CompilerParams(vmem_limit_bytes=20 * MIB),
        cost_estimate=pl.CostEstimate(
            flops=4 * cap * n * piece * width,
            bytes_accessed=16 * cap * width,
            transcendentals=cap * width,
        ),
    )(info, *pieces, w_gate, w_up, gate, up, near, cot_rows, share)


def in_terms(row):
    high = row.astype(BF).astype(F32)
    middle = (row - high).astype(BF).astype(F32)
    low = row - high - middle
    at = lax.broadcasted_iota(jnp.int32, (EXTRA, row.shape[1]), 0)
    terms = jnp.where(at == 0, high, jnp.where(at == 1, middle, jnp.where(at == 2, low, 0.0)))
    return terms.astype(BF)


def row_of(terms):
    return jnp.sum(terms.astype(F32), axis=0, keepdims=True)


def back_kernel(info, *refs):
    mine, other = refs[:CHUNKS], refs[CHUNKS : 2 * CHUNKS]
    route, _, wg, wu, own, first_out, third_out, second_out, gt, ut = refs[2 * CHUNKS :]
    piece = own.shape[1]
    chunk = mine[0].shape[1]
    first = info[3] == 0
    for c in range(CHUNKS):
        a, b = mine[c][...], other[c][...]
        gt[pl.ds(c * chunk, chunk), :] = jnp.where(first, a, b).T
        ut[pl.ds(c * chunk, chunk), :] = jnp.where(first, b, a).T

    targets = [(own, 0), (own, 1), (first_out, 0), (third_out, 0)]
    targets += [(first_out, 1), (third_out, 1), (second_out, 0), (second_out, 1)]

    def block(i, _):
        rows = pl.ds(pl.multiple_of(i * piece, piece), piece)
        out = jnp.dot(wg[rows, :], gt[...], preferred_element_type=F32)
        out += jnp.dot(wu[rows, :], ut[...], preferred_element_type=F32)
        for j, (ref, at) in enumerate(targets):

            @pl.when(i == j)
            def _(ref=ref, at=at):
                ref[at, :piece, :] = out.astype(ref.dtype)

        return 0

    lax.fori_loop(0, len(targets), block, 0)
    terms = in_terms(route[...])
    for ref in (first_out, third_out, second_out):
        for at in range(2):
            ref[at, piece:, :] = terms


def token_parts(info, mine, other, route, waited, weights, piece):
    cap, chunk = mine[0].shape
    depth, width = weights[0].shape
    pair, message = (2, piece, cap), (2, piece + EXTRA, cap)
    return pl.pallas_call(
        back_kernel,
        grid_spec=pltpu.PrefetchScalarGridSpec(
            num_scalar_prefetch=1,
            grid=(1,),
            in_specs=[whole((cap, chunk))] * (2 * CHUNKS)
            + [whole((1, cap)), pl.BlockSpec(memory_space=pl.ANY)]
            + [pl.BlockSpec(memory_space=pltpu.VMEM)] * 2,
            out_specs=[whole(pair)] + [whole(message)] * 3,
            scratch_shapes=[pltpu.VMEM((width, cap), BF), pltpu.VMEM((width, cap), BF)],
        ),
        out_shape=[jax.ShapeDtypeStruct(pair, F32)] + [jax.ShapeDtypeStruct(message, BF)] * 3,
        compiler_params=pltpu.CompilerParams(vmem_limit_bytes=14 * MIB),
        cost_estimate=pl.CostEstimate(
            flops=4 * cap * depth * width, bytes_accessed=4 * depth * width, transcendentals=0
        ),
    )(info, *mine, *other, route, waited, *weights)


def after(x, waited):
    def kernel(value, _, out):
        out[...] = value[...]

    return pl.pallas_call(
        kernel,
        grid=(1,),
        in_specs=[whole(x.shape), pl.BlockSpec(memory_space=pl.ANY)],
        out_specs=whole(x.shape),
        out_shape=jax.ShapeDtypeStruct(x.shape, x.dtype),
        compiler_params=pltpu.CompilerParams(vmem_limit_bytes=4 * MIB),
    )(x, waited)


def combine_kernel(own, route, first, third, second, kept, kept_route, sent):
    piece = own.shape[1]
    rows = [row_of(ref[0, piece:, :]) for ref in (first, third, second)]
    kept_route[...] = (route[...] + rows[0]) + (rows[1] + rows[2])
    for at in range(2):
        total = own[at]
        for ref in (first, third, second):
            total += ref[at, :piece, :].astype(F32)
        if at == 0:
            kept[...] = total
        else:
            sent[:piece, :] = total.astype(BF)
    sent[piece:, :] = in_terms(kept_route[...])


def combine(own, route, parts):
    _, piece, cap = own.shape
    shapes = [((piece, cap), F32), ((1, cap), F32), ((piece + EXTRA, cap), BF)]
    return pl.pallas_call(
        combine_kernel,
        out_shape=[jax.ShapeDtypeStruct(shape, kind) for shape, kind in shapes],
        compiler_params=pltpu.CompilerParams(vmem_limit_bytes=6 * MIB),
        cost_estimate=pl.CostEstimate(
            flops=8 * piece * cap, bytes_accessed=30 * piece * cap, transcendentals=0
        ),
    )(own, route, *parts)


def hop_kernel(has, n_waits, *refs):
    n = len(has)
    parts, refs = refs[:n], refs[n:]
    got, outs = refs[: sum(has)], refs[sum(has) + n_waits :]
    taken = 0
    for i in range(n):
        total = parts[i][0]
        if has[i]:
            total += got[taken][...].astype(F32)
            taken += 1
        outs[i][...] = total.astype(BF)


def hop_sums(base, places, arrived, waited):
    _, rows, cols = base.shape
    got = [a for a in arrived if a is not None]
    n = len(places)
    block = lambda j: pl.BlockSpec((1, rows, cols), lambda i: (j, 0, 0))
    return pl.pallas_call(
        lambda *a: hop_kernel([x is not None for x in arrived], len(waited), *a),
        grid=(1,),
        in_specs=[block(j) for j in places]
        + [whole((rows, cols))] * len(got)
        + [pl.BlockSpec(memory_space=pl.ANY)] * len(waited),
        out_specs=[whole((rows, cols))] * n,
        out_shape=[jax.ShapeDtypeStruct((rows, cols), BF)] * n,
        compiler_params=pltpu.CompilerParams(vmem_limit_bytes=6 * MIB),
        cost_estimate=pl.CostEstimate(
            flops=2 * n * rows * cols, bytes_accessed=8 * n * rows * cols, transcendentals=0
        ),
    )(*[base] * n, *got, *waited)


def far_kernel(n, n_z, info, *refs):
    out, send = refs[-2:]
    for y in range(n // 2):
        for x in range(2):
            at, there = placed(info, y + x * (n // 2), n_z)
            out[at] = refs[y][x]
            send[there] = refs[y][x]


def far_operand(info, arrays, n, n_z):
    rows, cap = arrays[0].shape[1:]
    return pl.pallas_call(
        lambda *a: far_kernel(n, n_z, *a),
        grid_spec=pltpu.PrefetchScalarGridSpec(
            num_scalar_prefetch=1,
            grid=(1,),
            in_specs=[whole(a.shape) for a in arrays],
            out_specs=[whole((n_z, rows, cap))] * 2,
        ),
        out_shape=[jax.ShapeDtypeStruct((n_z, rows, cap), BF)] * 2,
        compiler_params=pltpu.CompilerParams(vmem_limit_bytes=8 * MIB),
        cost_estimate=pl.CostEstimate(
            flops=0, bytes_accessed=4 * n * rows * cap, transcendentals=0
        ),
    )(info, *arrays)


def on_device(tokens, hidden_cot, w_gate, w_up, expert_ids, route_fixed):
    tok_dev, piece = tokens.shape
    width = w_gate.shape[1]
    n_tensor = lax.axis_size("tensor")
    n_dp = lax.axis_size("dp")
    n_z = n_dp // 4
    half = piece // 2
    xlo = n_tensor // 2
    t = lax.axis_index("tensor")
    dp = lax.axis_index("dp")
    z, xh, core = dp // 4, (dp // 2) % 2, dp % 2
    info = jnp.stack([t, z, xh, core]).astype(jnp.int32)
    tie = lax.optimization_barrier

    def over_tensor(x, k):
        return lax.ppermute(x, "tensor", [(i, i ^ k) for i in range(n_tensor)])

    def over_dp(x, k):
        return lax.ppermute(x, "dp", [(i, i ^ k) for i in range(n_dp)])

    def along_z(x, k):
        pairs = [(i, (i + 4 * (k if i % 2 == 0 else -k)) % n_dp) for i in range(n_dp)]
        return lax.ppermute(x, "dp", pairs)

    def over_both(x, k, m):
        n_all = n_dp * n_tensor
        pairs = [(i, i ^ (k * n_tensor + m)) for i in range(n_all)]
        return lax.ppermute(x, ("dp", "tensor"), pairs)

    selected = expert_ids == 0
    flag = jnp.any(selected, axis=1)
    place = jnp.arange(tok_dev, dtype=jnp.int32)
    upto = (place[:, None] <= place[None, :]).astype(BF)
    slot_of = jnp.dot(flag.astype(BF)[None, :], upto, preferred_element_type=F32)[0] - 1.0
    slot_of = jnp.where(flag, slot_of.astype(jnp.int32), -1)
    mask = slot_of[None, :] == jnp.arange(CAP, dtype=jnp.int32)[:, None]
    dispatch = mask.astype(BF)
    share_all = jnp.sum(jnp.where(selected, route_fixed, 0), axis=1).astype(F32) / 65536.0

    hidden_cot = pltpu.with_memory_space_constraint(hidden_cot, pltpu.HBM)
    tokens = pltpu.with_memory_space_constraint(tokens, pltpu.HBM)
    w_gate = pltpu.with_memory_space_constraint(w_gate, pltpu.HBM)
    w_up = pltpu.with_memory_space_constraint(w_up, pltpu.HBM)
    picked, far_piece = dispatch_tokens(info, slot_of[None, :], tokens)
    cot_rows, share = dispatch_cots(slot_of[None, :], share_all[None, :], hidden_cot)
    near = [None] * n_tensor
    near[xlo] = over_tensor(picked, xlo)
    near[1] = over_tensor(picked, 1)
    near[3] = over_tensor(picked, 3)
    far_other = over_both(far_piece, 2, xlo)
    picked, near[1], near[3], near[xlo], cot_rows, share, far_other, far_piece = tie(
        (picked, near[1], near[3], near[xlo], cot_rows, share, far_other, far_piece)
    )
    far_piece = over_dp(far_piece, 2)
    near[0] = picked
    near[xlo + 1] = over_tensor(near[1], xlo)
    near[xlo + 3] = over_tensor(near[3], xlo)
    near[2] = over_tensor(picked, 2)
    near[xlo + 2] = over_tensor(near[xlo], 2)
    soon, late = (0, xlo, 1, 3), (xlo + 1, xlo + 3, 2, xlo + 2)
    order = jnp.stack([t ^ k for k in soon + late] + [xh]).astype(jnp.int32)
    gate, up, near_soon, *weights = early(order, [near[k] for k in soon], w_gate, w_up)
    far_pair = jnp.stack([far_piece, far_other])
    late_near, gate, up, far_pair = tie(([near[k] for k in late], gate, up, far_pair))
    outs = forward(
        info, late_near, soon, late, *weights, gate, up, near_soon, cot_rows, share, n_z
    )
    mine, other = outs[:CHUNKS], outs[CHUNKS : 2 * CHUNKS]
    near_left, near_send, route_part = outs[2 * CHUNKS :]

    def to_partners(c):
        return [mine[c], over_dp(other[c], 1), over_dp(mine[c], 2), over_dp(other[c], 3)]

    cots = [to_partners(0)]
    far = [far_pair] + [over_tensor(far_pair, k) for k in (1, 2, 3)]
    far_left, far_send = far_operand(info, far, n_tensor, n_z)
    far_send, near_send = tie((far_send, near_send))
    far_sib = over_dp(far_send, 1)
    near_sib = over_dp(near_send, 1)
    own_part, *sent = token_parts(info, mine, other, route_part, far_left, weights, piece)

    def product(a, b):
        return jnp.dot(a.reshape(n_z * half, CAP), b, preferred_element_type=F32)

    close = product(near_left, cots[0][0]) + product(near_sib, cots[0][1])
    own_part, sent, mine, other, close = tie((own_part, sent, mine, other, close))
    for c in range(1, CHUNKS):
        mine, other, cots[-1] = tie((mine, other, cots[-1]))
        cots.append(to_partners(c))
    step = width // CHUNKS

    def sums_of(c, close):
        base = tie(close) + product(far_left, cots[c][2])
        base = tie(base + product(far_sib, cots[c][3]))
        return base.reshape(n_z, half, step)

    class Ring:
        def __init__(self, c, base):
            self.base = base
            self.up_hops = n_z // 2 - c % 2
            self.down_hops = n_z - 1 - self.up_hops
            self.rising = self.falling = None

        def hop(self, i, waited):
            places, arrived = [], []
            if i < self.up_hops:
                places.append(self.up_hops - i)
                arrived.append(self.rising)
            if i < self.down_hops:
                places.append((n_z - self.down_hops + i) % n_z)
                arrived.append(self.falling)
            out = hop_sums(self.base, places, arrived, waited)
            if i < self.up_hops:
                self.rising = along_z(out[0], 1)
            if i < self.down_hops:
                self.falling = along_z(out[-1], -1)
            return out[0]

        def finish(self):
            total = self.base[0] + self.rising.astype(F32) + self.falling.astype(F32)
            return total.astype(BF).reshape(2, half // 2, step)

    rings = [Ring(0, sums_of(0, close))]
    waited = rings[0].hop(0, [])
    sums = {1: over_tensor(after(sent[0], waited), 1)}
    for c in range(1, CHUNKS):
        lefts = [after(near_left, waited), near_sib]
        close = product(lefts[0], cots[c][0]) + product(lefts[1], cots[c][1])
        rings.append(Ring(c, sums_of(c, close)))
        waited = rings[c].hop(0, [waited])
    for i in range(1, n_z // 2):
        waited = rings[0].hop(i, [waited])
        if i < 3:
            sums[4 - i] = over_tensor(after(sent[i], waited), 4 - i)
        else:
            parts = [sums[1], sums[3], sums[2]]
            in_hbm = lambda a: pltpu.with_memory_space_constraint(a, pltpu.HBM)
            total, route_total, message = combine(
                in_hbm(own_part), in_hbm(route_part), [in_hbm(a) for a in parts]
            )
        for ring in rings[1:]:
            waited = ring.hop(i, [waited, message if i == 3 else sums[(1, 3)[i - 1]]])
    whole_rows = jnp.concatenate([ring.finish() for ring in rings], axis=2)
    kept = lax.dynamic_index_in_dim(whole_rows, core, 0, keepdims=False)
    swapped = over_dp(lax.dynamic_index_in_dim(whole_rows, 1 - core, 0, keepdims=False), 1)
    gate_grad = jnp.where(core == 0, kept, swapped)
    up_grad = jnp.where(core == 0, swapped, kept)

    message = over_tensor(message, xlo)
    total = total + message[:piece].astype(F32)
    route_total = route_total + row_of(message[piece:])
    token_grad = lax.dot_general(
        dispatch, total.astype(BF), (((0,), (1,)), ((), ())), preferred_element_type=F32
    ).astype(BF)
    route_grad = jnp.sum(jnp.where(mask, route_total[0][:, None], 0.0), axis=0)
    return token_grad, gate_grad, up_grad, route_grad


def solution(mesh):
    return jax.shard_map(
        on_device,
        mesh=mesh,
        in_specs=(
            P("dp", "tensor"),
            P("dp", "tensor"),
            P(None, "tensor"),
            P(None, "tensor"),
            P("dp", None),
            P("dp", None),
        ),
        out_specs=(P("dp", "tensor"), P("dp", "tensor"), P("dp", "tensor"), P("dp")),
        check_vma=False,
    )
```

```python
import jax
import jax.numpy as jnp
from jax import lax
from jax.experimental import pallas as pl
from jax.experimental.pallas import tpu as pltpu
from jax.sharding import PartitionSpec as P

CAP = 256
CHUNKS = 2
EXTRA = 16
BF = jnp.bfloat16
F32 = jnp.float32
MIB = 2**20


def whole(shape):
    return pl.BlockSpec(shape, lambda *_: (0,) * len(shape))


def placed(info, k, n_z):
    ahead = lax.rem((info[0] ^ k) - info[1] + n_z, n_z)
    behind = lax.rem(n_z - ahead, n_z)
    first = info[3] == 0
    return jnp.where(first, ahead, behind), jnp.where(first, behind, ahead)


def dispatch_kernel(info, slots, tokens, picked, far, turned):
    cap, rows = picked.shape[0], far.shape[0]
    tok_dev = slots.shape[1]
    ids = lax.broadcasted_iota(jnp.int32, (cap, tok_dev), 0)
    mask = (slots[...] == ids).astype(F32).astype(BF)
    got = jnp.dot(mask, tokens[...], preferred_element_type=F32)
    picked[...] = got.astype(BF)
    turned[...] = got.T.astype(BF)
    start = pl.multiple_of((1 - info[2]) * rows, rows)
    far[...] = turned[pl.ds(start, rows), :]


def dispatch_tokens(info, slots, tokens):
    tok_dev, piece = tokens.shape
    return pl.pallas_call(
        dispatch_kernel,
        grid_spec=pltpu.PrefetchScalarGridSpec(
            num_scalar_prefetch=1,
            grid=(1,),
            in_specs=[whole((1, tok_dev)), whole((tok_dev, piece))],
            out_specs=[whole((CAP, piece)), whole((piece // 2, CAP))],
            scratch_shapes=[pltpu.VMEM((piece, CAP), BF)],
        ),
        out_shape=[
            jax.ShapeDtypeStruct((CAP, piece), BF),
            jax.ShapeDtypeStruct((piece // 2, CAP), BF),
        ],
        compiler_params=pltpu.CompilerParams(vmem_limit_bytes=8 * MIB),
        cost_estimate=pl.CostEstimate(
            flops=2 * CAP * tok_dev * piece, bytes_accessed=4 * tok_dev * piece, transcendentals=0
        ),
    )(info, slots, tokens)


def cot_kernel(slots, share_all, cot, rows, share):
    cap, tok_dev = rows.shape[0], slots.shape[1]
    mask = slots[...] == lax.broadcasted_iota(jnp.int32, (cap, tok_dev), 0)
    hot = mask.astype(F32).astype(BF)
    rows[...] = jnp.dot(hot, cot[...], preferred_element_type=F32).astype(BF)
    share[...] = jnp.sum(jnp.where(mask, share_all[...], 0.0), axis=1, keepdims=True)


def dispatch_cots(slots, share_all, hidden_cot):
    tok_dev, width = hidden_cot.shape
    return pl.pallas_call(
        cot_kernel,
        out_shape=[
            jax.ShapeDtypeStruct((CAP, width), BF),
            jax.ShapeDtypeStruct((CAP, 1), F32),
        ],
        compiler_params=pltpu.CompilerParams(vmem_limit_bytes=8 * MIB),
        cost_estimate=pl.CostEstimate(
            flops=2 * CAP * tok_dev * width, bytes_accessed=4 * tok_dev * width, transcendentals=0
        ),
    )(slots, share_all, hidden_cot)


def early_kernel(n, order, *refs):
    pieces = refs[:n]
    wg, wu, gate, up, near, all_g, all_u, held, turned, sems = refs[n:]
    cap, piece = pieces[0].shape
    half = near.shape[1]

    def copies(i):
        start = pl.multiple_of(order[i] * piece, piece)
        return [
            pltpu.make_async_copy(
                w.at[pl.ds(start, piece)], ref.at[pl.ds(i * piece, piece)], sems.at[i, j]
            )
            for j, (w, ref) in enumerate(((wg, all_g), (wu, all_u)))
        ]

    every = [copies(i) for i in range(2 * n)]
    for pair in every:
        for copy in pair:
            copy.start()
    for k in range(n):
        held[:, k * piece : (k + 1) * piece] = pieces[k][...]

    def turn(k, _):
        turned[...] = held[:, pl.ds(pl.multiple_of(k * piece, piece), piece)].T
        start = pl.multiple_of(order[2 * n] * half, half)
        near[k] = turned[pl.ds(start, half), :]
        return 0

    lax.fori_loop(0, n, turn, 0)
    for pair in every[:n]:
        for copy in pair:
            copy.wait()
    block = gate.shape[1] // CHUNKS

    def multiply(c, _):
        here = pl.ds(pl.multiple_of(c * block, block), block)
        gate[:, here] = jnp.dot(held[...], all_g[: n * piece, here], preferred_element_type=F32)
        up[:, here] = jnp.dot(held[...], all_u[: n * piece, here], preferred_element_type=F32)
        return 0

    lax.fori_loop(0, CHUNKS, multiply, 0)
    for pair in every[n:]:
        for copy in pair:
            copy.wait()


def early(order, pieces, w_gate, w_up):
    n = len(pieces)
    cap, piece = pieces[0].shape
    width = w_gate.shape[1]
    hbm = pl.BlockSpec(memory_space=pl.ANY)
    return pl.pallas_call(
        lambda *a: early_kernel(n, *a),
        grid_spec=pltpu.PrefetchScalarGridSpec(
            num_scalar_prefetch=1,
            grid=(1,),
            in_specs=[whole((cap, piece))] * n + [hbm, hbm],
            out_specs=[whole((cap, width))] * 2
            + [whole((n, piece // 2, cap))]
            + [pl.BlockSpec(memory_space=pltpu.VMEM)] * 2,
            scratch_shapes=[
                pltpu.VMEM((cap, n * piece), BF),
                pltpu.VMEM((piece, cap), BF),
                pltpu.SemaphoreType.DMA((2 * n, 2)),
            ],
        ),
        out_shape=[jax.ShapeDtypeStruct((cap, width), F32)] * 2
        + [jax.ShapeDtypeStruct((n, piece // 2, cap), BF)]
        + [pltpu.VMEM((2 * n * piece, width), BF)] * 2,
        compiler_params=pltpu.CompilerParams(vmem_limit_bytes=14 * MIB),
        cost_estimate=pl.CostEstimate(
            flops=4 * cap * n * piece * width,
            bytes_accessed=8 * n * piece * width,
            transcendentals=0,
        ),
    )(order, *pieces, w_gate, w_up)


def forward_kernel(n, soon, late, n_z, info, *refs):
    pieces = refs[:n]
    wg, wu, gate_in, up_in, near_in, cot, share = refs[n : n + 7]
    mine, other = refs[n + 7 : n + 7 + CHUNKS], refs[n + 7 + CHUNKS : n + 7 + 2 * CHUNKS]
    near_left, near_send, route_out, held, turned, route = refs[n + 7 + 2 * CHUNKS :]
    step = pl.program_id(0)
    piece, cap = turned.shape
    half, block = near_left.shape[1], cot.shape[1]

    @pl.when(step == 0)
    def _():
        route[...] = jnp.zeros_like(route)
        for i in range(n):
            held[:, i * piece : (i + 1) * piece] = pieces[i][...]

    here = pl.ds(pl.multiple_of(step * block, block), block)
    gate = gate_in[...] + jnp.dot(held[...], wg[n * piece :, here], preferred_element_type=F32)
    up = up_in[...] + jnp.dot(held[...], wu[n * piece :, here], preferred_element_type=F32)
    sig = jax.nn.sigmoid(gate)
    activated = gate * sig
    hidden = (activated * up).astype(BF).astype(F32)
    cot_wide = cot[...].astype(F32)
    route[...] += jnp.sum(hidden * cot_wide, axis=1, keepdims=True)
    scaled = share[...] * cot_wide
    gate_cot = scaled * up * sig * (1.0 + gate * (1.0 - sig))
    up_cot = scaled * activated
    first = info[3] == 0
    own = jnp.where(first, gate_cot, up_cot).astype(BF)
    rest = jnp.where(first, up_cot, gate_cot).astype(BF)
    for c in range(CHUNKS):

        @pl.when(step == c)
        def _(c=c):
            mine[c][...] = own
            other[c][...] = rest

    @pl.when(step == CHUNKS - 1)
    def _():
        route_out[...] = jnp.broadcast_to(route[...], (cap, 128)).T[:1, :]
        for i, k in enumerate(soon):
            at, there = placed(info, k, n_z)
            near_left[at] = near_in[i]
            near_send[there] = near_in[i]
        for i, k in enumerate(late):
            turned[...] = held[:, i * piece : (i + 1) * piece].T
            start = pl.multiple_of(info[2] * half, half)
            at, there = placed(info, k, n_z)
            near_left[at] = turned[pl.ds(start, half), :]
            near_send[there] = turned[pl.ds(start, half), :]


def forward(info, pieces, soon, late, w_gate, w_up, gate, up, near, cot_rows, share, n_z):
    n = len(pieces)
    cap, piece = pieces[0].shape
    width = w_gate.shape[1]
    block = width // CHUNKS
    cols = pl.BlockSpec((cap, block), lambda j, *_: (0, j))
    near_left = (n_z, piece // 2, cap)
    outs = [((cap, block), BF)] * (2 * CHUNKS) + [(near_left, BF)] * 2 + [((1, cap), F32)]
    held = pl.BlockSpec(memory_space=pltpu.VMEM)
    return pl.pallas_call(
        lambda *a: forward_kernel(n, soon, late, n_z, *a),
        grid_spec=pltpu.PrefetchScalarGridSpec(
            num_scalar_prefetch=1,
            grid=(CHUNKS,),
            in_specs=[whole((cap, piece))] * n
            + [held, held, cols, cols, whole(near.shape), cols, whole((cap, 1))],
            out_specs=[whole(shape) for shape, _ in outs],
            scratch_shapes=[
                pltpu.VMEM((cap, n * piece), BF),
                pltpu.VMEM((piece, cap), BF),
                pltpu.VMEM((cap, 1), F32),
            ],
        ),
        out_shape=[jax.ShapeDtypeStruct(shape, kind) for shape, kind in outs],
        compiler_params=pltpu.CompilerParams(vmem_limit_bytes=20 * MIB),
        cost_estimate=pl.CostEstimate(
            flops=4 * cap * n * piece * width,
            bytes_accessed=16 * cap * width,
            transcendentals=cap * width,
        ),
    )(info, *pieces, w_gate, w_up, gate, up, near, cot_rows, share)


def in_terms(row):
    high = row.astype(BF).astype(F32)
    middle = (row - high).astype(BF).astype(F32)
    low = row - high - middle
    at = lax.broadcasted_iota(jnp.int32, (EXTRA, row.shape[1]), 0)
    terms = jnp.where(at == 0, high, jnp.where(at == 1, middle, jnp.where(at == 2, low, 0.0)))
    return terms.astype(BF)


def row_of(terms):
    return jnp.sum(terms.astype(F32), axis=0, keepdims=True)


def back_kernel(info, *refs):
    mine, other = refs[:CHUNKS], refs[CHUNKS : 2 * CHUNKS]
    route, _, wg, wu, own, first_out, third_out, second_out, gt, ut = refs[2 * CHUNKS :]
    piece = own.shape[1]
    chunk = mine[0].shape[1]
    first = info[3] == 0
    for c in range(CHUNKS):
        a, b = mine[c][...], other[c][...]
        gt[pl.ds(c * chunk, chunk), :] = jnp.where(first, a, b).T
        ut[pl.ds(c * chunk, chunk), :] = jnp.where(first, b, a).T

    targets = [(own, 0), (own, 1), (first_out, 0), (third_out, 0)]
    targets += [(first_out, 1), (third_out, 1), (second_out, 0), (second_out, 1)]

    def block(i, _):
        rows = pl.ds(pl.multiple_of(i * piece, piece), piece)
        out = jnp.dot(wg[rows, :], gt[...], preferred_element_type=F32)
        out += jnp.dot(wu[rows, :], ut[...], preferred_element_type=F32)
        for j, (ref, at) in enumerate(targets):

            @pl.when(i == j)
            def _(ref=ref, at=at):
                ref[at, :piece, :] = out.astype(ref.dtype)

        return 0

    lax.fori_loop(0, len(targets), block, 0)
    terms = in_terms(route[...])
    for ref in (first_out, third_out, second_out):
        for at in range(2):
            ref[at, piece:, :] = terms


def token_parts(info, mine, other, route, waited, weights, piece):
    cap, chunk = mine[0].shape
    depth, width = weights[0].shape
    pair, message = (2, piece, cap), (2, piece + EXTRA, cap)
    return pl.pallas_call(
        back_kernel,
        grid_spec=pltpu.PrefetchScalarGridSpec(
            num_scalar_prefetch=1,
            grid=(1,),
            in_specs=[whole((cap, chunk))] * (2 * CHUNKS)
            + [whole((1, cap)), pl.BlockSpec(memory_space=pl.ANY)]
            + [pl.BlockSpec(memory_space=pltpu.VMEM)] * 2,
            out_specs=[whole(pair)] + [whole(message)] * 3,
            scratch_shapes=[pltpu.VMEM((width, cap), BF), pltpu.VMEM((width, cap), BF)],
        ),
        out_shape=[jax.ShapeDtypeStruct(pair, F32)] + [jax.ShapeDtypeStruct(message, BF)] * 3,
        compiler_params=pltpu.CompilerParams(vmem_limit_bytes=14 * MIB),
        cost_estimate=pl.CostEstimate(
            flops=4 * cap * depth * width, bytes_accessed=4 * depth * width, transcendentals=0
        ),
    )(info, *mine, *other, route, waited, *weights)


def after(x, waited):
    def kernel(value, _, out):
        out[...] = value[...]

    return pl.pallas_call(
        kernel,
        grid=(1,),
        in_specs=[whole(x.shape), pl.BlockSpec(memory_space=pl.ANY)],
        out_specs=whole(x.shape),
        out_shape=jax.ShapeDtypeStruct(x.shape, x.dtype),
        compiler_params=pltpu.CompilerParams(vmem_limit_bytes=4 * MIB),
    )(x, waited)


def combine_kernel(own, route, first, third, second, kept, kept_route, sent):
    piece = own.shape[1]
    rows = [row_of(ref[0, piece:, :]) for ref in (first, third, second)]
    kept_route[...] = (route[...] + rows[0]) + (rows[1] + rows[2])
    for at in range(2):
        total = own[at]
        for ref in (first, third, second):
            total += ref[at, :piece, :].astype(F32)
        if at == 0:
            kept[...] = total
        else:
            sent[:piece, :] = total.astype(BF)
    sent[piece:, :] = in_terms(kept_route[...])


def combine(own, route, parts):
    _, piece, cap = own.shape
    shapes = [((piece, cap), F32), ((1, cap), F32), ((piece + EXTRA, cap), BF)]
    return pl.pallas_call(
        combine_kernel,
        out_shape=[jax.ShapeDtypeStruct(shape, kind) for shape, kind in shapes],
        compiler_params=pltpu.CompilerParams(vmem_limit_bytes=6 * MIB),
        cost_estimate=pl.CostEstimate(
            flops=8 * piece * cap, bytes_accessed=30 * piece * cap, transcendentals=0
        ),
    )(own, route, *parts)


def hop_kernel(has, n_waits, *refs):
    n = len(has)
    parts, refs = refs[:n], refs[n:]
    got, outs = refs[: sum(has)], refs[sum(has) + n_waits :]
    taken = 0
    for i in range(n):
        total = parts[i][0]
        if has[i]:
            total += got[taken][...].astype(F32)
            taken += 1
        outs[i][...] = total.astype(BF)


def hop_sums(base, places, arrived, waited):
    _, rows, cols = base.shape
    got = [a for a in arrived if a is not None]
    n = len(places)
    block = lambda j: pl.BlockSpec((1, rows, cols), lambda i: (j, 0, 0))
    return pl.pallas_call(
        lambda *a: hop_kernel([x is not None for x in arrived], len(waited), *a),
        grid=(1,),
        in_specs=[block(j) for j in places]
        + [whole((rows, cols))] * len(got)
        + [pl.BlockSpec(memory_space=pl.ANY)] * len(waited),
        out_specs=[whole((rows, cols))] * n,
        out_shape=[jax.ShapeDtypeStruct((rows, cols), BF)] * n,
        compiler_params=pltpu.CompilerParams(vmem_limit_bytes=6 * MIB),
        cost_estimate=pl.CostEstimate(
            flops=2 * n * rows * cols, bytes_accessed=8 * n * rows * cols, transcendentals=0
        ),
    )(*[base] * n, *got, *waited)


def far_kernel(n, n_z, info, *refs):
    out, send = refs[-2:]
    for y in range(n // 2):
        for x in range(2):
            at, there = placed(info, y + x * (n // 2), n_z)
            out[at] = refs[y][x]
            send[there] = refs[y][x]


def far_operand(info, arrays, n, n_z):
    rows, cap = arrays[0].shape[1:]
    return pl.pallas_call(
        lambda *a: far_kernel(n, n_z, *a),
        grid_spec=pltpu.PrefetchScalarGridSpec(
            num_scalar_prefetch=1,
            grid=(1,),
            in_specs=[whole(a.shape) for a in arrays],
            out_specs=[whole((n_z, rows, cap))] * 2,
        ),
        out_shape=[jax.ShapeDtypeStruct((n_z, rows, cap), BF)] * 2,
        compiler_params=pltpu.CompilerParams(vmem_limit_bytes=8 * MIB),
        cost_estimate=pl.CostEstimate(
            flops=0, bytes_accessed=4 * n * rows * cap, transcendentals=0
        ),
    )(info, *arrays)


def on_device(tokens, hidden_cot, w_gate, w_up, expert_ids, route_fixed):
    tok_dev, piece = tokens.shape
    width = w_gate.shape[1]
    n_tensor = lax.axis_size("tensor")
    n_dp = lax.axis_size("dp")
    n_z = n_dp // 4
    half = piece // 2
    xlo = n_tensor // 2
    t = lax.axis_index("tensor")
    dp = lax.axis_index("dp")
    z, xh, core = dp // 4, (dp // 2) % 2, dp % 2
    info = jnp.stack([t, z, xh, core]).astype(jnp.int32)
    tie = lax.optimization_barrier

    def over_tensor(x, k):
        return lax.ppermute(x, "tensor", [(i, i ^ k) for i in range(n_tensor)])

    def over_dp(x, k):
        return lax.ppermute(x, "dp", [(i, i ^ k) for i in range(n_dp)])

    def along_z(x, k):
        pairs = [(i, (i + 4 * (k if i % 2 == 0 else -k)) % n_dp) for i in range(n_dp)]
        return lax.ppermute(x, "dp", pairs)

    def over_both(x, k, m):
        n_all = n_dp * n_tensor
        pairs = [(i, i ^ (k * n_tensor + m)) for i in range(n_all)]
        return lax.ppermute(x, ("dp", "tensor"), pairs)

    selected = expert_ids == 0
    flag = jnp.any(selected, axis=1)
    place = jnp.arange(tok_dev, dtype=jnp.int32)
    upto = (place[:, None] <= place[None, :]).astype(BF)
    slot_of = jnp.dot(flag.astype(BF)[None, :], upto, preferred_element_type=F32)[0] - 1.0
    slot_of = jnp.where(flag, slot_of.astype(jnp.int32), -1)
    mask = slot_of[None, :] == jnp.arange(CAP, dtype=jnp.int32)[:, None]
    dispatch = mask.astype(BF)
    share_all = jnp.sum(jnp.where(selected, route_fixed, 0), axis=1).astype(F32) / 65536.0

    hidden_cot = pltpu.with_memory_space_constraint(hidden_cot, pltpu.HBM)
    tokens = pltpu.with_memory_space_constraint(tokens, pltpu.HBM)
    w_gate = pltpu.with_memory_space_constraint(w_gate, pltpu.HBM)
    w_up = pltpu.with_memory_space_constraint(w_up, pltpu.HBM)
    picked, far_piece = dispatch_tokens(info, slot_of[None, :], tokens)
    cot_rows, share = dispatch_cots(slot_of[None, :], share_all[None, :], hidden_cot)
    near = [None] * n_tensor
    near[xlo] = over_tensor(picked, xlo)
    near[1] = over_tensor(picked, 1)
    near[3] = over_tensor(picked, 3)
    far_other = over_both(far_piece, 2, xlo)
    picked, near[1], near[3], near[xlo], cot_rows, share, far_other, far_piece = tie(
        (picked, near[1], near[3], near[xlo], cot_rows, share, far_other, far_piece)
    )
    far_piece = over_dp(far_piece, 2)
    near[0] = picked
    near[xlo + 1] = over_tensor(near[1], xlo)
    near[xlo + 3] = over_tensor(near[3], xlo)
    near[2] = over_tensor(picked, 2)
    near[xlo + 2] = over_tensor(near[xlo], 2)
    soon, late = (0, xlo, 1, 3), (xlo + 1, xlo + 3, 2, xlo + 2)
    order = jnp.stack([t ^ k for k in soon + late] + [xh]).astype(jnp.int32)
    gate, up, near_soon, *weights = early(order, [near[k] for k in soon], w_gate, w_up)
    far_pair = jnp.stack([far_piece, far_other])
    late_near, gate, up, far_pair = tie(([near[k] for k in late], gate, up, far_pair))
    outs = forward(
        info, late_near, soon, late, *weights, gate, up, near_soon, cot_rows, share, n_z
    )
    mine, other = outs[:CHUNKS], outs[CHUNKS : 2 * CHUNKS]
    near_left, near_send, route_part = outs[2 * CHUNKS :]

    def to_partners(c):
        return [mine[c], over_dp(other[c], 1), over_dp(mine[c], 2), over_dp(other[c], 3)]

    cots = [to_partners(0)]
    near_sib = over_dp(near_send, 1)
    far_pair, near_sib = tie((far_pair, near_sib))
    far = [far_pair] + [over_tensor(far_pair, k) for k in (1, 2, 3)]
    own_part, *sent = token_parts(info, mine, other, route_part, far_pair, weights, piece)

    def product(a, b):
        return jnp.dot(a.reshape(n_z * half, CAP), b, preferred_element_type=F32)

    close = product(near_left, cots[0][0]) + product(near_sib, cots[0][1])
    far, own_part, sent, mine, other, close = tie((far, own_part, sent, mine, other, close))
    far_left, far_send = far_operand(info, far, n_tensor, n_z)
    far_sib = over_dp(far_send, 1)
    for c in range(1, CHUNKS):
        mine, other, cots[-1] = tie((mine, other, cots[-1]))
        cots.append(to_partners(c))
    step = width // CHUNKS

    def sums_of(c, close):
        base = tie(close) + product(far_left, cots[c][2])
        base = tie(base + product(far_sib, cots[c][3]))
        return base.reshape(n_z, half, step)

    class Ring:
        def __init__(self, c, base):
            self.base = base
            self.up_hops = n_z // 2 - c % 2
            self.down_hops = n_z - 1 - self.up_hops
            self.rising = self.falling = None

        def hop(self, i, waited):
            places, arrived = [], []
            if i < self.up_hops:
                places.append(self.up_hops - i)
                arrived.append(self.rising)
            if i < self.down_hops:
                places.append((n_z - self.down_hops + i) % n_z)
                arrived.append(self.falling)
            out = hop_sums(self.base, places, arrived, waited)
            if i < self.up_hops:
                self.rising = along_z(out[0], 1)
            if i < self.down_hops:
                self.falling = along_z(out[-1], -1)
            return out[0]

        def finish(self):
            total = self.base[0] + self.rising.astype(F32) + self.falling.astype(F32)
            return total.astype(BF).reshape(2, half // 2, step)

    rings = [Ring(0, sums_of(0, close))]
    waited = rings[0].hop(0, [])
    sums = {1: over_tensor(after(sent[0], waited), 1)}
    for c in range(1, CHUNKS):
        lefts = [after(near_left, waited), near_sib]
        close = product(lefts[0], cots[c][0]) + product(lefts[1], cots[c][1])
        rings.append(Ring(c, sums_of(c, close)))
        waited = rings[c].hop(0, [waited])
    for i in range(1, n_z // 2):
        waited = rings[0].hop(i, [waited])
        if i == 1:
            sums[3] = over_tensor(after(sent[1], waited), 3)
            sums[2] = over_tensor(after(sent[2], waited), 2)
        if i == 3:
            parts = [sums[1], sums[3], sums[2]]
            in_hbm = lambda a: pltpu.with_memory_space_constraint(a, pltpu.HBM)
            total, route_total, message = combine(
                in_hbm(own_part), in_hbm(route_part), [in_hbm(a) for a in parts]
            )
        for ring in rings[1:]:
            needed = ([sums[1]], [sums[3], sums[2]], [message] if i == 3 else [])[i - 1]
            waited = ring.hop(i, [waited, *needed])
    whole_rows = jnp.concatenate([ring.finish() for ring in rings], axis=2)
    kept = lax.dynamic_index_in_dim(whole_rows, core, 0, keepdims=False)
    swapped = over_dp(lax.dynamic_index_in_dim(whole_rows, 1 - core, 0, keepdims=False), 1)
    gate_grad = jnp.where(core == 0, kept, swapped)
    up_grad = jnp.where(core == 0, swapped, kept)

    message = over_tensor(message, xlo)
    total = total + message[:piece].astype(F32)
    route_total = route_total + row_of(message[piece:])
    token_grad = lax.dot_general(
        dispatch, total.astype(BF), (((0,), (1,)), ((), ())), preferred_element_type=F32
    ).astype(BF)
    route_grad = jnp.sum(jnp.where(mask, route_total[0][:, None], 0.0), axis=0)
    return token_grad, gate_grad, up_grad, route_grad


def solution(mesh):
    return jax.shard_map(
        on_device,
        mesh=mesh,
        in_specs=(
            P("dp", "tensor"),
            P("dp", "tensor"),
            P(None, "tensor"),
            P(None, "tensor"),
            P("dp", None),
            P("dp", None),
        ),
        out_specs=(P("dp", "tensor"), P("dp", "tensor"), P("dp", "tensor"), P("dp")),
        check_vma=False,
    )
```

```python
import jax
import jax.numpy as jnp
from jax import lax
from jax.experimental import pallas as pl
from jax.experimental.pallas import tpu as pltpu
from jax.sharding import PartitionSpec as P

CAP = 256
CHUNKS = 2
EXTRA = 16
BF = jnp.bfloat16
F32 = jnp.float32
MIB = 2**20


def whole(shape):
    return pl.BlockSpec(shape, lambda *_: (0,) * len(shape))


def placed(info, k, n_z):
    ahead = lax.rem((info[0] ^ k) - info[1] + n_z, n_z)
    behind = lax.rem(n_z - ahead, n_z)
    first = info[3] == 0
    return jnp.where(first, ahead, behind), jnp.where(first, behind, ahead)


def dispatch_kernel(info, slots, tokens, picked, far, turned):
    cap, rows = picked.shape[0], far.shape[0]
    tok_dev = slots.shape[1]
    ids = lax.broadcasted_iota(jnp.int32, (cap, tok_dev), 0)
    mask = (slots[...] == ids).astype(F32).astype(BF)
    got = jnp.dot(mask, tokens[...], preferred_element_type=F32)
    picked[...] = got.astype(BF)
    turned[...] = got.T.astype(BF)
    start = pl.multiple_of((1 - info[2]) * rows, rows)
    far[...] = turned[pl.ds(start, rows), :]


def dispatch_tokens(info, slots, tokens):
    tok_dev, piece = tokens.shape
    return pl.pallas_call(
        dispatch_kernel,
        grid_spec=pltpu.PrefetchScalarGridSpec(
            num_scalar_prefetch=1,
            grid=(1,),
            in_specs=[whole((1, tok_dev)), whole((tok_dev, piece))],
            out_specs=[whole((CAP, piece)), whole((piece // 2, CAP))],
            scratch_shapes=[pltpu.VMEM((piece, CAP), BF)],
        ),
        out_shape=[
            jax.ShapeDtypeStruct((CAP, piece), BF),
            jax.ShapeDtypeStruct((piece // 2, CAP), BF),
        ],
        compiler_params=pltpu.CompilerParams(vmem_limit_bytes=8 * MIB),
        cost_estimate=pl.CostEstimate(
            flops=2 * CAP * tok_dev * piece, bytes_accessed=4 * tok_dev * piece, transcendentals=0
        ),
    )(info, slots, tokens)


def cot_kernel(slots, share_all, cot, rows, share):
    cap, tok_dev = rows.shape[0], slots.shape[1]
    mask = slots[...] == lax.broadcasted_iota(jnp.int32, (cap, tok_dev), 0)
    hot = mask.astype(F32).astype(BF)
    rows[...] = jnp.dot(hot, cot[...], preferred_element_type=F32).astype(BF)
    share[...] = jnp.sum(jnp.where(mask, share_all[...], 0.0), axis=1, keepdims=True)


def dispatch_cots(slots, share_all, hidden_cot):
    tok_dev, width = hidden_cot.shape
    return pl.pallas_call(
        cot_kernel,
        out_shape=[
            jax.ShapeDtypeStruct((CAP, width), BF),
            jax.ShapeDtypeStruct((CAP, 1), F32),
        ],
        compiler_params=pltpu.CompilerParams(vmem_limit_bytes=8 * MIB),
        cost_estimate=pl.CostEstimate(
            flops=2 * CAP * tok_dev * width, bytes_accessed=4 * tok_dev * width, transcendentals=0
        ),
    )(slots, share_all, hidden_cot)


def early_kernel(n, order, *refs):
    pieces = refs[:n]
    wg, wu, gate, up, near, all_g, all_u, held, turned, sems = refs[n:]
    cap, piece = pieces[0].shape
    half = near.shape[1]

    def copies(i):
        start = pl.multiple_of(order[i] * piece, piece)
        return [
            pltpu.make_async_copy(
                w.at[pl.ds(start, piece)], ref.at[pl.ds(i * piece, piece)], sems.at[i, j]
            )
            for j, (w, ref) in enumerate(((wg, all_g), (wu, all_u)))
        ]

    every = [copies(i) for i in range(2 * n)]
    for pair in every:
        for copy in pair:
            copy.start()
    for k in range(n):
        held[:, k * piece : (k + 1) * piece] = pieces[k][...]

    def turn(k, _):
        turned[...] = held[:, pl.ds(pl.multiple_of(k * piece, piece), piece)].T
        start = pl.multiple_of(order[2 * n] * half, half)
        near[k] = turned[pl.ds(start, half), :]
        return 0

    lax.fori_loop(0, n, turn, 0)
    for pair in every[:n]:
        for copy in pair:
            copy.wait()
    block = gate.shape[1] // CHUNKS

    def multiply(c, _):
        here = pl.ds(pl.multiple_of(c * block, block), block)
        gate[:, here] = jnp.dot(held[...], all_g[: n * piece, here], preferred_element_type=F32)
        up[:, here] = jnp.dot(held[...], all_u[: n * piece, here], preferred_element_type=F32)
        return 0

    lax.fori_loop(0, CHUNKS, multiply, 0)
    for pair in every[n:]:
        for copy in pair:
            copy.wait()


def early(order, pieces, w_gate, w_up):
    n = len(pieces)
    cap, piece = pieces[0].shape
    width = w_gate.shape[1]
    hbm = pl.BlockSpec(memory_space=pl.ANY)
    return pl.pallas_call(
        lambda *a: early_kernel(n, *a),
        grid_spec=pltpu.PrefetchScalarGridSpec(
            num_scalar_prefetch=1,
            grid=(1,),
            in_specs=[whole((cap, piece))] * n + [hbm, hbm],
            out_specs=[whole((cap, width))] * 2
            + [whole((n, piece // 2, cap))]
            + [pl.BlockSpec(memory_space=pltpu.VMEM)] * 2,
            scratch_shapes=[
                pltpu.VMEM((cap, n * piece), BF),
                pltpu.VMEM((piece, cap), BF),
                pltpu.SemaphoreType.DMA((2 * n, 2)),
            ],
        ),
        out_shape=[jax.ShapeDtypeStruct((cap, width), F32)] * 2
        + [jax.ShapeDtypeStruct((n, piece // 2, cap), BF)]
        + [pltpu.VMEM((2 * n * piece, width), BF)] * 2,
        compiler_params=pltpu.CompilerParams(vmem_limit_bytes=14 * MIB),
        cost_estimate=pl.CostEstimate(
            flops=4 * cap * n * piece * width,
            bytes_accessed=8 * n * piece * width,
            transcendentals=0,
        ),
    )(order, *pieces, w_gate, w_up)


def forward_kernel(n, soon, late, n_z, info, *refs):
    pieces = refs[:n]
    wg, wu, gate_in, up_in, near_in, cot, share = refs[n : n + 7]
    mine, other = refs[n + 7 : n + 7 + CHUNKS], refs[n + 7 + CHUNKS : n + 7 + 2 * CHUNKS]
    near_left, near_send, route_out, held, turned, route = refs[n + 7 + 2 * CHUNKS :]
    step = pl.program_id(0)
    piece, cap = turned.shape
    half, block = near_left.shape[1], cot.shape[1]

    @pl.when(step == 0)
    def _():
        route[...] = jnp.zeros_like(route)
        for i in range(n):
            held[:, i * piece : (i + 1) * piece] = pieces[i][...]

    here = pl.ds(pl.multiple_of(step * block, block), block)
    gate = gate_in[...] + jnp.dot(held[...], wg[n * piece :, here], preferred_element_type=F32)
    up = up_in[...] + jnp.dot(held[...], wu[n * piece :, here], preferred_element_type=F32)
    sig = jax.nn.sigmoid(gate)
    activated = gate * sig
    hidden = (activated * up).astype(BF).astype(F32)
    cot_wide = cot[...].astype(F32)
    route[...] += jnp.sum(hidden * cot_wide, axis=1, keepdims=True)
    scaled = share[...] * cot_wide
    gate_cot = scaled * up * sig * (1.0 + gate * (1.0 - sig))
    up_cot = scaled * activated
    first = info[3] == 0
    own = jnp.where(first, gate_cot, up_cot).astype(BF)
    rest = jnp.where(first, up_cot, gate_cot).astype(BF)
    for c in range(CHUNKS):

        @pl.when(step == c)
        def _(c=c):
            mine[c][...] = own
            other[c][...] = rest

    @pl.when(step == CHUNKS - 1)
    def _():
        route_out[...] = jnp.broadcast_to(route[...], (cap, 128)).T[:1, :]
        for i, k in enumerate(soon):
            at, there = placed(info, k, n_z)
            near_left[at] = near_in[i]
            near_send[there] = near_in[i]
        for i, k in enumerate(late):
            turned[...] = held[:, i * piece : (i + 1) * piece].T
            start = pl.multiple_of(info[2] * half, half)
            at, there = placed(info, k, n_z)
            near_left[at] = turned[pl.ds(start, half), :]
            near_send[there] = turned[pl.ds(start, half), :]


def forward(info, pieces, soon, late, w_gate, w_up, gate, up, near, cot_rows, share, n_z):
    n = len(pieces)
    cap, piece = pieces[0].shape
    width = w_gate.shape[1]
    block = width // CHUNKS
    cols = pl.BlockSpec((cap, block), lambda j, *_: (0, j))
    near_left = (n_z, piece // 2, cap)
    outs = [((cap, block), BF)] * (2 * CHUNKS) + [(near_left, BF)] * 2 + [((1, cap), F32)]
    held = pl.BlockSpec(memory_space=pltpu.VMEM)
    return pl.pallas_call(
        lambda *a: forward_kernel(n, soon, late, n_z, *a),
        grid_spec=pltpu.PrefetchScalarGridSpec(
            num_scalar_prefetch=1,
            grid=(CHUNKS,),
            in_specs=[whole((cap, piece))] * n
            + [held, held, cols, cols, whole(near.shape), cols, whole((cap, 1))],
            out_specs=[whole(shape) for shape, _ in outs],
            scratch_shapes=[
                pltpu.VMEM((cap, n * piece), BF),
                pltpu.VMEM((piece, cap), BF),
                pltpu.VMEM((cap, 1), F32),
            ],
        ),
        out_shape=[jax.ShapeDtypeStruct(shape, kind) for shape, kind in outs],
        compiler_params=pltpu.CompilerParams(vmem_limit_bytes=20 * MIB),
        cost_estimate=pl.CostEstimate(
            flops=4 * cap * n * piece * width,
            bytes_accessed=16 * cap * width,
            transcendentals=cap * width,
        ),
    )(info, *pieces, w_gate, w_up, gate, up, near, cot_rows, share)


def in_terms(row):
    high = row.astype(BF).astype(F32)
    middle = (row - high).astype(BF).astype(F32)
    low = row - high - middle
    at = lax.broadcasted_iota(jnp.int32, (EXTRA, row.shape[1]), 0)
    terms = jnp.where(at == 0, high, jnp.where(at == 1, middle, jnp.where(at == 2, low, 0.0)))
    return terms.astype(BF)


def row_of(terms):
    return jnp.sum(terms.astype(F32), axis=0, keepdims=True)


def back_kernel(info, *refs):
    mine, other = refs[:CHUNKS], refs[CHUNKS : 2 * CHUNKS]
    route, _, wg, wu, own, first_out, third_out, second_out, gt, ut = refs[2 * CHUNKS :]
    piece = own.shape[1]
    chunk = mine[0].shape[1]
    first = info[3] == 0
    for c in range(CHUNKS):
        a, b = mine[c][...], other[c][...]
        gt[pl.ds(c * chunk, chunk), :] = jnp.where(first, a, b).T
        ut[pl.ds(c * chunk, chunk), :] = jnp.where(first, b, a).T

    targets = [(own, 0), (own, 1), (first_out, 0), (third_out, 0)]
    targets += [(first_out, 1), (third_out, 1), (second_out, 0), (second_out, 1)]

    def block(i, _):
        rows = pl.ds(pl.multiple_of(i * piece, piece), piece)
        out = jnp.dot(wg[rows, :], gt[...], preferred_element_type=F32)
        out += jnp.dot(wu[rows, :], ut[...], preferred_element_type=F32)
        for j, (ref, at) in enumerate(targets):

            @pl.when(i == j)
            def _(ref=ref, at=at):
                ref[at, :piece, :] = out.astype(ref.dtype)

        return 0

    lax.fori_loop(0, len(targets), block, 0)
    terms = in_terms(route[...])
    for ref in (first_out, third_out, second_out):
        for at in range(2):
            ref[at, piece:, :] = terms


def token_parts(info, mine, other, route, waited, weights, piece):
    cap, chunk = mine[0].shape
    depth, width = weights[0].shape
    pair, message = (2, piece, cap), (2, piece + EXTRA, cap)
    return pl.pallas_call(
        back_kernel,
        grid_spec=pltpu.PrefetchScalarGridSpec(
            num_scalar_prefetch=1,
            grid=(1,),
            in_specs=[whole((cap, chunk))] * (2 * CHUNKS)
            + [whole((1, cap)), pl.BlockSpec(memory_space=pl.ANY)]
            + [pl.BlockSpec(memory_space=pltpu.VMEM)] * 2,
            out_specs=[whole(pair)] + [whole(message)] * 3,
            scratch_shapes=[pltpu.VMEM((width, cap), BF), pltpu.VMEM((width, cap), BF)],
        ),
        out_shape=[jax.ShapeDtypeStruct(pair, F32)] + [jax.ShapeDtypeStruct(message, BF)] * 3,
        compiler_params=pltpu.CompilerParams(vmem_limit_bytes=14 * MIB),
        cost_estimate=pl.CostEstimate(
            flops=4 * cap * depth * width, bytes_accessed=4 * depth * width, transcendentals=0
        ),
    )(info, *mine, *other, route, waited, *weights)


def after(x, waited):
    def kernel(value, _, out):
        out[...] = value[...]

    return pl.pallas_call(
        kernel,
        grid=(1,),
        in_specs=[whole(x.shape), pl.BlockSpec(memory_space=pl.ANY)],
        out_specs=whole(x.shape),
        out_shape=jax.ShapeDtypeStruct(x.shape, x.dtype),
        compiler_params=pltpu.CompilerParams(vmem_limit_bytes=4 * MIB),
    )(x, waited)


def combine_kernel(own, route, first, third, second, kept, kept_route, sent):
    piece = own.shape[1]
    rows = [row_of(ref[0, piece:, :]) for ref in (first, third, second)]
    kept_route[...] = (route[...] + rows[0]) + (rows[1] + rows[2])
    for at in range(2):
        total = own[at]
        for ref in (first, third, second):
            total += ref[at, :piece, :].astype(F32)
        if at == 0:
            kept[...] = total
        else:
            sent[:piece, :] = total.astype(BF)
    sent[piece:, :] = in_terms(kept_route[...])


def combine(own, route, parts):
    _, piece, cap = own.shape
    shapes = [((piece, cap), F32), ((1, cap), F32), ((piece + EXTRA, cap), BF)]
    return pl.pallas_call(
        combine_kernel,
        out_shape=[jax.ShapeDtypeStruct(shape, kind) for shape, kind in shapes],
        compiler_params=pltpu.CompilerParams(vmem_limit_bytes=6 * MIB),
        cost_estimate=pl.CostEstimate(
            flops=8 * piece * cap, bytes_accessed=30 * piece * cap, transcendentals=0
        ),
    )(own, route, *parts)


def hop_kernel(has, n_waits, *refs):
    n = len(has)
    parts, refs = refs[:n], refs[n:]
    got, outs = refs[: sum(has)], refs[sum(has) + n_waits :]
    taken = 0
    for i in range(n):
        total = parts[i][0]
        if has[i]:
            total += got[taken][...].astype(F32)
            taken += 1
        outs[i][...] = total.astype(BF)


def hop_sums(base, places, arrived, waited):
    _, rows, cols = base.shape
    got = [a for a in arrived if a is not None]
    n = len(places)
    block = lambda j: pl.BlockSpec((1, rows, cols), lambda i: (j, 0, 0))
    return pl.pallas_call(
        lambda *a: hop_kernel([x is not None for x in arrived], len(waited), *a),
        grid=(1,),
        in_specs=[block(j) for j in places]
        + [whole((rows, cols))] * len(got)
        + [pl.BlockSpec(memory_space=pl.ANY)] * len(waited),
        out_specs=[whole((rows, cols))] * n,
        out_shape=[jax.ShapeDtypeStruct((rows, cols), BF)] * n,
        compiler_params=pltpu.CompilerParams(vmem_limit_bytes=6 * MIB),
        cost_estimate=pl.CostEstimate(
            flops=2 * n * rows * cols, bytes_accessed=8 * n * rows * cols, transcendentals=0
        ),
    )(*[base] * n, *got, *waited)


def far_kernel(n, n_z, info, *refs):
    out, send = refs[-2:]
    for y in range(n // 2):
        for x in range(2):
            at, there = placed(info, y + x * (n // 2), n_z)
            out[at] = refs[y][x]
            send[there] = refs[y][x]


def far_operand(info, arrays, n, n_z):
    rows, cap = arrays[0].shape[1:]
    return pl.pallas_call(
        lambda *a: far_kernel(n, n_z, *a),
        grid_spec=pltpu.PrefetchScalarGridSpec(
            num_scalar_prefetch=1,
            grid=(1,),
            in_specs=[whole(a.shape) for a in arrays],
            out_specs=[whole((n_z, rows, cap))] * 2,
        ),
        out_shape=[jax.ShapeDtypeStruct((n_z, rows, cap), BF)] * 2,
        compiler_params=pltpu.CompilerParams(vmem_limit_bytes=8 * MIB),
        cost_estimate=pl.CostEstimate(
            flops=0, bytes_accessed=4 * n * rows * cap, transcendentals=0
        ),
    )(info, *arrays)


def on_device(tokens, hidden_cot, w_gate, w_up, expert_ids, route_fixed):
    tok_dev, piece = tokens.shape
    width = w_gate.shape[1]
    n_tensor = lax.axis_size("tensor")
    n_dp = lax.axis_size("dp")
    n_z = n_dp // 4
    half = piece // 2
    xlo = n_tensor // 2
    t = lax.axis_index("tensor")
    dp = lax.axis_index("dp")
    z, xh, core = dp // 4, (dp // 2) % 2, dp % 2
    info = jnp.stack([t, z, xh, core]).astype(jnp.int32)
    tie = lax.optimization_barrier

    def over_tensor(x, k):
        return lax.ppermute(x, "tensor", [(i, i ^ k) for i in range(n_tensor)])

    def over_dp(x, k):
        return lax.ppermute(x, "dp", [(i, i ^ k) for i in range(n_dp)])

    def along_z(x, k):
        pairs = [(i, (i + 4 * (k if i % 2 == 0 else -k)) % n_dp) for i in range(n_dp)]
        return lax.ppermute(x, "dp", pairs)

    def over_both(x, k, m):
        n_all = n_dp * n_tensor
        pairs = [(i, i ^ (k * n_tensor + m)) for i in range(n_all)]
        return lax.ppermute(x, ("dp", "tensor"), pairs)

    selected = expert_ids == 0
    flag = jnp.any(selected, axis=1)
    place = jnp.arange(tok_dev, dtype=jnp.int32)
    upto = (place[:, None] <= place[None, :]).astype(BF)
    slot_of = jnp.dot(flag.astype(BF)[None, :], upto, preferred_element_type=F32)[0] - 1.0
    slot_of = jnp.where(flag, slot_of.astype(jnp.int32), -1)
    mask = slot_of[None, :] == jnp.arange(CAP, dtype=jnp.int32)[:, None]
    dispatch = mask.astype(BF)
    share_all = jnp.sum(jnp.where(selected, route_fixed, 0), axis=1).astype(F32) / 65536.0

    hidden_cot = pltpu.with_memory_space_constraint(hidden_cot, pltpu.HBM)
    tokens = pltpu.with_memory_space_constraint(tokens, pltpu.HBM)
    w_gate = pltpu.with_memory_space_constraint(w_gate, pltpu.HBM)
    w_up = pltpu.with_memory_space_constraint(w_up, pltpu.HBM)
    picked, far_piece = dispatch_tokens(info, slot_of[None, :], tokens)
    cot_rows, share = dispatch_cots(slot_of[None, :], share_all[None, :], hidden_cot)
    near = [None] * n_tensor
    near[xlo] = over_tensor(picked, xlo)
    near[1] = over_tensor(picked, 1)
    near[3] = over_tensor(picked, 3)
    far_other = over_both(far_piece, 2, xlo)
    picked, near[1], near[3], near[xlo], cot_rows, share, far_other, far_piece = tie(
        (picked, near[1], near[3], near[xlo], cot_rows, share, far_other, far_piece)
    )
    far_piece = over_dp(far_piece, 2)
    near[0] = picked
    near[xlo + 1] = over_tensor(near[1], xlo)
    near[xlo + 3] = over_tensor(near[3], xlo)
    near[2] = over_tensor(picked, 2)
    near[xlo + 2] = over_tensor(near[xlo], 2)
    soon, late = (0, xlo, 1, 3), (xlo + 1, xlo + 3, 2, xlo + 2)
    order = jnp.stack([t ^ k for k in soon + late] + [xh]).astype(jnp.int32)
    gate, up, near_soon, *weights = early(order, [near[k] for k in soon], w_gate, w_up)
    far_pair = jnp.stack([far_piece, far_other])
    late_near, gate, up, far_pair = tie(([near[k] for k in late], gate, up, far_pair))
    outs = forward(
        info, late_near, soon, late, *weights, gate, up, near_soon, cot_rows, share, n_z
    )
    mine, other = outs[:CHUNKS], outs[CHUNKS : 2 * CHUNKS]
    near_left, near_send, route_part = outs[2 * CHUNKS :]

    def to_partners(c):
        return [mine[c], over_dp(other[c], 1), over_dp(mine[c], 2), over_dp(other[c], 3)]

    cots = [to_partners(0)]
    near_sib = over_dp(near_send, 1)
    far_pair, near_sib = tie((far_pair, near_sib))
    far = [far_pair] + [over_tensor(far_pair, k) for k in (1, 2, 3)]
    own_part, *sent = token_parts(info, mine, other, route_part, far_pair, weights, piece)

    def product(a, b):
        return jnp.dot(a.reshape(n_z * half, CAP), b, preferred_element_type=F32)

    close = product(near_left, cots[0][0]) + product(near_sib, cots[0][1])
    far, own_part, sent, mine, other, close = tie((far, own_part, sent, mine, other, close))
    far_left, far_send = far_operand(info, far, n_tensor, n_z)
    far_sib = over_dp(far_send, 1)
    for c in range(1, CHUNKS):
        mine, other, cots[-1] = tie((mine, other, cots[-1]))
        cots.append(to_partners(c))
    step = width // CHUNKS

    def sums_of(c, close):
        base = tie(close) + product(far_left, cots[c][2])
        base = tie(base + product(far_sib, cots[c][3]))
        return base.reshape(n_z, half, step)

    class Ring:
        def __init__(self, c, base):
            self.base = base
            self.up_hops = n_z // 2 - c % 2
            self.down_hops = n_z - 1 - self.up_hops
            self.rising = self.falling = None

        def hop(self, i, waited):
            places, arrived = [], []
            if i < self.up_hops:
                places.append(self.up_hops - i)
                arrived.append(self.rising)
            if i < self.down_hops:
                places.append((n_z - self.down_hops + i) % n_z)
                arrived.append(self.falling)
            out = hop_sums(self.base, places, arrived, waited)
            if i < self.up_hops:
                self.rising = along_z(out[0], 1)
            if i < self.down_hops:
                self.falling = along_z(out[-1], -1)
            return out[0]

        def finish(self):
            total = self.base[0] + self.rising.astype(F32) + self.falling.astype(F32)
            return total.astype(BF).reshape(2, half // 2, step)

    rings = [Ring(0, sums_of(0, close))]
    waited = rings[0].hop(0, [])
    sums = {1: over_tensor(after(sent[0], waited), 1)}
    for c in range(1, CHUNKS):
        lefts = [after(near_left, waited), near_sib]
        close = product(lefts[0], cots[c][0]) + product(lefts[1], cots[c][1])
        rings.append(Ring(c, sums_of(c, close)))
        waited = rings[c].hop(0, [waited])
    for i in range(1, n_z // 2):
        waited = rings[0].hop(i, [waited])
        if i == 1:
            sums[3] = over_tensor(after(sent[1], waited), 3)
        if i == 3:
            parts = [sums[1], sums[3], sums[2]]
            in_hbm = lambda a: pltpu.with_memory_space_constraint(a, pltpu.HBM)
            total, route_total, message = combine(
                in_hbm(own_part), in_hbm(route_part), [in_hbm(a) for a in parts]
            )
        for ring in rings[1:]:
            needed = ([sums[1]], [sums[3]], [message] if i == 3 else [])[i - 1]
            waited = ring.hop(i, [waited, *needed])
        if i == 1:
            sums[2] = over_tensor(after(sent[2], waited), 2)
    whole_rows = jnp.concatenate([ring.finish() for ring in rings], axis=2)
    kept = lax.dynamic_index_in_dim(whole_rows, core, 0, keepdims=False)
    swapped = over_dp(lax.dynamic_index_in_dim(whole_rows, 1 - core, 0, keepdims=False), 1)
    gate_grad = jnp.where(core == 0, kept, swapped)
    up_grad = jnp.where(core == 0, swapped, kept)

    message = over_tensor(message, xlo)
    total = total + message[:piece].astype(F32)
    route_total = route_total + row_of(message[piece:])
    token_grad = lax.dot_general(
        dispatch, total.astype(BF), (((0,), (1,)), ((), ())), preferred_element_type=F32
    ).astype(BF)
    route_grad = jnp.sum(jnp.where(mask, route_total[0][:, None], 0.0), axis=0)
    return token_grad, gate_grad, up_grad, route_grad


def solution(mesh):
    return jax.shard_map(
        on_device,
        mesh=mesh,
        in_specs=(
            P("dp", "tensor"),
            P("dp", "tensor"),
            P(None, "tensor"),
            P(None, "tensor"),
            P("dp", None),
            P("dp", None),
        ),
        out_specs=(P("dp", "tensor"), P("dp", "tensor"), P("dp", "tensor"), P("dp")),
        check_vma=False,
    )
```
